512 devices in a mesh: lat: 16 (over z_hi, x, core), chan: 32 (over z_lo, y).
Axes of the slice: x: 4, y: 4, z: 16 (z_hi: 2, z_lo: 8; z = z_hi * 8 + z_lo), core: 2. Of those that a mesh axis runs over, the one named last changes fastest.
Arguments:
- block_input: bfloat16 [768, 128, 256], P('chan', 'lat'), may hold values from -6 to 6
- out_grad: bfloat16 [768, 128, 256], P('chan', 'lat'), may hold values from -6 to 6
- metric: float32 [128], P('lat'), may hold values from 1 to 4
- kernel: float32 [768, 49], P('chan'), may hold values from -0.875 to 0.875
- conv_bias: float32 [768], P('chan'), may hold values from -3 to 3
- ln_gain: float32 [768], replicated, may hold values from 0.1 to 1.9
- ln_bias: float32 [768], replicated, may hold values from -3 to 3
- w_in: bfloat16 [3072, 768], P('chan'), may hold values from -0.4375 to 0.4375
- b_in: float32 [3072], P('chan'), may hold values from -3 to 3
- w_out: bfloat16 [3072, 768], P('chan'), may hold values from -0.109375 to 0.109375
- b_out: float32 [768], P('chan'), may hold values from -3 to 3
- layer_scale: bfloat16 [768], replicated, may hold values from 0.5 to 2
Outputs:
- grad_input: float32 [768, 128, 256], P('chan', 'lat')
- grad_kernel: float32 [768, 49], P('chan')
- grad_conv_bias: float32 [768], P('chan')
- grad_ln_gain: float32 [768], P('chan')
- grad_ln_bias: float32 [768], P('chan')
- grad_w_in: float32 [3072, 768], P('chan')
- grad_b_in: float32 [3072], P('chan')
- grad_w_out: float32 [3072, 768], P('chan')
- grad_b_out: float32 [768], P('chan')
- grad_layer_scale: float32 [768], P('chan')
The draws below stay inside these ranges and needn't reach their ends.
All inputs are finite; a program needn't handle non-finite values.
Results may differ from the reference program's by a relative error of at most 0.035.
Values may be sent and summed in bfloat16 or wider, within the bound.
No kernel may reach another device: no remote copies, remote signals or barrier semaphores. Data moves between devices by JAX's collectives and lax.ppermute only.
A program may use at most 64 MiB of HBM per device.

```python
import math
import jax
import jax.numpy as jnp
from jax import lax

C = 768
H = 3072
LON = 256
LAT = 128
N_CHAN = 32


def spiked(drawn, own_key, source, target, blocks, factor):
    owner, partner = [(jnp.arange(drawn.shape[axis_at]) // (drawn.shape[axis_at] // blocks)).reshape([-1 if axis == axis_at else 1 for axis in range(drawn.ndim)]) for axis_at in (source, target)]
    chosen = jax.random.permutation(own_key, blocks)[partner]
    strong = (owner == chosen) | (owner == (partner + blocks // 2) % blocks)
    return jnp.where(strong, factor * drawn, drawn)


def block_levels(rng, shape, pieces, least, top_value):
    def one(dim, parts):
        steps = jax.random.uniform(jax.random.fold_in(jax.random.fold_in(rng, 6), dim), (parts,), jnp.float32, least / len(pieces), top_value / len(pieces))
        return jnp.repeat(jnp.exp(steps), shape[dim] // parts).reshape((-1,) + (1,) * (len(shape) - dim - 1))

    loudness = one(*pieces[0])
    for cut in pieces[1:]:
        loudness = loudness * one(*cut)
    return loudness


def bell_draw(key, dims, scale, reach, shards=(), held_as=jnp.bfloat16):
    values = jax.random.normal(key, dims, jnp.float32) * scale
    if len(shards) > 0:
        values = block_levels(key, dims, shards, -0.22, 0.18) * values
    return jnp.clip(values, min=-reach, max=reach).astype(held_as)


def heavy_noise(rng, extent, scale, limit, cuts, heavy, held_as=jnp.bfloat16):
    entries = scale * jax.random.normal(rng, extent, jnp.float32)
    if cuts:
        entries = entries * block_levels(rng, extent, cuts, -0.22, 0.18)
    return jnp.clip(spiked(entries, jax.random.fold_in(rng, 3), *heavy), -limit, limit).astype(held_as)


def setup_inputs(seed: int = 0) -> dict:
    seeds = jax.random.split(jax.random.key(seed), 13)
    return {
        "block_input": bell_draw(seeds[0], (C, LAT, LON), 1.0, 6.0, ((0, 32), (1, 16))),
        "out_grad": bell_draw(seeds[1], (C, LAT, LON), 1.0, 6.0, ((0, 32), (1, 16))),
        "metric": jnp.clip(jnp.exp(math.log(4.0) - 1.3862944 * jax.random.uniform(seeds[2], (LAT,), jnp.float32) ** block_levels(seeds[2], (LAT,), ((0, 16),), -0.2, 0.2)), 1.0, 4.0),
        "kernel": bell_draw(seeds[3], (C, 49), 49 ** -0.5, 0.875, ((0, 32),), jnp.float32),
        "conv_bias": bell_draw(seeds[4], (C,), 0.5, 3.0, ((0, 32),), jnp.float32),
        "ln_gain": jnp.clip(1.0 + 0.18 * jax.random.normal(seeds[5], (C,), jnp.float32), 0.1, 1.9),
        "ln_bias": bell_draw(seeds[6], (C,), 0.5, 3.0, (), jnp.float32),
        "w_in": heavy_noise(seeds[7], (H, C), C ** -0.5, 0.4375, ((0, 32),), (0, 1, 32, 2.75)),
        "b_in": bell_draw(seeds[8], (H,), 0.5, 3.0, ((0, 32),), jnp.float32),
        "w_out": bell_draw(seeds[9], (H, C), H ** -0.5, 0.109375, ((0, 32),)),
        "b_out": bell_draw(seeds[10], (C,), 0.5, 3.0, ((0, 32),), jnp.float32),
        "layer_scale": jnp.clip(jax.random.uniform(seeds[11], (C,), jnp.float32, 0.5, 2.0), 0.5, 2.0).astype(jnp.bfloat16),
    }


def gelu_exact(value):
    return jax.nn.gelu(value, approximate=False)

def reference(block_input, out_grad, metric, kernel, conv_bias, ln_gain, ln_bias, w_in, b_in, w_out, b_out, layer_scale):
    chans, rows, width = block_input.shape
    tokens = rows * width
    xfull = jnp.pad(block_input.astype(jnp.float32), ((0, 0), (3, 3), (3, 3)))
    conv = jnp.zeros((chans, rows, width), jnp.float32)
    for a in range(7):
        for b in range(7):
            conv = conv + kernel[:, a * 7 + b][:, None, None] * xfull[:, a:a + rows, b:b + width]
    h = (conv_bias[:, None, None] + metric[None, :, None] * conv).astype(jnp.bfloat16)
    hf = h.astype(jnp.float32).reshape(chans, tokens)
    mean = lax.optimization_barrier(jnp.sum(hf, 0)) / chans
    var = lax.optimization_barrier(jnp.sum(hf * hf, 0)) / chans - mean * mean
    rstd = 1.0 / jnp.sqrt(var + 1e-06)
    nhat = (hf - mean) * rstd
    n = (nhat * ln_gain[:, None] + ln_bias[:, None]).astype(jnp.bfloat16)
    dyf = out_grad.reshape(chans, tokens)
    gamma_f = layer_scale.astype(jnp.float32)
    dmlp = (gamma_f[:, None] * dyf.astype(jnp.float32)).astype(jnp.bfloat16)
    blocks = H // N_CHAN
    contract = (((1,), (1,)), ((), ()))

    def block_step(carry, item):
        dn_total, gam_total = carry
        w_block, b_block, o_block = item
        pre = jnp.dot(w_block, n, preferred_element_type=jnp.float32) + b_block[:, None]
        g, back = jax.vjp(gelu_exact, pre)
        g_b = g.astype(jnp.bfloat16)
        proj = lax.dot_general(g_b, dyf, contract, preferred_element_type=jnp.float32)
        dg = jnp.dot(o_block, dmlp, preferred_element_type=jnp.float32)
        dpre = back(dg)[0].astype(jnp.bfloat16)
        dw = lax.dot_general(dpre, n, contract, preferred_element_type=jnp.float32)
        db = lax.optimization_barrier(jnp.sum(dpre.astype(jnp.float32), 1))
        part = lax.dot_general(w_block, dpre, (((0,), (0,)), ((), ())), preferred_element_type=jnp.float32)
        part = lax.optimization_barrier(part.astype(jnp.bfloat16)).astype(jnp.float32)
        gam = lax.optimization_barrier(jnp.sum(o_block.astype(jnp.float32) * proj, 0))
        return ((dn_total + part, gam_total + gam), (dw, db, proj * gamma_f[None, :]))
    init = (jnp.zeros((chans, tokens), jnp.float32), jnp.zeros((chans,), jnp.float32))
    items = (w_in.reshape(N_CHAN, blocks, chans), b_in.reshape(N_CHAN, blocks), w_out.reshape(N_CHAN, blocks, chans))
    (dn, gam_sum), (dw_in, db_in, dw_out) = lax.scan(block_step, init, items)
    dnhat = ln_gain[:, None] * dn
    first = lax.optimization_barrier(jnp.sum(dnhat, 0)) / chans
    second = lax.optimization_barrier(jnp.sum(dnhat * nhat, 0)) / chans
    dh = rstd * (dnhat - first - nhat * second)
    grad_ln_gain = lax.optimization_barrier(jnp.sum(dn * nhat, 1))
    grad_ln_bias = lax.optimization_barrier(jnp.sum(dn, 1))
    dh3 = dh.reshape(chans, rows, width)
    grad_conv_bias = lax.optimization_barrier(jnp.sum(dh3, (1, 2)))
    dconv = metric[None, :, None] * dh3
    dpad = jnp.pad(dconv, ((0, 0), (3, 3), (3, 3)))
    spread = jnp.zeros((chans, rows, width), jnp.float32)
    taps = []
    for a in range(7):
        for b in range(7):
            spread = spread + kernel[:, a * 7 + b][:, None, None] * dpad[:, 6 - a:6 - a + rows, 6 - b:6 - b + width]
            taps.append(lax.optimization_barrier(jnp.sum(xfull[:, a:a + rows, b:b + width] * dconv, (1, 2))))
    grad_kernel = jnp.stack(taps, 1)
    grad_input = out_grad.astype(jnp.float32) + spread
    dysum = lax.optimization_barrier(jnp.sum(out_grad.astype(jnp.float32), (1, 2)))
    grad_b_out = gamma_f * dysum
    grad_layer_scale = gam_sum + b_out * dysum
    return (grad_input, grad_kernel, grad_conv_bias, grad_ln_gain, grad_ln_bias, dw_in.reshape(H, chans), db_in.reshape(H), dw_out.reshape(H, chans), grad_b_out, grad_layer_scale)
```

```python
import jax
import jax.numpy as jnp
from jax import lax
from jax.sharding import Mesh, PartitionSpec as P

LAT = ("zh", "x", "c")
CHAN = ("zl", "y")
GROUP = 8
F32 = jnp.float32
BF = jnp.bfloat16


def extended(cells, width):
    count = lax.axis_size(LAT)
    ends = count - 1
    head = lax.slice_in_dim(cells, 0, width, axis=1)
    tail = lax.slice_in_dim(cells, cells.shape[1] - width, cells.shape[1], axis=1)
    return jnp.concatenate(
        [
            lax.ppermute(tail, LAT, [(i, i + 1) for i in range(ends)]),
            cells,
            lax.ppermute(head, LAT, [(i + 1, i) for i in range(ends)]),
        ],
        axis=1,
    )


def gelu_exact(value):
    return jax.nn.gelu(value, approximate=False)


def two_parts(value):
    high = lax.reduce_precision(value, 8, 7)
    return high.astype(BF), (value - high).astype(BF)


def per_device(
    block_input,
    out_grad,
    metric,
    kernel,
    conv_bias,
    ln_gain,
    ln_bias,
    w_in,
    b_in,
    w_out,
    b_out,
    layer_scale,
):
    cdev, rows, width = block_input.shape
    chans = ln_gain.shape[0]
    tokens = rows * width
    nz, ny = lax.axis_size("zl"), lax.axis_size("y")
    nchan = nz * ny
    hdev = w_in.shape[0]
    part = hdev // GROUP
    hid = part * nchan
    piece = tokens // nchan
    member = lax.axis_index(("x", "c"))
    owner = lax.axis_index(CHAN)
    gamma_f = layer_scale.astype(F32)
    gamma_own = lax.dynamic_slice_in_dim(gamma_f, owner * cdev, cdev)

    bias_high, bias_low = two_parts(lax.dynamic_slice_in_dim(b_in, member * part, part))
    bias_row = jnp.zeros((1, chans), BF)
    bias_row = bias_row.at[0, :part].set(bias_high).at[0, part : 2 * part].set(bias_low)
    mine = jnp.concatenate(
        [
            lax.dynamic_slice_in_dim(w_in, member * part, part),
            lax.dynamic_slice_in_dim(w_out, member * part, part),
            bias_row,
        ],
        0,
    )
    shards = lax.all_gather(mine, "y", axis=0)
    shards = lax.all_gather(shards, "zl", axis=1)
    wi = shards[:, :, :part].reshape(hid, chans)
    wo = shards[:, :, part : 2 * part].reshape(hid, chans)
    bias_rows = shards[:, :, 2 * part].astype(F32)
    bi = (bias_rows[..., :part] + bias_rows[..., part : 2 * part]).reshape(hid)

    xpad = jnp.pad(extended(block_input, 3).astype(F32), ((0, 0), (0, 0), (3, 3)))
    conv = jnp.zeros((cdev, rows, width), F32)
    for a in range(7):
        for b in range(7):
            conv = conv + kernel[:, a * 7 + b][:, None, None] * xpad[:, a : a + rows, b : b + width]
    h = (conv_bias[:, None, None] + metric[None, :, None] * conv).astype(BF)

    both = jnp.concatenate(
        [h.reshape(cdev, nchan, piece), out_grad.reshape(cdev, nchan, piece)], 2
    ).transpose(1, 0, 2)
    both = lax.all_to_all(both, CHAN, 0, 0, tiled=True).reshape(chans, 2 * piece).T
    hf = both[:piece].astype(F32)
    dy_piece = both[piece:]
    mean = jnp.sum(hf, 1, keepdims=True) / chans
    var = jnp.sum(hf * hf, 1, keepdims=True) / chans - mean * mean
    rstd = 1.0 / jnp.sqrt(var + 1e-06)
    nhat = (hf - mean) * rstd
    n_piece = (nhat * ln_gain + ln_bias).astype(BF)

    pair = jnp.concatenate([n_piece, dy_piece], 0)
    pair = lax.all_gather(pair, "x", axis=0)
    pair = lax.all_gather(pair, "c", axis=0)
    n = pair[:, :, :piece].reshape(GROUP * piece, chans)
    dy = pair[:, :, piece:].reshape(GROUP * piece, chans)

    over_last = (((1,), (1,)), ((), ()))
    over_first = (((0,), (0,)), ((), ()))
    pre = lax.dot_general(n, wi, over_last, preferred_element_type=F32) + bi
    g, back = jax.vjp(gelu_exact, pre)
    g_b = g.astype(BF)
    dmlp = (gamma_f * dy.astype(F32)).astype(BF)
    grad_g = lax.dot_general(dmlp, wo, over_last, preferred_element_type=F32)
    dpre = back(grad_g)[0].astype(BF)
    dn_part = jnp.dot(dpre, wi, preferred_element_type=F32).astype(BF)
    dw_in = lax.dot_general(dpre, n, over_first, preferred_element_type=F32)
    proj = lax.dot_general(g_b, dy, over_first, preferred_element_type=F32)
    db_in = jnp.sum(dpre.astype(F32), 0)
    gam_part = jnp.sum(wo.astype(F32) * proj, 0)
    dw_out = proj * gamma_f

    grid = (ny, nz, part)
    db_row = jnp.pad(db_in.astype(BF).reshape(grid)[:, :, None, :], ((0, 0), (0, 0), (0, 0), (0, chans - part)))
    dws = jnp.concatenate(
        [dw_in.astype(BF).reshape(grid + (chans,)), dw_out.astype(BF).reshape(grid + (chans,)), db_row], 2
    )
    dws = lax.psum_scatter(dws, "y", scatter_dimension=0, tiled=False)

    dn = lax.all_to_all(dn_part.reshape(GROUP, piece, chans), ("c", "x"), 0, 0, tiled=True)
    dn = jnp.sum(dn.astype(F32), 0)
    dnhat = ln_gain * dn
    s1 = jnp.sum(dnhat, 1, keepdims=True) / chans
    s2 = jnp.sum(dnhat * nhat, 1, keepdims=True) / chans
    dh = rstd * (dnhat - s1 - nhat * s2)
    extra = []
    for value in (jnp.sum(dn * nhat, 0), jnp.sum(dn, 0), gam_part):
        extra += list(two_parts(value))
    payload = jnp.concatenate([dh.astype(BF), jnp.stack(extra, 0)], 0)
    payload = payload.T.reshape(nchan, cdev, piece + 6)
    payload = lax.all_to_all(payload, CHAN, 0, 0, tiled=True)
    dh3 = payload[:, :, :piece].transpose(1, 0, 2).reshape(cdev, rows, width).astype(F32)
    sums = jnp.sum(payload[:, :, piece:].astype(F32), 0)
    sums = sums[:, 0::2] + sums[:, 1::2]

    dws = lax.all_to_all(dws, "zl", 0, 0, tiled=True)
    dws = jnp.sum(dws.astype(F32), 0)

    dconv = metric[None, :, None] * dh3
    taps = []
    for a in range(7):
        for b in range(7):
            taps.append(jnp.sum(xpad[:, a : a + rows, b : b + width] * dconv, (1, 2)))
    dpad = jnp.pad(extended(dconv.astype(BF), 3).astype(F32), ((0, 0), (0, 0), (3, 3)))
    spread = jnp.zeros((cdev, rows, width), F32)
    for a in range(7):
        for b in range(7):
            spread = (
                spread
                + kernel[:, a * 7 + b][:, None, None]
                * dpad[:, 6 - a : 6 - a + rows, 6 - b : 6 - b + width]
            )
    grad_input = out_grad.astype(F32) + spread
    dysum = jnp.sum(out_grad.astype(F32), (1, 2))

    small = jnp.concatenate(
        [jnp.stack(taps, 1), jnp.sum(dh3, (1, 2))[:, None], sums, dysum[:, None]], 1
    )
    n_small = small.size
    small_rows = -(-n_small // chans)
    small = jnp.pad(small.reshape(n_small), (0, small_rows * chans - n_small)).reshape(small_rows, chans)
    swap = [(0, 1), (1, 0)]
    high, low = two_parts(small)
    mine = jnp.concatenate([dws.astype(BF), high, low], 0)
    other = lax.ppermute(mine, "zh", swap).astype(F32)
    wrows = 2 * part + 1
    dws = dws + other[:wrows]
    small = small + other[wrows : wrows + small_rows] + other[wrows + small_rows :]
    high, low = two_parts(small)
    mine = jnp.concatenate([dws.astype(BF), high, low], 0)
    gathered = lax.all_gather(mine, "c", axis=0)
    gathered = lax.all_gather(gathered, "x", axis=0).reshape(GROUP, -1, chans).astype(F32)
    grad_w_in = gathered[:, :part].reshape(hdev, chans)
    grad_w_out = gathered[:, part : 2 * part].reshape(hdev, chans)
    grad_b_in = gathered[:, 2 * part, :part].reshape(hdev)
    small = jnp.sum(gathered[:, wrows : wrows + small_rows] + gathered[:, wrows + small_rows :], 0)
    small = small.reshape(-1)[:n_small].reshape(cdev, -1)
    taps_n = kernel.shape[1]
    dysum = small[:, taps_n + 4]
    return (
        grad_input,
        small[:, :taps_n],
        small[:, taps_n],
        small[:, taps_n + 1],
        small[:, taps_n + 2],
        grad_w_in,
        grad_b_in,
        grad_w_out,
        gamma_own * dysum,
        small[:, taps_n + 3] + b_out * dysum,
    )


def solution(mesh):
    split = Mesh(mesh.devices.reshape(2, 4, 2, 8, 4), ("zh", "x", "c", "zl", "y"))
    return jax.shard_map(
        per_device,
        mesh=split,
        in_specs=(
            P(CHAN, LAT, None),
            P(CHAN, LAT, None),
            P(LAT),
            P(CHAN, None),
            P(CHAN),
            P(),
            P(),
            P(CHAN, None),
            P(CHAN),
            P(CHAN, None),
            P(CHAN),
            P(),
        ),
        out_specs=(
            P(CHAN, LAT, None),
            P(CHAN, None),
            P(CHAN),
            P(CHAN),
            P(CHAN),
            P(CHAN, None),
            P(CHAN),
            P(CHAN, None),
            P(CHAN),
            P(CHAN),
        ),
        check_vma=False,
    )
```

```python
import jax
import jax.numpy as jnp
from jax import lax
from jax.sharding import Mesh, PartitionSpec as P

LAT = ("zh", "x", "c")
CHAN = ("zl", "y")
SLOT = 16
GROUP = 8
F32 = jnp.float32
BF = jnp.bfloat16


def extended(cells, width):
    count = lax.axis_size(LAT)
    ends = count - 1
    head = lax.slice_in_dim(cells, 0, width, axis=1)
    tail = lax.slice_in_dim(cells, cells.shape[1] - width, cells.shape[1], axis=1)
    return jnp.concatenate(
        [
            lax.ppermute(tail, LAT, [(i, i + 1) for i in range(ends)]),
            cells,
            lax.ppermute(head, LAT, [(i + 1, i) for i in range(ends)]),
        ],
        axis=1,
    )


def gelu_exact(value):
    return jax.nn.gelu(value, approximate=False)


def two_parts(value):
    high = lax.reduce_precision(value, 8, 7)
    return high.astype(BF), (value - high).astype(BF)


def to_all(block, axis):
    count = lax.axis_size(axis)
    return lax.all_to_all(jnp.broadcast_to(block[None], (count,) + block.shape), axis, 0, 0, tiled=True)


def exchange(blocks):
    return lax.all_to_all(blocks, CHAN, 0, 0, tiled=True)


def with_other_core(block):
    return jnp.concatenate([block, lax.ppermute(block, "c", [(0, 1), (1, 0)])], 0)


def pieces(cells):
    half = cells.shape[0] // 2
    return jnp.concatenate([cells[:half], cells[half:]], 2).transpose(1, 0, 2)


def halves(owners, slot, per_owner):
    shape = (owners * slot, owners * per_owner)
    row = lax.broadcasted_iota(jnp.int32, shape, 0)
    chan = lax.broadcasted_iota(jnp.int32, shape, 1)
    half = per_owner // 2
    inside = row % slot < half
    first = (row // slot) * per_owner + row % slot
    return [(inside & (chan == first + shift)).astype(BF) for shift in (0, half)]


def flipped(block, bit):
    return lax.ppermute(block, "zl", [(i, i ^ bit) for i in range(lax.axis_size("zl"))])


def gather_chan(block):
    parts = block[None]
    for bit in (4, 2, 1):
        parts = jnp.concatenate([parts, flipped(parts, bit)], 0)
    count = lax.axis_size("y")
    ahead = [lax.ppermute(parts, "y", [((i + k) % count, i) for i in range(count)]) for k in range(1, count)]
    return jnp.concatenate([parts] + ahead, 0)


def scatter_chan(blocks):
    count = lax.axis_size("y")
    parts = blocks.reshape((count, -1) + blocks.shape[1:])
    total = parts[0].astype(F32)
    for k in range(1, count):
        total = total + lax.ppermute(parts[k], "y", [(i, (i + k) % count) for i in range(count)]).astype(F32)
    for bit in (1, 2, 4):
        keep = total.shape[0] // 2
        total = total[:keep] + flipped(total[keep:].astype(BF), bit).astype(F32)
    return total[0]


def channels_last(blocks, picks):
    flat = blocks.reshape(-1, blocks.shape[2])
    piece = flat.shape[1] // 2
    over_first = (((0,), (0,)), ((), ()))
    parts = [
        lax.dot_general(flat[:, i * piece : (i + 1) * piece], pick, over_first, preferred_element_type=F32)
        for i, pick in enumerate(picks)
    ]
    return (parts[0] + parts[1]).astype(BF)


def per_device(
    block_input,
    out_grad,
    metric,
    kernel,
    conv_bias,
    ln_gain,
    ln_bias,
    w_in,
    b_in,
    w_out,
    b_out,
    layer_scale,
):
    cdev, rows, width = block_input.shape
    chans = ln_gain.shape[0]
    tokens = rows * width
    nz, ny = lax.axis_size("zl"), lax.axis_size("y")
    nchan = nz * ny
    hdev = w_in.shape[0]
    part = hdev // GROUP
    hid = part * nchan
    piece = tokens // nchan
    member = lax.axis_index(("x", "c"))
    owner = lax.axis_index(CHAN)
    gamma_f = layer_scale.astype(F32)
    gamma_own = lax.dynamic_slice_in_dim(gamma_f, owner * cdev, cdev)

    bias_parts = two_parts(lax.dynamic_slice_in_dim(b_in, member * part, part))
    bias_row = jnp.concatenate(bias_parts + (jnp.zeros((chans - 2 * part,), BF),))[None]
    mine = jnp.concatenate(
        [
            lax.dynamic_slice_in_dim(w_in, member * part, part),
            lax.dynamic_slice_in_dim(w_out, member * part, part),
            bias_row,
        ],
        0,
    )
    shards = gather_chan(mine)
    wi = shards[:, :part].reshape(hid, chans)
    wo = shards[:, part : 2 * part].reshape(hid, chans)
    bias_rows = shards[:, 2 * part].astype(F32)
    bi = (bias_rows[:, :part] + bias_rows[:, part : 2 * part]).reshape(hid)

    xpad = jnp.pad(extended(block_input, 3).astype(F32), ((0, 0), (0, 0), (3, 3)))
    conv = jnp.zeros((cdev, rows, width), F32)
    for a in range(7):
        for b in range(7):
            conv = conv + kernel[:, a * 7 + b][:, None, None] * xpad[:, a : a + rows, b : b + width]
    h = (conv_bias[:, None, None] + metric[None, :, None] * conv).astype(BF)

    both = jnp.concatenate(
        [pieces(h.reshape(cdev, nchan, piece)), pieces(out_grad.reshape(cdev, nchan, piece))], 1
    )
    both = exchange(both)
    hf = channels_last(both[:, : cdev // 2], halves(nchan, cdev // 2, cdev)).astype(F32)
    dy_piece = channels_last(both[:, cdev // 2 :], halves(nchan, cdev // 2, cdev))
    mean = jnp.sum(hf, 1, keepdims=True) / chans
    var = jnp.sum(hf * hf, 1, keepdims=True) / chans - mean * mean
    rstd = 1.0 / jnp.sqrt(var + 1e-06)
    nhat = (hf - mean) * rstd
    n_piece = (nhat * ln_gain + ln_bias).astype(BF)

    pair = with_other_core(to_all(jnp.concatenate([n_piece, dy_piece], 0), "x"))
    n = pair[:, :piece].reshape(GROUP * piece, chans)
    dy = pair[:, piece:].reshape(GROUP * piece, chans)

    over_last = (((1,), (1,)), ((), ()))
    over_first = (((0,), (0,)), ((), ()))
    pre = lax.dot_general(n, wi, over_last, preferred_element_type=F32) + bi
    g, back = jax.vjp(gelu_exact, pre)
    g_b = g.astype(BF)
    dmlp = (gamma_f * dy.astype(F32)).astype(BF)
    grad_g = lax.dot_general(dmlp, wo, over_last, preferred_element_type=F32)
    dpre = back(grad_g)[0].astype(BF)
    turned = jnp.roll(dpre, dpre.shape[0] // 2, 0)
    ordered = jnp.where(lax.axis_index("c") == 0, dpre, turned)
    dn_part = jnp.dot(ordered, wi, preferred_element_type=F32).astype(BF)
    dw_in = lax.dot_general(dpre, n, over_first, preferred_element_type=F32)
    proj = lax.dot_general(g_b, dy, over_first, preferred_element_type=F32)
    db_in = jnp.sum(dpre.astype(F32), 0)
    gam_part = jnp.sum(wo.astype(F32) * proj, 0)
    dw_out = proj * gamma_f

    db_row = jnp.pad(db_in.astype(BF).reshape(nchan, 1, part), ((0, 0), (0, 0), (0, chans - part)))
    dws = scatter_chan(
        jnp.concatenate(
            [dw_in.astype(BF).reshape(nchan, part, chans), dw_out.astype(BF).reshape(nchan, part, chans), db_row], 1
        )
    )

    dn = lax.all_to_all(dn_part.reshape(GROUP, piece, chans), ("c", "x"), 0, 0, tiled=True)
    dn = jnp.sum(dn.astype(F32), 0)
    dnhat = ln_gain * dn
    s1 = jnp.sum(dnhat, 1, keepdims=True) / chans
    s2 = jnp.sum(dnhat * nhat, 1, keepdims=True) / chans
    dh = rstd * (dnhat - s1 - nhat * s2)
    extra = jnp.stack([jnp.sum(dn * nhat, 0), jnp.sum(dn, 0), gam_part], 0)
    extra = extra.reshape(3, nchan, cdev).transpose(1, 0, 2).reshape(nchan, 3 * cdev)
    extra = jnp.stack(two_parts(jnp.pad(extra, ((0, 0), (0, 2 * piece - 3 * cdev)))), 1)
    picks = halves(nchan, SLOT, cdev)
    payload = jnp.concatenate(
        [lax.dot_general(pick, dh.astype(BF), over_last, preferred_element_type=F32) for pick in picks], 1
    ).astype(BF).reshape(nchan, SLOT, 2 * piece)
    half = cdev // 2
    payload = exchange(jnp.concatenate([payload[:, :half], extra, payload[:, half + 2 :]], 1))
    dh3 = jnp.concatenate([payload[:, :half, :piece], payload[:, :half, piece:]], 1)
    dh3 = dh3.transpose(1, 0, 2).reshape(cdev, rows, width).astype(F32)
    sums = jnp.sum(payload[:, half : half + 2].astype(F32), (0, 1))[: 3 * cdev].reshape(3, cdev).T

    dconv = metric[None, :, None] * dh3
    taps = []
    for a in range(7):
        for b in range(7):
            taps.append(jnp.sum(xpad[:, a : a + rows, b : b + width] * dconv, (1, 2)))
    dpad = jnp.pad(extended(dconv.astype(BF), 3).astype(F32), ((0, 0), (0, 0), (3, 3)))
    spread = jnp.zeros((cdev, rows, width), F32)
    for a in range(7):
        for b in range(7):
            spread = (
                spread
                + kernel[:, a * 7 + b][:, None, None]
                * dpad[:, 6 - a : 6 - a + rows, 6 - b : 6 - b + width]
            )
    grad_input = out_grad.astype(F32) + spread
    dysum = jnp.sum(out_grad.astype(F32), (1, 2))

    small = jnp.concatenate(
        [jnp.stack(taps, 1), jnp.sum(dh3, (1, 2))[:, None], sums, dysum[:, None]], 1
    )
    n_small = small.size
    small_rows = -(-n_small // chans)
    small = jnp.pad(small.reshape(n_small), (0, small_rows * chans - n_small)).reshape(small_rows, chans)
    swap = [(0, 1), (1, 0)]
    high, low = two_parts(small)
    mine = jnp.concatenate([dws.astype(BF), high, low], 0)
    other = lax.ppermute(mine, "zh", swap).astype(F32)
    wrows = 2 * part + 1
    dws = dws + other[:wrows]
    small = small + other[wrows : wrows + small_rows] + other[wrows + small_rows :]
    high, low = two_parts(small)
    mine = jnp.concatenate([dws.astype(BF), high, low], 0)
    gathered = to_all(mine, ("x", "c")).astype(F32)
    grad_w_in = gathered[:, :part].reshape(hdev, chans)
    grad_w_out = gathered[:, part : 2 * part].reshape(hdev, chans)
    grad_b_in = gathered[:, 2 * part, :part].reshape(hdev)
    small = jnp.sum(gathered[:, wrows : wrows + small_rows] + gathered[:, wrows + small_rows :], 0)
    small = small.reshape(-1)[:n_small].reshape(cdev, -1)
    taps_n = kernel.shape[1]
    dysum = small[:, taps_n + 4]
    return (
        grad_input,
        small[:, :taps_n],
        small[:, taps_n],
        small[:, taps_n + 1],
        small[:, taps_n + 2],
        grad_w_in,
        grad_b_in,
        grad_w_out,
        gamma_own * dysum,
        small[:, taps_n + 3] + b_out * dysum,
    )


def solution(mesh):
    split = Mesh(mesh.devices.reshape(2, 4, 2, 8, 4), ("zh", "x", "c", "zl", "y"))
    return jax.shard_map(
        per_device,
        mesh=split,
        in_specs=(
            P(CHAN, LAT, None),
            P(CHAN, LAT, None),
            P(LAT),
            P(CHAN, None),
            P(CHAN),
            P(),
            P(),
            P(CHAN, None),
            P(CHAN),
            P(CHAN, None),
            P(CHAN),
            P(),
        ),
        out_specs=(
            P(CHAN, LAT, None),
            P(CHAN, None),
            P(CHAN),
            P(CHAN),
            P(CHAN),
            P(CHAN, None),
            P(CHAN),
            P(CHAN, None),
            P(CHAN),
            P(CHAN),
        ),
        check_vma=False,
    )
```

```python
import jax
import jax.numpy as jnp
from jax import lax
from jax.experimental import pallas as pl
from jax.experimental.pallas import tpu as pltpu
from jax.sharding import Mesh, PartitionSpec as P

LAT = ("zh", "x", "c")
CHAN = ("zl", "y")
GROUP = 8
F32 = jnp.float32
BF = jnp.bfloat16
EXT = 16
VMEM_BYTES = 48 * 1024 * 1024
SIDE = 128


def vmem():
    return pl.BlockSpec(memory_space=pltpu.VMEM)


def smem():
    return pl.BlockSpec(memory_space=pltpu.SMEM)


def call(body, out_shape, in_specs, scratch=()):
    many = isinstance(out_shape, (list, tuple))
    return pl.pallas_call(
        body,
        out_shape=out_shape,
        in_specs=in_specs,
        out_specs=[vmem()] * len(out_shape) if many else vmem(),
        scratch_shapes=list(scratch),
        compiler_params=pltpu.CompilerParams(vmem_limit_bytes=VMEM_BYTES),
    )


def fill_rows(x_ref, up_ref, down_ref, ext):
    rows = x_ref.shape[1]
    ext[:, :3, :] = up_ref[...].astype(F32)
    ext[:, 3 : 3 + rows, :] = x_ref[...].astype(F32)
    ext[:, 3 + rows : 6 + rows, :] = down_ref[...].astype(F32)


def fill_shifts(cells, shifted):
    width = cells.shape[1]
    lane = lax.broadcasted_iota(jnp.int32, cells.shape, 1)
    for b in range(7):
        move = b - 3
        if move == 0:
            shifted[b] = cells
        else:
            turned = pltpu.roll(cells, (-move) % width, 1)
            inside = lane < width - move if move > 0 else lane >= -move
            shifted[b] = jnp.where(inside, turned, 0.0)


def stencil(taps_ref, c, shifted, rows, flip):
    total = None
    for a in range(7):
        for b in range(7):
            tap = a * 7 + b
            term = taps_ref[c, 48 - tap if flip else tap] * shifted[b, a : a + rows, :]
            total = term if total is None else total + term
    return total


def forward_body(taps_ref, bias_ref, x_ref, up_ref, down_ref, metric_ref, dy_ref, out_ref, ext, shifted, h_rows, dy_rows):
    cdev, rows, width = x_ref.shape
    fill_rows(x_ref, up_ref, down_ref, ext)
    dy_rows[...] = dy_ref[...].astype(F32)
    metric = jnp.broadcast_to(metric_ref[...], (rows, width))

    def channel(c, carry):
        fill_shifts(ext[c], shifted)
        h_rows[c] = bias_ref[c] + metric * stencil(taps_ref, c, shifted, rows, False)
        return carry

    lax.fori_loop(0, cdev, channel, 0)
    low = lax.broadcasted_iota(jnp.int32, (cdev, 128), 1) < 64
    for r in range(rows):
        h_row, dy_row = h_rows[:, r, :], dy_rows[:, r, :]
        for t in range(width // 128):
            h_tile, dy_tile = h_row[:, t * 128 : t * 128 + 128], dy_row[:, t * 128 : t * 128 + 128]
            at = (r * width + t * 128) // 64
            out_ref[at] = jnp.where(low, h_tile, pltpu.roll(dy_tile, 64, 1)).astype(BF)
            out_ref[at + 1] = jnp.where(low, pltpu.roll(h_tile, 64, 1), dy_tile).astype(BF)


def forward(taps, bias, x, up, down, metric, dy):
    cdev, rows, width = x.shape
    return call(
        forward_body,
        jax.ShapeDtypeStruct((rows * width // 64, cdev, 128), BF),
        [smem(), smem()] + [vmem()] * 5,
        [
            pltpu.VMEM((cdev, EXT, width), F32),
            pltpu.VMEM((7, EXT, width), F32),
            pltpu.VMEM((cdev, rows, width), F32),
            pltpu.VMEM((cdev, rows, width), F32),
        ],
    )(taps, bias, x, up, down, metric[:, None], dy)


def norm_body(recv_ref, gain_ref, bias_ref, pair_ref, nhat_ref, rstd_ref):
    chans, lanes = recv_ref.shape
    piece = lanes // 2
    both = recv_ref[...].astype(F32).T
    h = both[:piece]
    mean = jnp.sum(h, 1, keepdims=True) / chans
    var = jnp.sum(h * h, 1, keepdims=True) / chans - mean * mean
    rstd = 1.0 / jnp.sqrt(var + 1e-06)
    nhat = (h - mean) * rstd
    nhat_ref[...] = nhat
    rstd_ref[...] = jnp.broadcast_to(rstd, rstd_ref.shape)
    n = (nhat * gain_ref[...] + bias_ref[...]).astype(BF)
    dy = both[piece:].astype(BF)
    for k in range(pair_ref.shape[0]):
        pair_ref[k, :piece] = n
        pair_ref[k, piece:] = dy


def norm(recv, gain, bias, copies):
    chans, lanes = recv.shape
    return call(
        norm_body,
        [
            jax.ShapeDtypeStruct((copies, lanes, chans), BF),
            jax.ShapeDtypeStruct((lanes // 2, chans), F32),
            jax.ShapeDtypeStruct((lanes // 2, 128), F32),
        ],
        [vmem()] * 3,
    )(recv, gain[None], bias[None])


def norm_back_body(recv_ref, nhat_ref, rstd_ref, gain_ref, gam_ref, out_ref, flat):
    piece, chans = nhat_ref.shape
    dn = recv_ref[0].astype(F32)
    for k in range(1, recv_ref.shape[0]):
        dn = dn + recv_ref[k].astype(F32)
    nhat = nhat_ref[...]
    dnhat = dn * gain_ref[...]
    s1 = jnp.sum(dnhat, 1, keepdims=True) / chans
    s2 = jnp.sum(dnhat * nhat, 1, keepdims=True) / chans
    dh = rstd_ref[:, :1] * (dnhat - s1 - nhat * s2)
    flat[:piece] = dh
    flat[piece:] = jnp.zeros((flat.shape[0] - piece, chans), F32)
    sums = (jnp.sum(dn * nhat, 0, keepdims=True), jnp.sum(dn, 0, keepdims=True), gam_ref[...])
    for k, value in enumerate(sums):
        high = value.astype(BF).astype(F32)
        flat[piece + 2 * k : piece + 2 * k + 1] = high
        flat[piece + 2 * k + 1 : piece + 2 * k + 2] = value - high
    blocks = flat[...].T.reshape(out_ref.shape[0], 24, 128)
    one, two, three = blocks[:, :8], blocks[:, 8:16], blocks[:, 16:]
    lane = lax.broadcasted_iota(jnp.int32, one.shape, 2)
    out_ref[:, :8] = jnp.where(lane < 64, one, pltpu.roll(three, 64, 2)).astype(BF)
    last = jnp.where(lane < 72, one, jnp.where(lane < 80, pltpu.roll(two, 8, 2), pltpu.roll(three, 16, 2)))
    out_ref[:, 8:] = jnp.where(lane < 64, two, last).astype(BF)


def norm_back(recv, nhat, rstd, gain, gam, owners):
    piece, chans = nhat.shape
    return call(
        norm_back_body,
        jax.ShapeDtypeStruct((owners, 16, 128), BF),
        [vmem()] * 5,
        [pltpu.VMEM((128, chans), F32)],
    )(recv, nhat, rstd, gain[None], gam[None])


def taps_body(recv_ref, x_ref, up_ref, down_ref, metric_ref, dy_ref, dconv_ref, ends_ref, sums_ref, extra_ref, ext, shifted, dh_rows, prods):
    cdev, rows, width = x_ref.shape
    fill_rows(x_ref, up_ref, down_ref, ext)
    low16 = lax.broadcasted_iota(jnp.int32, (16, 128), 1) < 64
    low8 = lax.broadcasted_iota(jnp.int32, (8, 128), 1) < 64
    extra = jnp.zeros((8, 128), F32)
    for r in range(rows):
        for t in range(width // 128):
            at = (r * width + t * 128) // 64
            first, second = recv_ref[at].astype(F32), recv_ref[at + 1].astype(F32)
            lanes = slice(t * 128, t * 128 + 128)
            dh_rows[:16, r, lanes] = jnp.where(low16, first, pltpu.roll(second, 64, 1))
            dh_rows[16:, r, lanes] = jnp.where(low8, pltpu.roll(first[:8], 64, 1), second[:8])
            extra = extra + first[8:] + second[8:]
    for g in range(3):
        extra_ref[8 * g : 8 * g + 8] = pltpu.roll(extra, 64 - 8 * g, 1)
    metric = jnp.broadcast_to(metric_ref[...], (rows, width))

    def channel(c, carry):
        fill_shifts(ext[c], shifted)
        dh = dh_rows[c]
        dconv = metric * dh
        dconv_ref[c] = dconv
        ends_ref[0, c] = dconv[:3].astype(BF)
        ends_ref[1, c] = dconv[rows - 3 :].astype(BF)
        for a in range(7):
            for b in range(7):
                product = shifted[b, a : a + rows, :] * dconv
                prods[(a * 7 + b) * 8 : (a * 7 + b) * 8 + 8, :] = product[:, :128] + product[:, 128:]
        dy = dy_ref[c].astype(F32)
        prods[392:400, :] = dh[:, :128] + dh[:, 128:]
        prods[400:408, :] = dy[:, :128] + dy[:, 128:]
        total = prods[pl.ds(0, 56, 8), :]
        for i in range(1, 8):
            total = total + prods[pl.ds(i, 56, 8), :]
        sums_ref[c] = total
        return carry

    prods[408:, :] = jnp.zeros((prods.shape[0] - 408, 128), F32)
    lax.fori_loop(0, cdev, channel, 0)


def tap_sums(recv, x, up, down, metric, dy):
    cdev, rows, width = x.shape
    return call(
        taps_body,
        [
            jax.ShapeDtypeStruct((cdev, rows, width), F32),
            jax.ShapeDtypeStruct((2, cdev, 3, width), BF),
            jax.ShapeDtypeStruct((cdev, 56, 128), F32),
            jax.ShapeDtypeStruct((cdev, 128), F32),
        ],
        [vmem()] * 6,
        [
            pltpu.VMEM((cdev, EXT, width), F32),
            pltpu.VMEM((7, EXT, width), F32),
            pltpu.VMEM((cdev, rows, width), F32),
            pltpu.VMEM((448, 128), F32),
        ],
    )(recv, x, up, down, metric[:, None], dy)


def spread_body(taps_ref, x_ref, up_ref, down_ref, dy_ref, out_ref, ext, shifted):
    cdev, rows, width = x_ref.shape
    fill_rows(x_ref, up_ref, down_ref, ext)

    def channel(c, carry):
        fill_shifts(ext[c], shifted)
        out_ref[c] = dy_ref[c].astype(F32) + stencil(taps_ref, c, shifted, rows, True)
        return carry

    lax.fori_loop(0, cdev, channel, 0)


def spread_back(taps, dconv, up, down, dy):
    cdev, rows, width = dconv.shape
    return call(
        spread_body,
        jax.ShapeDtypeStruct((cdev, rows, width), F32),
        [smem()] + [vmem()] * 4,
        [pltpu.VMEM((cdev, EXT, width), F32), pltpu.VMEM((7, EXT, width), F32)],
    )(taps, dconv, up, down, dy)


def gelu_exact(value):
    return jax.nn.gelu(value, approximate=False)


def two_parts(value):
    high = lax.reduce_precision(value, 8, 7)
    return high.astype(BF), (value - high).astype(BF)


def to_all(block, axis):
    count = lax.axis_size(axis)
    return lax.all_to_all(jnp.broadcast_to(block[None], (count,) + block.shape), axis, 0, 0, tiled=True)


def exchange(blocks):
    return lax.all_to_all(blocks, CHAN, 0, 0, tiled=True)


def halos(first, last):
    ends = lax.axis_size(LAT) - 1
    up = lax.ppermute(last, LAT, [(i, i + 1) for i in range(ends)])
    down = lax.ppermute(first, LAT, [(i + 1, i) for i in range(ends)])
    return up, down


def with_other_core(block):
    return jnp.concatenate([block, lax.ppermute(block, "c", [(0, 1), (1, 0)])], 0)


def from_ring(block):
    count = lax.axis_size("y")
    ahead = [lax.ppermute(block, "y", [((i + k) % count, i) for i in range(count)]) for k in range(1, count)]
    return jnp.stack([block] + ahead, 0)


def to_ring(blocks):
    count = lax.axis_size("y")
    total = blocks[0].astype(F32)
    for k in range(1, count):
        total = total + lax.ppermute(blocks[k], "y", [(i, (i + k) % count) for i in range(count)]).astype(F32)
    return total


def per_device(
    block_input,
    out_grad,
    metric,
    kernel,
    conv_bias,
    ln_gain,
    ln_bias,
    w_in,
    b_in,
    w_out,
    b_out,
    layer_scale,
):
    cdev, rows, width = block_input.shape
    chans = ln_gain.shape[0]
    tokens = rows * width
    nz, ny = lax.axis_size("zl"), lax.axis_size("y")
    nchan = nz * ny
    hdev = w_in.shape[0]
    part = hdev // GROUP
    hid = part * nchan
    piece = tokens // nchan
    member = lax.axis_index(("x", "c"))
    owner = lax.axis_index(CHAN)
    gamma_f = layer_scale.astype(F32)
    gamma_own = lax.dynamic_slice_in_dim(gamma_f, owner * cdev, cdev)

    side = jnp.pad(jnp.stack(two_parts(lax.dynamic_slice_in_dim(b_in, member * part, part)), 1), ((0, part), (0, SIDE - 2)))
    mine = jnp.concatenate(
        [lax.dynamic_slice_in_dim(w_in, member * part, part), lax.dynamic_slice_in_dim(w_out, member * part, part)], 0
    )
    shards = to_all(jnp.concatenate([mine, side], 1), "zl")

    up, down = halos(block_input[:, :3], block_input[:, rows - 3 :])
    blocks = forward(kernel, conv_bias, block_input, up, down, metric, out_grad)
    blocks, shards = lax.optimization_barrier((blocks, shards))

    shards = from_ring(shards).reshape(nchan, 2 * part, chans + SIDE)
    wi = shards[:, :part, :chans].reshape(hid, chans)
    wo = shards[:, part:, :chans].reshape(hid, chans)
    bi = jnp.sum(shards[:, :part, chans : chans + 2].astype(F32), 2).reshape(hid)

    recv = exchange(blocks).reshape(chans, 2 * piece)
    pair, nhat, rstd = norm(recv, ln_gain, ln_bias, GROUP // 2)
    pair = with_other_core(lax.all_to_all(pair, "x", 0, 0, tiled=True))
    n = pair[:, :piece].reshape(GROUP * piece, chans)
    dy = pair[:, piece:].reshape(GROUP * piece, chans)

    over_last = (((1,), (1,)), ((), ()))
    over_first = (((0,), (0,)), ((), ()))
    pre = lax.dot_general(n, wi, over_last, preferred_element_type=F32) + bi
    g, back = jax.vjp(gelu_exact, pre)
    g_b = g.astype(BF)
    dmlp = (gamma_f * dy.astype(F32)).astype(BF)
    grad_g = lax.dot_general(dmlp, wo, over_last, preferred_element_type=F32)
    dpre = back(grad_g)[0].astype(BF)
    turned = jnp.roll(dpre, dpre.shape[0] // 2, 0)
    ordered = jnp.where(lax.axis_index("c") == 0, dpre, turned)
    dn = jnp.dot(ordered, wi, preferred_element_type=F32).astype(BF)
    dn = lax.all_to_all(dn.reshape(GROUP, piece, chans), ("c", "x"), 0, 0, tiled=True)
    dw_in = lax.dot_general(dpre, n, over_first, preferred_element_type=F32)
    proj = lax.dot_general(g_b, dy, over_first, preferred_element_type=F32)
    db_in = jnp.sum(dpre.astype(F32), 0)
    gam_part = jnp.sum(wo.astype(F32) * proj, 0)
    dw_out = proj * gamma_f

    side = jnp.broadcast_to(db_in.astype(BF).reshape(nchan, part, 1), (nchan, part, SIDE))
    dws = jnp.concatenate(
        [
            jnp.concatenate([dw_in.astype(BF).reshape(nchan, part, chans), side], 2),
            jnp.pad(dw_out.astype(BF).reshape(nchan, part, chans), ((0, 0), (0, 0), (0, SIDE))),
        ],
        1,
    )
    dws = to_ring(dws.reshape(ny, nz, 2 * part, chans + SIDE)).astype(BF)
    dws = lax.all_to_all(dws, "zl", 0, 0, tiled=True)
    dws = jnp.sum(dws.astype(F32), 0)

    payload = exchange(norm_back(dn, nhat, rstd, ln_gain, gam_part, nchan))
    dconv, ends, taps, extra = tap_sums(payload, block_input, up, down, metric, out_grad)
    dup, ddown = halos(ends[0], ends[1])
    grad_input = spread_back(kernel, dconv, dup, ddown, out_grad)

    small = jnp.concatenate([jnp.sum(taps, 2), extra[:, :8]], 1)
    mine = jnp.concatenate([dws.astype(BF)] + list(two_parts(small)), 1)
    other = lax.ppermute(mine, "zh", [(0, 1), (1, 0)]).astype(F32)
    wide = chans + SIDE
    count = small.shape[1]
    dws = dws + other[:, :wide]
    small = small + other[:, wide : wide + count] + other[:, wide + count :]
    mine = jnp.concatenate([dws.astype(BF)] + list(two_parts(small)), 1)
    gathered = to_all(mine, ("x", "c")).astype(F32)
    grad_w_in = gathered[:, :part, :chans].reshape(hdev, chans)
    grad_w_out = gathered[:, part:, :chans].reshape(hdev, chans)
    grad_b_in = gathered[:, :part, chans].reshape(hdev)
    small = jnp.sum(gathered[:, :, wide : wide + count] + gathered[:, :, wide + count :], 0)
    n_taps = kernel.shape[1]
    dysum = small[:, n_taps + 1]
    rest = small[:, count - 8 :]
    return (
        grad_input,
        small[:, :n_taps],
        small[:, n_taps],
        rest[:, 0] + rest[:, 1],
        rest[:, 2] + rest[:, 3],
        grad_w_in,
        grad_b_in,
        grad_w_out,
        gamma_own * dysum,
        rest[:, 4] + rest[:, 5] + b_out * dysum,
    )


def solution(mesh):
    split = Mesh(mesh.devices.reshape(2, 4, 2, 8, 4), ("zh", "x", "c", "zl", "y"))
    return jax.shard_map(
        per_device,
        mesh=split,
        in_specs=(
            P(CHAN, LAT, None),
            P(CHAN, LAT, None),
            P(LAT),
            P(CHAN, None),
            P(CHAN),
            P(),
            P(),
            P(CHAN, None),
            P(CHAN),
            P(CHAN, None),
            P(CHAN),
            P(),
        ),
        out_specs=(
            P(CHAN, LAT, None),
            P(CHAN, None),
            P(CHAN),
            P(CHAN),
            P(CHAN),
            P(CHAN, None),
            P(CHAN),
            P(CHAN, None),
            P(CHAN),
            P(CHAN),
        ),
        check_vma=False,
    )
```

```python
import functools

import jax
import jax.numpy as jnp
from jax import lax
from jax.experimental import pallas as pl
from jax.experimental.pallas import tpu as pltpu
from jax.sharding import Mesh, PartitionSpec as P

LAT = ("zh", "x", "c")
CHAN = ("zl", "y")
GROUP = 8
F32 = jnp.float32
BF = jnp.bfloat16
EXT = 16
VMEM_BYTES = 48 * 1024 * 1024
SIDE = 128


def vmem():
    return pl.BlockSpec(memory_space=pltpu.VMEM)


def smem():
    return pl.BlockSpec(memory_space=pltpu.SMEM)


def call(body, out_shape, in_specs, scratch=()):
    many = isinstance(out_shape, (list, tuple))
    return pl.pallas_call(
        body,
        out_shape=out_shape,
        in_specs=in_specs,
        out_specs=[vmem()] * len(out_shape) if many else vmem(),
        scratch_shapes=list(scratch),
        compiler_params=pltpu.CompilerParams(vmem_limit_bytes=VMEM_BYTES),
    )


def fill_rows(x_ref, up_ref, down_ref, ext):
    rows = x_ref.shape[1]
    ext[:, :3, :] = up_ref[...].astype(F32)
    ext[:, 3 : 3 + rows, :] = x_ref[...].astype(F32)
    ext[:, 3 + rows : 6 + rows, :] = down_ref[...].astype(F32)


def fill_shifts(cells, shifted):
    width = cells.shape[1]
    lane = lax.broadcasted_iota(jnp.int32, cells.shape, 1)
    for b in range(7):
        move = b - 3
        if move == 0:
            shifted[b] = cells
        else:
            turned = pltpu.roll(cells, (-move) % width, 1)
            inside = lane < width - move if move > 0 else lane >= -move
            shifted[b] = jnp.where(inside, turned, 0.0)


def stencil(taps_ref, c, shifted, rows, flip):
    total = None
    for a in range(7):
        for b in range(7):
            tap = a * 7 + b
            term = taps_ref[c, 48 - tap if flip else tap] * shifted[b, a : a + rows, :]
            total = term if total is None else total + term
    return total


def forward_body(taps_ref, bias_ref, x_ref, up_ref, down_ref, metric_ref, dy_ref, out_ref, ext, shifted, h_rows, dy_rows):
    cdev, rows, width = x_ref.shape
    fill_rows(x_ref, up_ref, down_ref, ext)
    dy_rows[...] = dy_ref[...].astype(F32)
    metric = jnp.broadcast_to(metric_ref[...], (rows, width))

    def channel(c, carry):
        fill_shifts(ext[c], shifted)
        h_rows[c] = bias_ref[c] + metric * stencil(taps_ref, c, shifted, rows, False)
        return carry

    lax.fori_loop(0, cdev, channel, 0)
    low = lax.broadcasted_iota(jnp.int32, (cdev, 128), 1) < 64
    for r in range(rows):
        h_row, dy_row = h_rows[:, r, :], dy_rows[:, r, :]
        for t in range(width // 128):
            h_tile, dy_tile = h_row[:, t * 128 : t * 128 + 128], dy_row[:, t * 128 : t * 128 + 128]
            at = (r * width + t * 128) // 64
            out_ref[at] = jnp.where(low, h_tile, pltpu.roll(dy_tile, 64, 1)).astype(BF)
            out_ref[at + 1] = jnp.where(low, pltpu.roll(h_tile, 64, 1), dy_tile).astype(BF)


def forward(taps, bias, x, up, down, metric, dy):
    cdev, rows, width = x.shape
    return call(
        forward_body,
        jax.ShapeDtypeStruct((rows * width // 64, cdev, 128), BF),
        [smem(), smem()] + [vmem()] * 5,
        [
            pltpu.VMEM((cdev, EXT, width), F32),
            pltpu.VMEM((7, EXT, width), F32),
            pltpu.VMEM((cdev, rows, width), F32),
            pltpu.VMEM((cdev, rows, width), F32),
        ],
    )(taps, bias, x, up, down, metric[:, None], dy)


def norm_body(recv_ref, gain_ref, bias_ref, pair_ref, nhat_ref, rstd_ref):
    chans, lanes = recv_ref.shape
    piece = lanes // 2
    both = recv_ref[...].astype(F32).T
    h = both[:piece]
    mean = jnp.sum(h, 1, keepdims=True) / chans
    var = jnp.sum(h * h, 1, keepdims=True) / chans - mean * mean
    rstd = 1.0 / jnp.sqrt(var + 1e-06)
    nhat = (h - mean) * rstd
    nhat_ref[...] = nhat
    rstd_ref[...] = jnp.broadcast_to(rstd, rstd_ref.shape)
    n = (nhat * gain_ref[...] + bias_ref[...]).astype(BF)
    dy = both[piece:].astype(BF)
    for k in range(pair_ref.shape[0]):
        pair_ref[k, :piece] = n
        pair_ref[k, piece:] = dy


def norm(recv, gain, bias, copies):
    chans, lanes = recv.shape
    return call(
        norm_body,
        [
            jax.ShapeDtypeStruct((copies, lanes, chans), BF),
            jax.ShapeDtypeStruct((lanes // 2, chans), F32),
            jax.ShapeDtypeStruct((lanes // 2, 128), F32),
        ],
        [vmem()] * 3,
    )(recv, gain[None], bias[None])


def norm_back_body(recv_ref, nhat_ref, rstd_ref, gain_ref, gam_ref, out_ref, flat):
    piece, chans = nhat_ref.shape
    dn = recv_ref[0].astype(F32)
    for k in range(1, recv_ref.shape[0]):
        dn = dn + recv_ref[k].astype(F32)
    nhat = nhat_ref[...]
    dnhat = dn * gain_ref[...]
    s1 = jnp.sum(dnhat, 1, keepdims=True) / chans
    s2 = jnp.sum(dnhat * nhat, 1, keepdims=True) / chans
    dh = rstd_ref[:, :1] * (dnhat - s1 - nhat * s2)
    flat[:piece] = dh
    flat[piece:] = jnp.zeros((flat.shape[0] - piece, chans), F32)
    sums = (jnp.sum(dn * nhat, 0, keepdims=True), jnp.sum(dn, 0, keepdims=True), gam_ref[...])
    for k, value in enumerate(sums):
        high = value.astype(BF).astype(F32)
        flat[piece + 2 * k : piece + 2 * k + 1] = high
        flat[piece + 2 * k + 1 : piece + 2 * k + 2] = value - high
    blocks = flat[...].T.reshape(out_ref.shape[0], 24, 128)
    one, two, three = blocks[:, :8], blocks[:, 8:16], blocks[:, 16:]
    lane = lax.broadcasted_iota(jnp.int32, one.shape, 2)
    out_ref[:, :8] = jnp.where(lane < 64, one, pltpu.roll(three, 64, 2)).astype(BF)
    last = jnp.where(lane < 72, one, jnp.where(lane < 80, pltpu.roll(two, 8, 2), pltpu.roll(three, 16, 2)))
    out_ref[:, 8:] = jnp.where(lane < 64, two, last).astype(BF)


def norm_back(recv, nhat, rstd, gain, gam, owners):
    piece, chans = nhat.shape
    return call(
        norm_back_body,
        jax.ShapeDtypeStruct((owners, 16, 128), BF),
        [vmem()] * 5,
        [pltpu.VMEM((128, chans), F32)],
    )(recv, nhat, rstd, gain[None], gam[None])


def taps_body(recv_ref, x_ref, up_ref, down_ref, metric_ref, dy_ref, dconv_ref, ends_ref, sums_ref, extra_ref, ext, shifted, dh_rows, prods):
    cdev, rows, width = x_ref.shape
    fill_rows(x_ref, up_ref, down_ref, ext)
    low16 = lax.broadcasted_iota(jnp.int32, (16, 128), 1) < 64
    low8 = lax.broadcasted_iota(jnp.int32, (8, 128), 1) < 64
    extra = jnp.zeros((8, 128), F32)
    for r in range(rows):
        for t in range(width // 128):
            at = (r * width + t * 128) // 64
            first, second = recv_ref[at].astype(F32), recv_ref[at + 1].astype(F32)
            lanes = slice(t * 128, t * 128 + 128)
            dh_rows[:16, r, lanes] = jnp.where(low16, first, pltpu.roll(second, 64, 1))
            dh_rows[16:, r, lanes] = jnp.where(low8, pltpu.roll(first[:8], 64, 1), second[:8])
            extra = extra + first[8:] + second[8:]
    for g in range(3):
        extra_ref[8 * g : 8 * g + 8] = pltpu.roll(extra, 64 - 8 * g, 1)
    metric = jnp.broadcast_to(metric_ref[...], (rows, width))

    def channel(c, carry):
        fill_shifts(ext[c], shifted)
        dh = dh_rows[c]
        dconv = metric * dh
        dconv_ref[c] = dconv
        ends_ref[0, c] = dconv[:3].astype(BF)
        ends_ref[1, c] = dconv[rows - 3 :].astype(BF)
        for a in range(7):
            for b in range(7):
                product = shifted[b, a : a + rows, :] * dconv
                prods[(a * 7 + b) * 8 : (a * 7 + b) * 8 + 8, :] = product[:, :128] + product[:, 128:]
        dy = dy_ref[c].astype(F32)
        prods[392:400, :] = dh[:, :128] + dh[:, 128:]
        prods[400:408, :] = dy[:, :128] + dy[:, 128:]
        total = prods[pl.ds(0, 56, 8), :]
        for i in range(1, 8):
            total = total + prods[pl.ds(i, 56, 8), :]
        sums_ref[c] = total
        return carry

    prods[408:, :] = jnp.zeros((prods.shape[0] - 408, 128), F32)
    lax.fori_loop(0, cdev, channel, 0)


def tap_sums(recv, x, up, down, metric, dy):
    cdev, rows, width = x.shape
    return call(
        taps_body,
        [
            jax.ShapeDtypeStruct((cdev, rows, width), F32),
            jax.ShapeDtypeStruct((2, cdev, 3, width), BF),
            jax.ShapeDtypeStruct((cdev, 56, 128), F32),
            jax.ShapeDtypeStruct((cdev, 128), F32),
        ],
        [vmem()] * 6,
        [
            pltpu.VMEM((cdev, EXT, width), F32),
            pltpu.VMEM((7, EXT, width), F32),
            pltpu.VMEM((cdev, rows, width), F32),
            pltpu.VMEM((448, 128), F32),
        ],
    )(recv, x, up, down, metric[:, None], dy)


def spread_body(taps_ref, x_ref, up_ref, down_ref, dy_ref, out_ref, ext, shifted):
    cdev, rows, width = x_ref.shape
    fill_rows(x_ref, up_ref, down_ref, ext)

    def channel(c, carry):
        fill_shifts(ext[c], shifted)
        out_ref[c] = dy_ref[c].astype(F32) + stencil(taps_ref, c, shifted, rows, True)
        return carry

    lax.fori_loop(0, cdev, channel, 0)


def spread_back(taps, dconv, up, down, dy):
    cdev, rows, width = dconv.shape
    return call(
        spread_body,
        jax.ShapeDtypeStruct((cdev, rows, width), F32),
        [smem()] + [vmem()] * 4,
        [pltpu.VMEM((cdev, EXT, width), F32), pltpu.VMEM((7, EXT, width), F32)],
    )(taps, dconv, up, down, dy)


def picks(blocks, part):
    shape = (blocks * 2 * part, blocks * part)
    row = lax.broadcasted_iota(jnp.int32, shape, 0)
    place = lax.broadcasted_iota(jnp.int32, shape, 1)
    block = jnp.floor((row.astype(F32) + 0.5) * (0.5 / part)).astype(jnp.int32)
    inside = row - block * 2 * part
    first = (inside < part) & (place == block * part + inside)
    second = (inside >= part) & (place == block * part + inside - part)
    return [jnp.where(m, 1.0, 0.0).astype(BF) for m in (first, second)]


def dot(a, b, a_dim, b_dim):
    return lax.dot_general(a, b, (((a_dim,), (b_dim,)), ((), ())), preferred_element_type=F32)


def weights_body(part, own_ref, one_ref, two_ref, three_ref, wi_ref, wo_ref, bi_ref, rows):
    blocks = 0
    for ref in (own_ref, one_ref, two_ref, three_ref):
        for k in range(ref.shape[0]):
            at = blocks * 2 * part
            rows[at : at + 2 * part] = ref[k].astype(F32)
            blocks += 1
    chans = wi_ref.shape[1]
    flat = rows[...].astype(BF)
    first, second = picks(blocks, part)
    wi_ref[...] = dot(first, flat[:, :chans], 0, 0).astype(BF)
    wo_ref[...] = dot(second, flat[:, :chans], 0, 0).astype(BF)
    both = dot(flat[:, chans:], first, 0, 0)
    bi_ref[...] = both[:1] + both[1:2]


def weights(parts, part, chans):
    blocks = sum(p.shape[0] for p in parts)
    return call(
        functools.partial(weights_body, part),
        [
            jax.ShapeDtypeStruct((blocks * part, chans), BF),
            jax.ShapeDtypeStruct((blocks * part, chans), BF),
            jax.ShapeDtypeStruct((1, blocks * part), F32),
        ],
        [vmem()] * 4,
        [pltpu.VMEM((blocks * 2 * part, parts[0].shape[2]), F32)],
    )(*parts)


def mlp_body(core_ref, own_ref, other_ref, wi_ref, wo_ref, bi_ref, gamma_ref, dn_ref, n_ref, dy_ref, g_ref, dpre_ref):
    members, lanes, _ = own_ref.shape
    piece = lanes // 2
    for at, ref in ((0, own_ref), (members, other_ref)):
        for k in range(members):
            n_ref[(at + k) * piece : (at + k + 1) * piece] = ref[k, :piece]
            dy_ref[(at + k) * piece : (at + k + 1) * piece] = ref[k, piece:]
    pre = dot(n_ref[...], wi_ref[...], 1, 1) + bi_ref[...]
    cdf = 0.5 + 0.5 * lax.erf(pre * (0.5**0.5))
    g_ref[...] = (pre * cdf).astype(BF)
    slope = cdf + pre * (jnp.exp(-0.5 * pre * pre) * (0.5 / 3.141592653589793) ** 0.5)
    dmlp = (gamma_ref[...] * dy_ref[...].astype(F32)).astype(BF)
    dpre = (slope * dot(dmlp, wo_ref[...], 1, 1)).astype(BF)
    dpre_ref[...] = dpre
    dn = dot(dpre, wi_ref[...], 1, 0).astype(BF)
    core = core_ref[0]
    for k in range(members):
        dn_ref[core * members + k] = dn[k * piece : (k + 1) * piece]
        dn_ref[(1 - core) * members + k] = dn[(members + k) * piece : (members + k + 1) * piece]


def mlp(core, own, other, wi, wo, bi, gamma):
    members, lanes, chans = own.shape
    toks, hid = members * lanes, wi.shape[0]
    return call(
        mlp_body,
        [
            jax.ShapeDtypeStruct((2 * members, lanes // 2, chans), BF),
            jax.ShapeDtypeStruct((toks, chans), BF),
            jax.ShapeDtypeStruct((toks, chans), BF),
            jax.ShapeDtypeStruct((toks, hid), BF),
            jax.ShapeDtypeStruct((toks, hid), BF),
        ],
        [smem()] + [vmem()] * 6,
    )(core, own, other, wi, wo, bi, gamma[None])


def grads_body(part, n_ref, dy_ref, g_ref, dpre_ref, wo_ref, gamma_ref, out_ref, gam_ref):
    toks, chans = n_ref.shape
    hid = g_ref.shape[1]
    first, second = picks(hid // part, part)
    dw_in = dot(dpre_ref[...], n_ref[...], 0, 0).astype(BF)
    proj = dot(g_ref[...], dy_ref[...], 0, 0)
    gam_ref[...] = jnp.sum(wo_ref[...].astype(F32) * proj, 0, keepdims=True)
    dw_out = (proj * gamma_ref[...]).astype(BF)
    out_ref[:, :chans] = (dot(first, dw_in, 1, 0) + dot(second, dw_out, 1, 0)).astype(BF)
    ones = jnp.ones((toks, out_ref.shape[1] - chans), BF)
    out_ref[:, chans:] = dot(first, dot(dpre_ref[...], ones, 0, 0).astype(BF), 1, 0).astype(BF)


def grads(part, side, n, dy, g, dpre, wo, gamma):
    toks, chans = n.shape
    return call(
        functools.partial(grads_body, part),
        [jax.ShapeDtypeStruct((2 * g.shape[1], chans + side), BF), jax.ShapeDtypeStruct((1, chans), F32)],
        [vmem()] * 6,
    )(n, dy, g, dpre, wo, gamma[None])


def two_parts(value):
    high = lax.reduce_precision(value, 8, 7)
    return high.astype(BF), (value - high).astype(BF)


def to_all(block, axis):
    count = lax.axis_size(axis)
    return lax.all_to_all(jnp.broadcast_to(block[None], (count,) + block.shape), axis, 0, 0, tiled=True)


def exchange(blocks):
    return lax.all_to_all(blocks, CHAN, 0, 0, tiled=True)


def halos(first, last):
    count = lax.axis_size(LAT)
    place = lax.axis_index(LAT)
    even = place % 2 == 0
    pairs = [(i, i + 1) for i in range(0, count, 2)]
    within = lax.ppermute(jnp.where(even, last, first), LAT, pairs + [(j, i) for i, j in pairs])
    pairs = [(i, i + 1) for i in range(1, count - 1, 2)]
    across = lax.ppermute(jnp.where(even, first, last), LAT, pairs + [(j, i) for i, j in pairs])
    return jnp.where(even, across, within), jnp.where(even, within, across)


def from_ring(block):
    count = lax.axis_size("y")
    ahead = [lax.ppermute(block, "y", [((i + k) % count, i) for i in range(count)]) for k in range(1, count)]
    return [block] + ahead


def to_ring(blocks):
    count = lax.axis_size("y")
    total = blocks[0].astype(F32)
    for k in range(1, count):
        total = total + lax.ppermute(blocks[k], "y", [(i, (i + k) % count) for i in range(count)]).astype(F32)
    return total


def per_device(
    block_input,
    out_grad,
    metric,
    kernel,
    conv_bias,
    ln_gain,
    ln_bias,
    w_in,
    b_in,
    w_out,
    b_out,
    layer_scale,
):
    cdev, rows, width = block_input.shape
    chans = ln_gain.shape[0]
    tokens = rows * width
    nz, ny = lax.axis_size("zl"), lax.axis_size("y")
    nchan = nz * ny
    hdev = w_in.shape[0]
    part = hdev // GROUP
    piece = tokens // nchan
    member = lax.axis_index(("x", "c"))
    owner = lax.axis_index(CHAN)
    gamma_f = layer_scale.astype(F32)
    gamma_own = lax.dynamic_slice_in_dim(gamma_f, owner * cdev, cdev)

    side = jnp.pad(jnp.stack(two_parts(lax.dynamic_slice_in_dim(b_in, member * part, part)), 1), ((0, part), (0, SIDE - 2)))
    mine = jnp.concatenate(
        [lax.dynamic_slice_in_dim(w_in, member * part, part), lax.dynamic_slice_in_dim(w_out, member * part, part)], 0
    )
    shards = to_all(jnp.concatenate([mine, side], 1), "zl")

    up, down = halos(block_input[:, :3], block_input[:, rows - 3 :])
    blocks = forward(kernel, conv_bias, block_input, up, down, metric, out_grad)
    blocks, shards = lax.optimization_barrier((blocks, shards))

    recv = exchange(blocks)
    wi, wo, bi = weights(from_ring(shards), part, chans)

    recv, wi, wo, bi = lax.optimization_barrier((recv, wi, wo, bi))
    recv = recv.reshape(chans, 2 * piece)
    pair, nhat, rstd = norm(recv, ln_gain, ln_bias, GROUP // 2)
    pair = lax.all_to_all(pair, "x", 0, 0, tiled=True)
    other = lax.ppermute(pair, "c", [(0, 1), (1, 0)])

    core = lax.axis_index("c").astype(jnp.int32)[None]
    dn, n, dy, g, dpre = mlp(core, pair, other, wi, wo, bi, gamma_f)
    dn = lax.all_to_all(dn, ("c", "x"), 0, 0, tiled=True)

    dws, gam_part = grads(part, SIDE, n, dy, g, dpre, wo, gamma_f)
    dws = to_ring(dws.reshape(ny, nz, 2 * part, chans + SIDE)).astype(BF)
    dws = lax.all_to_all(dws, "zl", 0, 0, tiled=True)
    dws = jnp.sum(dws.astype(F32), 0)

    payload = exchange(norm_back(dn, nhat, rstd, ln_gain, gam_part[0], nchan))
    dconv, ends, taps, extra = tap_sums(payload, block_input, up, down, metric, out_grad)
    dup, ddown = halos(ends[0], ends[1])

    small = jnp.concatenate([jnp.sum(taps, 2), extra[:, :8]], 1)
    mine = jnp.concatenate([dws.astype(BF)] + list(two_parts(small)), 1)
    other = lax.ppermute(mine, "zh", [(0, 1), (1, 0)]).astype(F32)
    wide = chans + SIDE
    count = small.shape[1]
    dws = dws + other[:, :wide]
    small = small + other[:, wide : wide + count] + other[:, wide + count :]
    mine = jnp.concatenate([dws.astype(BF)] + list(two_parts(small)), 1)
    mine, dup, ddown = lax.optimization_barrier((mine, dup, ddown))
    grad_input = spread_back(kernel, dconv, dup, ddown, out_grad)
    gathered = to_all(mine, ("x", "c")).astype(F32)
    grad_w_in = gathered[:, :part, :chans].reshape(hdev, chans)
    grad_w_out = gathered[:, part:, :chans].reshape(hdev, chans)
    grad_b_in = gathered[:, :part, chans].reshape(hdev)
    small = jnp.sum(gathered[:, :, wide : wide + count] + gathered[:, :, wide + count :], 0)
    n_taps = kernel.shape[1]
    dysum = small[:, n_taps + 1]
    rest = small[:, count - 8 :]
    return (
        grad_input,
        small[:, :n_taps],
        small[:, n_taps],
        rest[:, 0] + rest[:, 1],
        rest[:, 2] + rest[:, 3],
        grad_w_in,
        grad_b_in,
        grad_w_out,
        gamma_own * dysum,
        rest[:, 4] + rest[:, 5] + b_out * dysum,
    )


def solution(mesh):
    split = Mesh(mesh.devices.reshape(2, 4, 2, 8, 4), ("zh", "x", "c", "zl", "y"))
    return jax.shard_map(
        per_device,
        mesh=split,
        in_specs=(
            P(CHAN, LAT, None),
            P(CHAN, LAT, None),
            P(LAT),
            P(CHAN, None),
            P(CHAN),
            P(),
            P(),
            P(CHAN, None),
            P(CHAN),
            P(CHAN, None),
            P(CHAN),
            P(),
        ),
        out_specs=(
            P(CHAN, LAT, None),
            P(CHAN, None),
            P(CHAN),
            P(CHAN),
            P(CHAN),
            P(CHAN, None),
            P(CHAN),
            P(CHAN, None),
            P(CHAN),
            P(CHAN),
        ),
        check_vma=False,
    )
```

```python
import functools

import jax
import jax.numpy as jnp
from jax import lax
from jax.experimental import pallas as pl
from jax.experimental.pallas import tpu as pltpu
from jax.sharding import Mesh, PartitionSpec as P

LAT = ("zh", "x", "c")
CHAN = ("zl", "y")
GROUP = 8
F32 = jnp.float32
BF = jnp.bfloat16
EXT = 16
VMEM_BYTES = 20 * 1024 * 1024
SIDE = 128


def vmem():
    return pl.BlockSpec(memory_space=pltpu.VMEM)


def smem():
    return pl.BlockSpec(memory_space=pltpu.SMEM)


def call(body, out_shape, in_specs, scratch=()):
    many = isinstance(out_shape, (list, tuple))
    return pl.pallas_call(
        body,
        out_shape=out_shape,
        in_specs=in_specs,
        out_specs=[vmem()] * len(out_shape) if many else vmem(),
        scratch_shapes=list(scratch),
        compiler_params=pltpu.CompilerParams(vmem_limit_bytes=VMEM_BYTES),
    )


def fill_rows(x_ref, up_ref, down_ref, ext):
    rows = x_ref.shape[1]
    ext[:, :3, :] = up_ref[...].astype(F32)
    ext[:, 3 : 3 + rows, :] = x_ref[...].astype(F32)
    ext[:, 3 + rows : 6 + rows, :] = down_ref[...].astype(F32)


def row_shifts(ext, c, rows):
    return [ext[c, a : a + rows, :] for a in range(7)]


def along(cells, move):
    width = cells.shape[1]
    if move == 0:
        return cells
    lane = lax.broadcasted_iota(jnp.int32, cells.shape, 1)
    inside = lane < width - move if move > 0 else lane >= -move
    return jnp.where(inside, pltpu.roll(cells, (-move) % width, 1), 0.0)


def stencil(taps_ref, c, shifts, flip):
    total = None
    for b in range(7):
        column = None
        for a in range(7):
            tap = a * 7 + b
            term = taps_ref[c, 48 - tap if flip else tap] * shifts[a]
            column = term if column is None else column + term
        column = along(column, b - 3)
        total = column if total is None else total + column
    return total


def forward_body(taps_ref, bias_ref, x_ref, up_ref, down_ref, metric_ref, dy_ref, out_ref, ext, h_rows, dy_rows):
    cdev, rows, width = x_ref.shape
    fill_rows(x_ref, up_ref, down_ref, ext)
    dy_rows[...] = dy_ref[...].astype(F32)
    metric = jnp.broadcast_to(metric_ref[...], (rows, width))

    def channel(c, carry):
        h_rows[c] = bias_ref[c] + metric * stencil(taps_ref, c, row_shifts(ext, c, rows), False)
        return carry

    lax.fori_loop(0, cdev, channel, 0)
    low = lax.broadcasted_iota(jnp.int32, (cdev, 128), 1) < 64
    for r in range(rows):
        h_row, dy_row = h_rows[:, r, :], dy_rows[:, r, :]
        for t in range(width // 128):
            h_tile, dy_tile = h_row[:, t * 128 : t * 128 + 128], dy_row[:, t * 128 : t * 128 + 128]
            at = (r * width + t * 128) // 64
            out_ref[at] = jnp.where(low, h_tile, pltpu.roll(dy_tile, 64, 1)).astype(BF)
            out_ref[at + 1] = jnp.where(low, pltpu.roll(h_tile, 64, 1), dy_tile).astype(BF)


def forward(taps, bias, x, up, down, metric, dy):
    cdev, rows, width = x.shape
    return call(
        forward_body,
        jax.ShapeDtypeStruct((rows * width // 64, cdev, 128), BF),
        [smem(), smem()] + [vmem()] * 5,
        [
            pltpu.VMEM((cdev, EXT, width), F32),
            pltpu.VMEM((cdev, rows, width), F32),
            pltpu.VMEM((cdev, rows, width), F32),
        ],
    )(taps, bias, x, up, down, metric[:, None], dy)


def norm_body(recv_ref, gain_ref, bias_ref, pair_ref, nhat_ref, rstd_ref):
    chans, lanes = recv_ref.shape
    piece = lanes // 2
    both = recv_ref[...].astype(F32).T
    h = both[:piece]
    mean = jnp.sum(h, 1, keepdims=True) / chans
    var = jnp.sum(h * h, 1, keepdims=True) / chans - mean * mean
    rstd = 1.0 / jnp.sqrt(var + 1e-06)
    nhat = (h - mean) * rstd
    nhat_ref[...] = nhat
    rstd_ref[...] = jnp.broadcast_to(rstd, rstd_ref.shape)
    n = (nhat * gain_ref[...] + bias_ref[...]).astype(BF)
    dy = both[piece:].astype(BF)
    for k in range(pair_ref.shape[0]):
        pair_ref[k, :piece] = n
        pair_ref[k, piece:] = dy


def norm(recv, gain, bias, copies):
    chans, lanes = recv.shape
    return call(
        norm_body,
        [
            jax.ShapeDtypeStruct((copies, lanes, chans), BF),
            jax.ShapeDtypeStruct((lanes // 2, chans), F32),
            jax.ShapeDtypeStruct((lanes // 2, 128), F32),
        ],
        [vmem()] * 3,
    )(recv, gain[None], bias[None])


def norm_back_body(recv_ref, nhat_ref, rstd_ref, gain_ref, gam_ref, db_ref, out_ref, flat):
    piece, chans = nhat_ref.shape
    dn = recv_ref[0].astype(F32)
    for k in range(1, recv_ref.shape[0]):
        dn = dn + recv_ref[k].astype(F32)
    nhat = nhat_ref[...]
    dnhat = dn * gain_ref[...]
    s1 = jnp.sum(dnhat, 1, keepdims=True) / chans
    s2 = jnp.sum(dnhat * nhat, 1, keepdims=True) / chans
    dh = rstd_ref[:, :1] * (dnhat - s1 - nhat * s2)
    flat[:piece] = dh
    flat[piece:] = jnp.zeros((flat.shape[0] - piece, chans), F32)
    sums = (jnp.sum(dn * nhat, 0, keepdims=True), jnp.sum(dn, 0, keepdims=True), gam_ref[...], db_ref[...])
    for k, value in enumerate(sums):
        high = value.astype(BF).astype(F32)
        flat[piece + 2 * k : piece + 2 * k + 1] = high
        flat[piece + 2 * k + 1 : piece + 2 * k + 2] = value - high
    blocks = flat[...].T.reshape(out_ref.shape[0], 24, 128)
    one, two, three = blocks[:, :8], blocks[:, 8:16], blocks[:, 16:]
    lane = lax.broadcasted_iota(jnp.int32, one.shape, 2)
    out_ref[:, :8] = jnp.where(lane < 64, one, pltpu.roll(three, 64, 2)).astype(BF)
    last = jnp.where(lane < 72, one, jnp.where(lane < 80, pltpu.roll(two, 8, 2), pltpu.roll(three, 16, 2)))
    out_ref[:, 8:] = jnp.where(lane < 64, two, last).astype(BF)


def norm_back(recv, nhat, rstd, gain, gam, db, owners):
    piece, chans = nhat.shape
    return call(
        norm_back_body,
        jax.ShapeDtypeStruct((owners, 16, 128), BF),
        [vmem()] * 6,
        [pltpu.VMEM((128, chans), F32)],
    )(recv, nhat, rstd, gain[None], gam, db)


def taps_body(recv_ref, x_ref, up_ref, down_ref, metric_ref, dy_ref, dconv_ref, ends_ref, sums_ref, extra_ref, ext, dh_rows, prods):
    cdev, rows, width = x_ref.shape
    fill_rows(x_ref, up_ref, down_ref, ext)
    low16 = lax.broadcasted_iota(jnp.int32, (16, 128), 1) < 64
    low8 = lax.broadcasted_iota(jnp.int32, (8, 128), 1) < 64
    extra = jnp.zeros((8, 128), F32)
    for r in range(rows):
        for t in range(width // 128):
            at = (r * width + t * 128) // 64
            first, second = recv_ref[at].astype(F32), recv_ref[at + 1].astype(F32)
            lanes = slice(t * 128, t * 128 + 128)
            dh_rows[:16, r, lanes] = jnp.where(low16, first, pltpu.roll(second, 64, 1))
            dh_rows[16:, r, lanes] = jnp.where(low8, pltpu.roll(first[:8], 64, 1), second[:8])
            extra = extra + first[8:] + second[8:]
    for g in range(3):
        extra_ref[8 * g : 8 * g + 8] = pltpu.roll(extra, 64 - 8 * g, 1)
    metric = jnp.broadcast_to(metric_ref[...], (rows, width))

    def channel(c, carry):
        dh = dh_rows[c]
        dconv = metric * dh
        dconv_ref[c] = dconv
        ends_ref[0, c] = dconv[:3].astype(BF)
        ends_ref[1, c] = dconv[rows - 3 :].astype(BF)
        shifts = row_shifts(ext, c, rows)
        for b in range(7):
            moved = along(dconv, 3 - b)
            for a in range(7):
                product = shifts[a] * moved
                prods[(a * 7 + b) * 8 : (a * 7 + b) * 8 + 8, :] = product[:, :128] + product[:, 128:]
        dy = dy_ref[c].astype(F32)
        prods[392:400, :] = dh[:, :128] + dh[:, 128:]
        prods[400:408, :] = dy[:, :128] + dy[:, 128:]
        total = prods[pl.ds(0, 56, 8), :]
        for i in range(1, 8):
            total = total + prods[pl.ds(i, 56, 8), :]
        sums_ref[c] = total
        return carry

    prods[408:, :] = jnp.zeros((prods.shape[0] - 408, 128), F32)
    lax.fori_loop(0, cdev, channel, 0)


def tap_sums(recv, x, up, down, metric, dy):
    cdev, rows, width = x.shape
    return call(
        taps_body,
        [
            jax.ShapeDtypeStruct((cdev, rows, width), F32),
            jax.ShapeDtypeStruct((2, cdev, 3, width), BF),
            jax.ShapeDtypeStruct((cdev, 56, 128), F32),
            jax.ShapeDtypeStruct((cdev, 128), F32),
        ],
        [vmem()] * 6,
        [
            pltpu.VMEM((cdev, EXT, width), F32),
            pltpu.VMEM((cdev, rows, width), F32),
            pltpu.VMEM((448, 128), F32),
        ],
    )(recv, x, up, down, metric[:, None], dy)


def spread_body(taps_ref, x_ref, up_ref, down_ref, dy_ref, out_ref, ext):
    cdev, rows, width = x_ref.shape
    fill_rows(x_ref, up_ref, down_ref, ext)

    def channel(c, carry):
        out_ref[c] = dy_ref[c].astype(F32) + stencil(taps_ref, c, row_shifts(ext, c, rows), True)
        return carry

    lax.fori_loop(0, cdev, channel, 0)


def spread_back(taps, dconv, up, down, dy):
    cdev, rows, width = dconv.shape
    return call(
        spread_body,
        jax.ShapeDtypeStruct((cdev, rows, width), F32),
        [smem()] + [vmem()] * 4,
        [pltpu.VMEM((cdev, EXT, width), F32)],
    )(taps, dconv, up, down, dy)


def picks(blocks, part):
    shape = (blocks * 2 * part, blocks * part)
    row = lax.broadcasted_iota(jnp.int32, shape, 0)
    place = lax.broadcasted_iota(jnp.int32, shape, 1)
    block = jnp.floor((row.astype(F32) + 0.5) * (0.5 / part)).astype(jnp.int32)
    inside = row - block * 2 * part
    first = (inside < part) & (place == block * part + inside)
    second = (inside >= part) & (place == block * part + inside - part)
    return [jnp.where(m, 1.0, 0.0).astype(BF) for m in (first, second)]


def dot(a, b, a_dim, b_dim):
    return lax.dot_general(a, b, (((a_dim,), (b_dim,)), ((), ())), preferred_element_type=F32)


def weights_body(part, own_ref, one_ref, two_ref, three_ref, wi_ref, wo_ref, bi_ref, rows):
    blocks = 0
    for ref in (own_ref, one_ref, two_ref, three_ref):
        for k in range(ref.shape[0]):
            at = blocks * 2 * part
            rows[at : at + 2 * part] = ref[k].astype(F32)
            blocks += 1
    chans = wi_ref.shape[1]
    flat = rows[...].astype(BF)
    first, second = picks(blocks, part)
    wi_ref[...] = dot(first, flat[:, :chans], 0, 0).astype(BF)
    wo_ref[...] = dot(second, flat[:, :chans], 0, 0).astype(BF)
    both = dot(flat[:, chans:], first, 0, 0)
    bi_ref[...] = both[:1] + both[1:2]


def weights(parts, part, chans):
    blocks = sum(p.shape[0] for p in parts)
    return call(
        functools.partial(weights_body, part),
        [
            jax.ShapeDtypeStruct((blocks * part, chans), BF),
            jax.ShapeDtypeStruct((blocks * part, chans), BF),
            jax.ShapeDtypeStruct((1, blocks * part), F32),
        ],
        [vmem()] * 4,
        [pltpu.VMEM((blocks * 2 * part, parts[0].shape[2]), F32)],
    )(*parts)


def mlp_body(core_ref, own_ref, other_ref, wi_ref, wo_ref, bi_ref, gamma_ref, dn_ref, n_ref, dy_ref, g_ref, dpre_ref):
    members, lanes, _ = own_ref.shape
    piece = lanes // 2
    for at, ref in ((0, own_ref), (members, other_ref)):
        for k in range(members):
            n_ref[(at + k) * piece : (at + k + 1) * piece] = ref[k, :piece]
            dy_ref[(at + k) * piece : (at + k + 1) * piece] = ref[k, piece:]
    pre = dot(n_ref[...], wi_ref[...], 1, 1) + bi_ref[...]
    cdf = 0.5 + 0.5 * lax.erf(pre * (0.5**0.5))
    g_ref[...] = (pre * cdf).astype(BF)
    slope = cdf + pre * (jnp.exp(-0.5 * pre * pre) * (0.5 / 3.141592653589793) ** 0.5)
    dmlp = (gamma_ref[...] * dy_ref[...].astype(F32)).astype(BF)
    dpre = (slope * dot(dmlp, wo_ref[...], 1, 1)).astype(BF)
    dpre_ref[...] = dpre
    dn = dot(dpre, wi_ref[...], 1, 0).astype(BF)
    core = core_ref[0]
    for k in range(members):
        dn_ref[core * members + k] = dn[k * piece : (k + 1) * piece]
        dn_ref[(1 - core) * members + k] = dn[(members + k) * piece : (members + k + 1) * piece]


def mlp(core, own, other, wi, wo, bi, gamma):
    members, lanes, chans = own.shape
    toks, hid = members * lanes, wi.shape[0]
    return call(
        mlp_body,
        [
            jax.ShapeDtypeStruct((2 * members, lanes // 2, chans), BF),
            jax.ShapeDtypeStruct((toks, chans), BF),
            jax.ShapeDtypeStruct((toks, chans), BF),
            jax.ShapeDtypeStruct((toks, hid), BF),
            jax.ShapeDtypeStruct((toks, hid), BF),
        ],
        [smem()] + [vmem()] * 6,
    )(core, own, other, wi, wo, bi, gamma[None])


def grads_body(part, ny, y_ref, n_ref, dy_ref, g_ref, dpre_ref, wo_ref, gamma_ref, out_ref, gam_ref, db_ref):
    toks = n_ref.shape[0]
    hid = g_ref.shape[1]
    first, second = picks(hid // part, part)
    dw_in = dot(dpre_ref[...], n_ref[...], 0, 0).astype(BF)
    proj = dot(g_ref[...], dy_ref[...], 0, 0)
    gam_ref[...] = jnp.sum(wo_ref[...].astype(F32) * proj, 0, keepdims=True)
    dw_out = (proj * gamma_ref[...]).astype(BF)
    out_ref[...] = (dot(first, dw_in, 1, 0) + dot(second, dw_out, 1, 0)).astype(BF)
    nz = hid // part // ny
    lane = lax.broadcasted_iota(jnp.int32, (db_ref.shape[1], hid), 0)
    place = lax.broadcasted_iota(jnp.int32, (1, hid), 1)
    block = jnp.floor((place.astype(F32) + 0.5) * (1.0 / part)).astype(jnp.int32)
    ring = jnp.floor((block.astype(F32) + 0.5) * (1.0 / nz)).astype(jnp.int32)
    ahead = ring + y_ref[0]
    owner = (block - ring * nz) * ny + jnp.where(ahead >= ny, ahead - ny, ahead)
    spot = jnp.where(lane == owner * 2 * part + place - block * part, 1.0, 0.0).astype(BF)
    db = dot(jnp.ones((16, toks), BF), dpre_ref[...], 1, 0).astype(BF)
    db_ref[...] = dot(db, spot, 1, 1)[:1]


def grads(part, ny, y, n, dy, g, dpre, wo, gamma):
    toks, chans = n.shape
    return call(
        functools.partial(grads_body, part, ny),
        [
            jax.ShapeDtypeStruct((2 * g.shape[1], chans), BF),
            jax.ShapeDtypeStruct((1, chans), F32),
            jax.ShapeDtypeStruct((1, 2 * g.shape[1]), F32),
        ],
        [smem()] + [vmem()] * 6,
    )(y, n, dy, g, dpre, wo, gamma[None])


def slices_body(part, member_ref, w_in_ref, w_out_ref, b_ref, out_ref):
    hdev, chans = w_in_ref.shape
    row = lax.broadcasted_iota(jnp.int32, (2 * part, hdev), 0)
    place = lax.broadcasted_iota(jnp.int32, (2 * part, hdev), 1)
    start = member_ref[0] * part
    first = jnp.where((row < part) & (place == start + row), 1.0, 0.0).astype(BF)
    second = jnp.where((row >= part) & (place == start + row - part), 1.0, 0.0).astype(BF)
    rows = (dot(first, w_in_ref[...], 1, 0) + dot(second, w_out_ref[...], 1, 0)).astype(BF)
    bias = jnp.broadcast_to(b_ref[...], (SIDE, hdev))
    high = bias.astype(BF)
    low = (bias - high.astype(F32)).astype(BF)
    line = lax.broadcasted_iota(jnp.int32, (SIDE, hdev), 0)
    high = jnp.where(line == 0, high.astype(F32), jnp.where(line == 1, low.astype(F32), 0.0)).astype(BF)
    side = dot(first, high, 1, 1).astype(BF)
    for k in range(out_ref.shape[0]):
        out_ref[k, :, :chans] = rows
        out_ref[k, :, chans:] = side


def slices(part, copies, member, w_in, w_out, b_in):
    return call(
        functools.partial(slices_body, part),
        jax.ShapeDtypeStruct((copies, 2 * part, w_in.shape[1] + SIDE), BF),
        [smem()] + [vmem()] * 3,
    )(member, w_in, w_out, b_in[None])


def results_body(part, gathered_ref, dw_in_ref, dw_out_ref, side_ref, total_ref):
    chans = dw_in_ref.shape[1]
    total = None
    for k in range(gathered_ref.shape[0]):
        block = gathered_ref[k].astype(F32)
        dw_in_ref[k * part : (k + 1) * part] = block[:part, :chans]
        dw_out_ref[k * part : (k + 1) * part] = block[part:, :chans]
        side = block[:, chans:]
        side = side + pltpu.roll(side, 64, 1)
        side_ref[k] = side
        total = side if total is None else total + side
    total_ref[...] = total


def results(part, gathered, chans):
    members, rows, lanes = gathered.shape
    return call(
        functools.partial(results_body, part),
        [
            jax.ShapeDtypeStruct((members * part, chans), F32),
            jax.ShapeDtypeStruct((members * part, chans), F32),
            jax.ShapeDtypeStruct((members, rows, lanes - chans), F32),
            jax.ShapeDtypeStruct((rows, lanes - chans), F32),
        ],
        [vmem()],
    )(gathered)


def two_parts(value):
    high = lax.reduce_precision(value, 8, 7)
    return high.astype(BF), (value - high).astype(BF)


def to_all(block, axis):
    count = lax.axis_size(axis)
    return lax.all_to_all(jnp.broadcast_to(block[None], (count,) + block.shape), axis, 0, 0, tiled=True)


def exchange(blocks):
    return lax.all_to_all(blocks, CHAN, 0, 0, tiled=True)


def halos(first, last):
    count = lax.axis_size(LAT)
    place = lax.axis_index(LAT)
    even = place % 2 == 0
    pairs = [(i, i + 1) for i in range(0, count, 2)]
    within = lax.ppermute(jnp.where(even, last, first), LAT, pairs + [(j, i) for i, j in pairs])
    pairs = [(i, i + 1) for i in range(1, count - 1, 2)]
    across = lax.ppermute(jnp.where(even, first, last), LAT, pairs + [(j, i) for i, j in pairs])
    return jnp.where(even, across, within), jnp.where(even, within, across)


def from_ring(block):
    count = lax.axis_size("y")
    ahead = [lax.ppermute(block, "y", [((i + k) % count, i) for i in range(count)]) for k in range(1, count)]
    return [block] + ahead


def to_ring(blocks):
    count = lax.axis_size("y")
    total = blocks[0].astype(F32)
    for k in range(1, count):
        total = total + lax.ppermute(blocks[k], "y", [(i, (i + k) % count) for i in range(count)]).astype(F32)
    return total


def per_device(
    block_input,
    out_grad,
    metric,
    kernel,
    conv_bias,
    ln_gain,
    ln_bias,
    w_in,
    b_in,
    w_out,
    b_out,
    layer_scale,
):
    cdev, rows, width = block_input.shape
    chans = ln_gain.shape[0]
    tokens = rows * width
    nz, ny = lax.axis_size("zl"), lax.axis_size("y")
    nchan = nz * ny
    hdev = w_in.shape[0]
    part = hdev // GROUP
    piece = tokens // nchan
    owner = lax.axis_index(CHAN)
    gamma_f = layer_scale.astype(F32)
    gamma_own = lax.dynamic_slice_in_dim(gamma_f, owner * cdev, cdev)

    member = lax.axis_index(("x", "c")).astype(jnp.int32)[None]
    shards = lax.all_to_all(slices(part, nz, member, w_in, w_out, b_in), "zl", 0, 0, tiled=True)

    up, down = halos(block_input[:, :3], block_input[:, rows - 3 :])
    blocks = forward(kernel, conv_bias, block_input, up, down, metric, out_grad)
    blocks, shards = lax.optimization_barrier((blocks, shards))

    recv = exchange(blocks)
    wi, wo, bi = weights(from_ring(shards), part, chans)

    recv = recv.reshape(chans, 2 * piece)
    pair, nhat, rstd = norm(recv, ln_gain, ln_bias, GROUP // 2)
    pair = lax.all_to_all(pair, "x", 0, 0, tiled=True)
    other = lax.ppermute(pair, "c", [(0, 1), (1, 0)])

    core = lax.axis_index("c").astype(jnp.int32)[None]
    dn, n, dy, g, dpre = mlp(core, pair, other, wi, wo, bi, gamma_f)
    dn = lax.all_to_all(dn, ("c", "x"), 0, 0, tiled=True)

    dws, gam_part, db_part = grads(part, ny, lax.axis_index("y").astype(jnp.int32)[None], n, dy, g, dpre, wo, gamma_f)
    dws = to_ring(dws.reshape(ny, nz, 2 * part, chans)).astype(BF)
    dws = lax.all_to_all(dws, "zl", 0, 0, tiled=True)
    dws = jnp.sum(dws.astype(F32), 0)

    payload = exchange(norm_back(dn, nhat, rstd, ln_gain, gam_part, db_part, nchan))
    dconv, ends, taps, extra = tap_sums(payload, block_input, up, down, metric, out_grad)
    dup, ddown = halos(ends[0], ends[1])

    small = jnp.concatenate([jnp.sum(taps, 2), extra[:, :8]], 1)
    mine = jnp.concatenate([dws.astype(BF)] + list(two_parts(small)), 1)
    other = lax.ppermute(mine, "zh", [(0, 1), (1, 0)]).astype(F32)
    count = small.shape[1]
    dws = dws + other[:, :chans]
    small = small + other[:, chans : chans + count] + other[:, chans + count :]
    mine = jnp.concatenate([dws.astype(BF)] + list(two_parts(small)), 1)
    mine, dup, ddown = lax.optimization_barrier((mine, dup, ddown))
    grad_input = spread_back(kernel, dconv, dup, ddown, out_grad)
    grad_w_in, grad_w_out, side, small = results(part, to_all(mine, ("x", "c")), chans)
    n_taps = kernel.shape[1]
    dysum = small[:, n_taps + 1]
    rest = small[:, count - 8 : count]
    return (
        grad_input,
        small[:, :n_taps],
        small[:, n_taps],
        rest[:, 0] + rest[:, 1],
        rest[:, 2] + rest[:, 3],
        grad_w_in,
        (side[:, :part, count - 2] + side[:, :part, count - 1]).reshape(hdev),
        grad_w_out,
        gamma_own * dysum,
        rest[:, 4] + rest[:, 5] + b_out * dysum,
    )


def solution(mesh):
    split = Mesh(mesh.devices.reshape(2, 4, 2, 8, 4), ("zh", "x", "c", "zl", "y"))
    return jax.shard_map(
        per_device,
        mesh=split,
        in_specs=(
            P(CHAN, LAT, None),
            P(CHAN, LAT, None),
            P(LAT),
            P(CHAN, None),
            P(CHAN),
            P(),
            P(),
            P(CHAN, None),
            P(CHAN),
            P(CHAN, None),
            P(CHAN),
            P(),
        ),
        out_specs=(
            P(CHAN, LAT, None),
            P(CHAN, None),
            P(CHAN),
            P(CHAN),
            P(CHAN),
            P(CHAN, None),
            P(CHAN),
            P(CHAN, None),
            P(CHAN),
            P(CHAN),
        ),
        check_vma=False,
    )
```

```python
import functools

import jax
import jax.numpy as jnp
from jax import lax
from jax.experimental import pallas as pl
from jax.experimental.pallas import tpu as pltpu
from jax.sharding import Mesh, PartitionSpec as P

LAT = ("zh", "x", "c")
CHAN = ("zl", "y")
GROUP = 8
F32 = jnp.float32
BF = jnp.bfloat16
EXT = 16
VMEM_BYTES = 20 * 1024 * 1024
SIDE = 128


def vmem():
    return pl.BlockSpec(memory_space=pltpu.VMEM)


def smem():
    return pl.BlockSpec(memory_space=pltpu.SMEM)


def call(body, out_shape, in_specs, scratch=()):
    many = isinstance(out_shape, (list, tuple))
    return pl.pallas_call(
        body,
        out_shape=out_shape,
        in_specs=in_specs,
        out_specs=[vmem()] * len(out_shape) if many else vmem(),
        scratch_shapes=list(scratch),
        compiler_params=pltpu.CompilerParams(vmem_limit_bytes=VMEM_BYTES),
    )


def fill_rows(x_ref, up_ref, down_ref, ext):
    rows = x_ref.shape[1]
    ext[:, :3, :] = up_ref[...].astype(F32)
    ext[:, 3 : 3 + rows, :] = x_ref[...].astype(F32)
    ext[:, 3 + rows : 6 + rows, :] = down_ref[...].astype(F32)


def row_shifts(ext, c, rows):
    return [ext[c, a : a + rows, :] for a in range(7)]


def along(cells, move):
    width = cells.shape[1]
    if move == 0:
        return cells
    lane = lax.broadcasted_iota(jnp.int32, cells.shape, 1)
    inside = lane < width - move if move > 0 else lane >= -move
    return jnp.where(inside, pltpu.roll(cells, (-move) % width, 1), 0.0)


def stencil(taps_ref, c, shifts, flip):
    total = None
    for b in range(7):
        column = None
        for a in range(7):
            tap = a * 7 + b
            term = taps_ref[c, 48 - tap if flip else tap] * shifts[a]
            column = term if column is None else column + term
        column = along(column, b - 3)
        total = column if total is None else total + column
    return total


def forward_body(taps_ref, bias_ref, x_ref, up_ref, down_ref, metric_ref, dy_ref, out_ref, ext, h_rows, dy_rows):
    cdev, rows, width = x_ref.shape
    fill_rows(x_ref, up_ref, down_ref, ext)
    dy_rows[...] = dy_ref[...].astype(F32)
    metric = jnp.broadcast_to(metric_ref[...], (rows, width))

    def channel(c, carry):
        h_rows[c] = bias_ref[c] + metric * stencil(taps_ref, c, row_shifts(ext, c, rows), False)
        return carry

    lax.fori_loop(0, cdev, channel, 0, unroll=4)
    low = lax.broadcasted_iota(jnp.int32, (cdev, 128), 1) < 64
    for r in range(rows):
        h_row, dy_row = h_rows[:, r, :], dy_rows[:, r, :]
        for t in range(width // 128):
            h_tile, dy_tile = h_row[:, t * 128 : t * 128 + 128], dy_row[:, t * 128 : t * 128 + 128]
            at = (r * width + t * 128) // 64
            out_ref[at] = jnp.where(low, h_tile, pltpu.roll(dy_tile, 64, 1)).astype(BF)
            out_ref[at + 1] = jnp.where(low, pltpu.roll(h_tile, 64, 1), dy_tile).astype(BF)


def forward(taps, bias, x, up, down, metric, dy):
    cdev, rows, width = x.shape
    return call(
        forward_body,
        jax.ShapeDtypeStruct((rows * width // 64, cdev, 128), BF),
        [smem(), smem()] + [vmem()] * 5,
        [
            pltpu.VMEM((cdev, EXT, width), F32),
            pltpu.VMEM((cdev, rows, width), F32),
            pltpu.VMEM((cdev, rows, width), F32),
        ],
    )(taps, bias, x, up, down, metric[:, None], dy)


def norm_body(recv_ref, gain_ref, bias_ref, pair_ref, nhat_ref, rstd_ref):
    chans, lanes = recv_ref.shape
    piece = lanes // 2
    both = recv_ref[...].astype(F32).T
    h = both[:piece]
    mean = jnp.sum(h, 1, keepdims=True) / chans
    var = jnp.sum(h * h, 1, keepdims=True) / chans - mean * mean
    rstd = 1.0 / jnp.sqrt(var + 1e-06)
    nhat = (h - mean) * rstd
    nhat_ref[...] = nhat
    rstd_ref[...] = jnp.broadcast_to(rstd, rstd_ref.shape)
    n = (nhat * gain_ref[...] + bias_ref[...]).astype(BF)
    dy = both[piece:].astype(BF)
    for k in range(pair_ref.shape[0]):
        pair_ref[k, :piece] = n
        pair_ref[k, piece:] = dy


def norm(recv, gain, bias, copies):
    chans, lanes = recv.shape
    return call(
        norm_body,
        [
            jax.ShapeDtypeStruct((copies, lanes, chans), BF),
            jax.ShapeDtypeStruct((lanes // 2, chans), F32),
            jax.ShapeDtypeStruct((lanes // 2, 128), F32),
        ],
        [vmem()] * 3,
    )(recv, gain[None], bias[None])


def norm_back_body(recv_ref, nhat_ref, rstd_ref, gain_ref, gam_ref, db_ref, out_ref, flat):
    piece, chans = nhat_ref.shape
    dn = recv_ref[0].astype(F32)
    for k in range(1, recv_ref.shape[0]):
        dn = dn + recv_ref[k].astype(F32)
    nhat = nhat_ref[...]
    dnhat = dn * gain_ref[...]
    s1 = jnp.sum(dnhat, 1, keepdims=True) / chans
    s2 = jnp.sum(dnhat * nhat, 1, keepdims=True) / chans
    dh = rstd_ref[:, :1] * (dnhat - s1 - nhat * s2)
    flat[:piece] = dh
    flat[piece:] = jnp.zeros((flat.shape[0] - piece, chans), F32)
    sums = (jnp.sum(dn * nhat, 0, keepdims=True), jnp.sum(dn, 0, keepdims=True), gam_ref[...], db_ref[...])
    for k, value in enumerate(sums):
        high = value.astype(BF).astype(F32)
        flat[piece + 2 * k : piece + 2 * k + 1] = high
        flat[piece + 2 * k + 1 : piece + 2 * k + 2] = value - high
    blocks = flat[...].T.reshape(out_ref.shape[0], 24, 128)
    one, two, three = blocks[:, :8], blocks[:, 8:16], blocks[:, 16:]
    lane = lax.broadcasted_iota(jnp.int32, one.shape, 2)
    out_ref[:, :8] = jnp.where(lane < 64, one, pltpu.roll(three, 64, 2)).astype(BF)
    last = jnp.where(lane < 72, one, jnp.where(lane < 80, pltpu.roll(two, 8, 2), pltpu.roll(three, 16, 2)))
    out_ref[:, 8:] = jnp.where(lane < 64, two, last).astype(BF)


def norm_back(recv, nhat, rstd, gain, gam, db, owners):
    piece, chans = nhat.shape
    return call(
        norm_back_body,
        jax.ShapeDtypeStruct((owners, 16, 128), BF),
        [vmem()] * 6,
        [pltpu.VMEM((128, chans), F32)],
    )(recv, nhat, rstd, gain[None], gam, db)


def taps_body(recv_ref, x_ref, up_ref, down_ref, metric_ref, dy_ref, dconv_ref, ends_ref, sums_ref, extra_ref, ext, dh_rows, prods):
    cdev, rows, width = x_ref.shape
    fill_rows(x_ref, up_ref, down_ref, ext)
    low16 = lax.broadcasted_iota(jnp.int32, (16, 128), 1) < 64
    low8 = lax.broadcasted_iota(jnp.int32, (8, 128), 1) < 64
    extra = jnp.zeros((8, 128), F32)
    for r in range(rows):
        for t in range(width // 128):
            at = (r * width + t * 128) // 64
            first, second = recv_ref[at].astype(F32), recv_ref[at + 1].astype(F32)
            lanes = slice(t * 128, t * 128 + 128)
            dh_rows[:16, r, lanes] = jnp.where(low16, first, pltpu.roll(second, 64, 1))
            dh_rows[16:, r, lanes] = jnp.where(low8, pltpu.roll(first[:8], 64, 1), second[:8])
            extra = extra + first[8:] + second[8:]
    for g in range(3):
        extra_ref[8 * g : 8 * g + 8] = pltpu.roll(extra, 64 - 8 * g, 1)
    metric = jnp.broadcast_to(metric_ref[...], (rows, width))

    def channel(c, carry):
        dh = dh_rows[c]
        dconv = metric * dh
        dconv_ref[c] = dconv
        ends_ref[0, c] = dconv[:3].astype(BF)
        ends_ref[1, c] = dconv[rows - 3 :].astype(BF)
        shifts = row_shifts(ext, c, rows)
        for b in range(7):
            moved = along(dconv, 3 - b)
            for a in range(7):
                product = shifts[a] * moved
                prods[(a * 7 + b) * 8 : (a * 7 + b) * 8 + 8, :] = product[:, :128] + product[:, 128:]
        dy = dy_ref[c].astype(F32)
        prods[392:400, :] = dh[:, :128] + dh[:, 128:]
        prods[400:408, :] = dy[:, :128] + dy[:, 128:]
        total = prods[pl.ds(0, 56, 8), :]
        for i in range(1, 8):
            total = total + prods[pl.ds(i, 56, 8), :]
        sums_ref[c] = total
        return carry

    prods[408:, :] = jnp.zeros((prods.shape[0] - 408, 128), F32)
    lax.fori_loop(0, cdev, channel, 0, unroll=4)


def tap_sums(recv, x, up, down, metric, dy):
    cdev, rows, width = x.shape
    return call(
        taps_body,
        [
            jax.ShapeDtypeStruct((cdev, rows, width), F32),
            jax.ShapeDtypeStruct((2, cdev, 3, width), BF),
            jax.ShapeDtypeStruct((cdev, 56, 128), F32),
            jax.ShapeDtypeStruct((cdev, 128), F32),
        ],
        [vmem()] * 6,
        [
            pltpu.VMEM((cdev, EXT, width), F32),
            pltpu.VMEM((cdev, rows, width), F32),
            pltpu.VMEM((448, 128), F32),
        ],
    )(recv, x, up, down, metric[:, None], dy)


def spread_body(taps_ref, x_ref, up_ref, down_ref, dy_ref, out_ref, ext):
    cdev, rows, width = x_ref.shape
    fill_rows(x_ref, up_ref, down_ref, ext)

    def channel(c, carry):
        out_ref[c] = dy_ref[c].astype(F32) + stencil(taps_ref, c, row_shifts(ext, c, rows), True)
        return carry

    lax.fori_loop(0, cdev, channel, 0, unroll=4)


def spread_back(taps, dconv, up, down, dy):
    cdev, rows, width = dconv.shape
    return call(
        spread_body,
        jax.ShapeDtypeStruct((cdev, rows, width), F32),
        [smem()] + [vmem()] * 4,
        [pltpu.VMEM((cdev, EXT, width), F32)],
    )(taps, dconv, up, down, dy)


def picks(blocks, part):
    shape = (blocks * 2 * part, blocks * part)
    row = lax.broadcasted_iota(jnp.int32, shape, 0)
    place = lax.broadcasted_iota(jnp.int32, shape, 1)
    block = jnp.floor((row.astype(F32) + 0.5) * (0.5 / part)).astype(jnp.int32)
    inside = row - block * 2 * part
    first = (inside < part) & (place == block * part + inside)
    second = (inside >= part) & (place == block * part + inside - part)
    return [jnp.where(m, 1.0, 0.0).astype(BF) for m in (first, second)]


def dot(a, b, a_dim, b_dim):
    return lax.dot_general(a, b, (((a_dim,), (b_dim,)), ((), ())), preferred_element_type=F32)


def weights_body(part, own_ref, one_ref, low_ref, high_ref, last_ref, wi_ref, wo_ref, bi_ref, rows):
    blocks = 0
    for ref in (own_ref, one_ref, low_ref, high_ref, last_ref):
        for k in range(ref.shape[0]):
            at = blocks * 2 * part
            rows[at : at + 2 * part] = ref[k].astype(F32)
            blocks += 1
    chans = wi_ref.shape[1]
    flat = rows[...].astype(BF)
    first, second = picks(blocks, part)
    wi_ref[...] = dot(first, flat[:, :chans], 0, 0).astype(BF)
    wo_ref[...] = dot(second, flat[:, :chans], 0, 0).astype(BF)
    both = dot(flat[:, chans:], first, 0, 0)
    bi_ref[...] = both[:1] + both[1:2]


def weights(parts, part, chans):
    blocks = sum(p.shape[0] for p in parts)
    return call(
        functools.partial(weights_body, part),
        [
            jax.ShapeDtypeStruct((blocks * part, chans), BF),
            jax.ShapeDtypeStruct((blocks * part, chans), BF),
            jax.ShapeDtypeStruct((1, blocks * part), F32),
        ],
        [vmem()] * len(parts),
        [pltpu.VMEM((blocks * 2 * part, parts[0].shape[2]), F32)],
    )(*parts)


def mlp_body(core_ref, own_ref, other_ref, wi_ref, wo_ref, bi_ref, gamma_ref, dn_ref, n_ref, dy_ref, g_ref, dpre_ref):
    members, lanes, _ = own_ref.shape
    piece = lanes // 2
    for at, ref in ((0, own_ref), (members, other_ref)):
        for k in range(members):
            n_ref[(at + k) * piece : (at + k + 1) * piece] = ref[k, :piece]
            dy_ref[(at + k) * piece : (at + k + 1) * piece] = ref[k, piece:]
    pre = dot(n_ref[...], wi_ref[...], 1, 1) + bi_ref[...]
    cdf = 0.5 + 0.5 * lax.erf(pre * (0.5**0.5))
    g_ref[...] = (pre * cdf).astype(BF)
    slope = cdf + pre * (jnp.exp(-0.5 * pre * pre) * (0.5 / 3.141592653589793) ** 0.5)
    dmlp = (gamma_ref[...] * dy_ref[...].astype(F32)).astype(BF)
    dpre = (slope * dot(dmlp, wo_ref[...], 1, 1)).astype(BF)
    dpre_ref[...] = dpre
    dn = dot(dpre, wi_ref[...], 1, 0).astype(BF)
    core = core_ref[0]
    for k in range(members):
        dn_ref[core * members + k] = dn[k * piece : (k + 1) * piece]
        dn_ref[(1 - core) * members + k] = dn[(members + k) * piece : (members + k + 1) * piece]


def mlp(core, own, other, wi, wo, bi, gamma):
    members, lanes, chans = own.shape
    toks, hid = members * lanes, wi.shape[0]
    return call(
        mlp_body,
        [
            jax.ShapeDtypeStruct((2 * members, lanes // 2, chans), BF),
            jax.ShapeDtypeStruct((toks, chans), BF),
            jax.ShapeDtypeStruct((toks, chans), BF),
            jax.ShapeDtypeStruct((toks, hid), BF),
            jax.ShapeDtypeStruct((toks, hid), BF),
        ],
        [smem()] + [vmem()] * 6,
    )(core, own, other, wi, wo, bi, gamma[None])


def grads_body(part, ny, y_ref, n_ref, dy_ref, g_ref, dpre_ref, wo_ref, gamma_ref, out_ref, gam_ref, db_ref):
    toks = n_ref.shape[0]
    hid = g_ref.shape[1]
    first, second = picks(hid // part, part)
    dw_in = dot(dpre_ref[...], n_ref[...], 0, 0).astype(BF)
    proj = dot(g_ref[...], dy_ref[...], 0, 0)
    gam_ref[...] = jnp.sum(wo_ref[...].astype(F32) * proj, 0, keepdims=True)
    dw_out = (proj * gamma_ref[...]).astype(BF)
    out_ref[...] = (dot(first, dw_in, 1, 0) + dot(second, dw_out, 1, 0)).astype(BF)
    nz = hid // part // ny
    lane = lax.broadcasted_iota(jnp.int32, (db_ref.shape[1], hid), 0)
    place = lax.broadcasted_iota(jnp.int32, (1, hid), 1)
    block = jnp.floor((place.astype(F32) + 0.5) * (1.0 / part)).astype(jnp.int32)
    ring = jnp.floor((block.astype(F32) + 0.5) * (1.0 / nz)).astype(jnp.int32)
    ahead = ring + y_ref[0]
    owner = (block - ring * nz) * ny + jnp.where(ahead >= ny, ahead - ny, ahead)
    spot = jnp.where(lane == owner * 2 * part + place - block * part, 1.0, 0.0).astype(BF)
    db = dot(jnp.ones((16, toks), BF), dpre_ref[...], 1, 0).astype(BF)
    db_ref[...] = dot(db, spot, 1, 1)[:1]


def grads(part, ny, y, n, dy, g, dpre, wo, gamma):
    toks, chans = n.shape
    return call(
        functools.partial(grads_body, part, ny),
        [
            jax.ShapeDtypeStruct((2 * g.shape[1], chans), BF),
            jax.ShapeDtypeStruct((1, chans), F32),
            jax.ShapeDtypeStruct((1, 2 * g.shape[1]), F32),
        ],
        [smem()] + [vmem()] * 6,
    )(y, n, dy, g, dpre, wo, gamma[None])


def slices_body(part, member_ref, w_in_ref, w_out_ref, b_ref, out_ref):
    hdev, chans = w_in_ref.shape
    row = lax.broadcasted_iota(jnp.int32, (2 * part, hdev), 0)
    place = lax.broadcasted_iota(jnp.int32, (2 * part, hdev), 1)
    start = member_ref[0] * part
    first = jnp.where((row < part) & (place == start + row), 1.0, 0.0).astype(BF)
    second = jnp.where((row >= part) & (place == start + row - part), 1.0, 0.0).astype(BF)
    rows = (dot(first, w_in_ref[...], 1, 0) + dot(second, w_out_ref[...], 1, 0)).astype(BF)
    bias = jnp.broadcast_to(b_ref[...], (SIDE, hdev))
    high = bias.astype(BF)
    low = (bias - high.astype(F32)).astype(BF)
    line = lax.broadcasted_iota(jnp.int32, (SIDE, hdev), 0)
    high = jnp.where(line == 0, high.astype(F32), jnp.where(line == 1, low.astype(F32), 0.0)).astype(BF)
    side = dot(first, high, 1, 1).astype(BF)
    for k in range(out_ref.shape[0]):
        out_ref[k, :, :chans] = rows
        out_ref[k, :, chans:] = side


def slices(part, copies, member, w_in, w_out, b_in):
    return call(
        functools.partial(slices_body, part),
        jax.ShapeDtypeStruct((copies, 2 * part, w_in.shape[1] + SIDE), BF),
        [smem()] + [vmem()] * 3,
    )(member, w_in, w_out, b_in[None])


def results_body(part, n_taps, gathered_ref, gamma_ref, b_out_ref, dw_in_ref, dw_out_ref, taps_ref, db_ref, rest_ref):
    chans = dw_in_ref.shape[1]
    total = None
    for k in range(gathered_ref.shape[0]):
        block = gathered_ref[k].astype(F32)
        dw_in_ref[k * part : (k + 1) * part] = block[:part, :chans]
        dw_out_ref[k * part : (k + 1) * part] = block[part:, :chans]
        side = block[:, chans:]
        side = side + pltpu.roll(side, 64, 1)
        line = side.T
        db_ref[k : k + 1] = (line[62:63] + line[63:64])[:, :part]
        total = side if total is None else total + side
    taps_ref[...] = total[:, :n_taps]
    lines = total.T
    dysum = lines[n_taps + 1 : n_taps + 2]
    rest_ref[0:1] = lines[n_taps : n_taps + 1]
    rest_ref[1:2] = lines[56:57] + lines[57:58]
    rest_ref[2:3] = lines[58:59] + lines[59:60]
    rest_ref[3:4] = gamma_ref[...] * dysum
    rest_ref[4:5] = lines[60:61] + lines[61:62] + b_out_ref[...] * dysum


def results(part, n_taps, gathered, chans, gamma, b_out):
    members, rows, _ = gathered.shape
    return call(
        functools.partial(results_body, part, n_taps),
        [
            jax.ShapeDtypeStruct((members * part, chans), F32),
            jax.ShapeDtypeStruct((members * part, chans), F32),
            jax.ShapeDtypeStruct((rows, n_taps), F32),
            jax.ShapeDtypeStruct((members, part), F32),
            jax.ShapeDtypeStruct((5, rows), F32),
        ],
        [vmem()] * 3,
    )(gathered, gamma[None], b_out[None])


def two_parts(value):
    high = lax.reduce_precision(value, 8, 7)
    return high.astype(BF), (value - high).astype(BF)


def to_all(block, axis):
    count = lax.axis_size(axis)
    return lax.all_to_all(jnp.broadcast_to(block[None], (count,) + block.shape), axis, 0, 0, tiled=True)


def exchange(blocks):
    return lax.all_to_all(blocks, CHAN, 0, 0, tiled=True)


def halos(first, last):
    count = lax.axis_size(LAT)
    place = lax.axis_index(LAT)
    even = place % 2 == 0
    pairs = [(i, i + 1) for i in range(0, count, 2)]
    within = lax.ppermute(jnp.where(even, last, first), LAT, pairs + [(j, i) for i, j in pairs])
    pairs = [(i, i + 1) for i in range(1, count - 1, 2)]
    across = lax.ppermute(jnp.where(even, first, last), LAT, pairs + [(j, i) for i, j in pairs])
    return jnp.where(even, across, within), jnp.where(even, within, across)


def along_ring(block, ahead):
    count = lax.axis_size("y")
    return lax.ppermute(block, "y", [((i + ahead) % count, i) for i in range(count)])


def to_ring(blocks):
    count = lax.axis_size("y")
    total = blocks[0].astype(F32)
    for k in range(1, count):
        total = total + lax.ppermute(blocks[k], "y", [(i, (i + k) % count) for i in range(count)]).astype(F32)
    return total


def per_device(
    block_input,
    out_grad,
    metric,
    kernel,
    conv_bias,
    ln_gain,
    ln_bias,
    w_in,
    b_in,
    w_out,
    b_out,
    layer_scale,
):
    cdev, rows, width = block_input.shape
    chans = ln_gain.shape[0]
    tokens = rows * width
    nz, ny = lax.axis_size("zl"), lax.axis_size("y")
    nchan = nz * ny
    hdev = w_in.shape[0]
    part = hdev // GROUP
    piece = tokens // nchan
    owner = lax.axis_index(CHAN)
    gamma_f = layer_scale.astype(F32)
    gamma_own = lax.dynamic_slice_in_dim(gamma_f, owner * cdev, cdev)

    member = lax.axis_index(("x", "c")).astype(jnp.int32)[None]
    shards = lax.all_to_all(slices(part, nz, member, w_in, w_out, b_in), "zl", 0, 0, tiled=True)

    up, down = halos(block_input[:, :3], block_input[:, rows - 3 :])
    blocks = forward(kernel, conv_bias, block_input, up, down, metric, out_grad)
    blocks, shards = lax.optimization_barrier((blocks, shards))

    recv = exchange(blocks)
    one, last = along_ring(shards, 1), along_ring(shards, -1)
    recv, one, last = lax.optimization_barrier((recv, one, last))

    pair, nhat, rstd = norm(recv.reshape(chans, 2 * piece), ln_gain, ln_bias, GROUP // 2)
    pair = lax.all_to_all(pair, "x", 0, 0, tiled=True)
    low, high = along_ring(one[: nz // 2], 1), along_ring(last[nz // 2 :], -1)
    pair, low, high = lax.optimization_barrier((pair, low, high))
    wi, wo, bi = weights([shards, one, low, high, last], part, chans)
    other = lax.ppermute(pair, "c", [(0, 1), (1, 0)])

    core = lax.axis_index("c").astype(jnp.int32)[None]
    dn, n, dy, g, dpre = mlp(core, pair, other, wi, wo, bi, gamma_f)
    dn = lax.all_to_all(dn, ("c", "x"), 0, 0, tiled=True)

    dws, gam_part, db_part = grads(part, ny, lax.axis_index("y").astype(jnp.int32)[None], n, dy, g, dpre, wo, gamma_f)
    dws = to_ring(dws.reshape(ny, nz, 2 * part, chans)).astype(BF)
    dws = lax.all_to_all(dws, "zl", 0, 0, tiled=True)
    dws = jnp.sum(dws.astype(F32), 0)

    payload = exchange(norm_back(dn, nhat, rstd, ln_gain, gam_part, db_part, nchan))
    dconv, ends, taps, extra = tap_sums(payload, block_input, up, down, metric, out_grad)
    dup, ddown = halos(ends[0], ends[1])

    small = jnp.concatenate([jnp.sum(taps, 2), extra[:, :8]], 1)
    mine = jnp.concatenate([dws.astype(BF)] + list(two_parts(small)), 1)
    other = lax.ppermute(mine, "zh", [(0, 1), (1, 0)]).astype(F32)
    count = small.shape[1]
    dws = dws + other[:, :chans]
    small = small + other[:, chans : chans + count] + other[:, chans + count :]
    mine = jnp.concatenate([dws.astype(BF)] + list(two_parts(small)), 1)
    mine, dup, ddown = lax.optimization_barrier((mine, dup, ddown))
    grad_input = spread_back(kernel, dconv, dup, ddown, out_grad)
    grad_w_in, grad_w_out, grad_kernel, db, rest = results(
        part, kernel.shape[1], to_all(mine, ("x", "c")), chans, gamma_own, b_out
    )
    return (
        grad_input,
        grad_kernel,
        rest[0],
        rest[1],
        rest[2],
        grad_w_in,
        db.reshape(hdev),
        grad_w_out,
        rest[3],
        rest[4],
    )


def solution(mesh):
    split = Mesh(mesh.devices.reshape(2, 4, 2, 8, 4), ("zh", "x", "c", "zl", "y"))
    return jax.shard_map(
        per_device,
        mesh=split,
        in_specs=(
            P(CHAN, LAT, None),
            P(CHAN, LAT, None),
            P(LAT),
            P(CHAN, None),
            P(CHAN),
            P(),
            P(),
            P(CHAN, None),
            P(CHAN),
            P(CHAN, None),
            P(CHAN),
            P(),
        ),
        out_specs=(
            P(CHAN, LAT, None),
            P(CHAN, None),
            P(CHAN),
            P(CHAN),
            P(CHAN),
            P(CHAN, None),
            P(CHAN),
            P(CHAN, None),
            P(CHAN),
            P(CHAN),
        ),
        check_vma=False,
    )
```

```python
import functools

import jax
import jax.numpy as jnp
from jax import lax
from jax.experimental import pallas as pl
from jax.experimental.pallas import tpu as pltpu
from jax.sharding import Mesh, PartitionSpec as P

LAT = ("zh", "x", "c")
ZLO = ("zq", "zp")
CHAN = ("zq", "zp", "y")
GROUP = 8
F32 = jnp.float32
BF = jnp.bfloat16
EXT = 16
VMEM_BYTES = 20 * 1024 * 1024
SIDE = 128


def vmem():
    return pl.BlockSpec(memory_space=pltpu.VMEM)


def smem():
    return pl.BlockSpec(memory_space=pltpu.SMEM)


def call(body, out_shape, in_specs, scratch=()):
    many = isinstance(out_shape, (list, tuple))
    return pl.pallas_call(
        body,
        out_shape=out_shape,
        in_specs=in_specs,
        out_specs=[vmem()] * len(out_shape) if many else vmem(),
        scratch_shapes=list(scratch),
        compiler_params=pltpu.CompilerParams(vmem_limit_bytes=VMEM_BYTES),
    )


def fill_rows(x_ref, up_ref, down_ref, ext):
    rows = x_ref.shape[1]
    ext[:, :3, :] = up_ref[...].astype(F32)
    ext[:, 3 : 3 + rows, :] = x_ref[...].astype(F32)
    ext[:, 3 + rows : 6 + rows, :] = down_ref[...].astype(F32)


def row_shifts(ext, c, rows):
    return [ext[c, a : a + rows, :] for a in range(7)]


def along(cells, move):
    width = cells.shape[1]
    if move == 0:
        return cells
    lane = lax.broadcasted_iota(jnp.int32, cells.shape, 1)
    inside = lane < width - move if move > 0 else lane >= -move
    return jnp.where(inside, pltpu.roll(cells, (-move) % width, 1), 0.0)


def stencil(taps_ref, c, shifts, flip):
    total = None
    for b in range(7):
        column = None
        for a in range(7):
            tap = a * 7 + b
            term = taps_ref[c, 48 - tap if flip else tap] * shifts[a]
            column = term if column is None else column + term
        column = along(column, b - 3)
        total = column if total is None else total + column
    return total


def forward_body(taps_ref, bias_ref, x_ref, up_ref, down_ref, metric_ref, dy_ref, out_ref, ext, h_rows, dy_rows):
    cdev, rows, width = x_ref.shape
    fill_rows(x_ref, up_ref, down_ref, ext)
    dy_rows[...] = dy_ref[...].astype(F32)
    metric = jnp.broadcast_to(metric_ref[...], (rows, width))

    def channel(c, carry):
        h_rows[c] = bias_ref[c] + metric * stencil(taps_ref, c, row_shifts(ext, c, rows), False)
        return carry

    lax.fori_loop(0, cdev, channel, 0, unroll=8)
    low = lax.broadcasted_iota(jnp.int32, (cdev, 128), 1) < 64
    for r in range(rows):
        h_row, dy_row = h_rows[:, r, :], dy_rows[:, r, :]
        for t in range(width // 128):
            h_tile, dy_tile = h_row[:, t * 128 : t * 128 + 128], dy_row[:, t * 128 : t * 128 + 128]
            at = (r * width + t * 128) // 64
            out_ref[at] = jnp.where(low, h_tile, pltpu.roll(dy_tile, 64, 1)).astype(BF)
            out_ref[at + 1] = jnp.where(low, pltpu.roll(h_tile, 64, 1), dy_tile).astype(BF)


def forward(taps, bias, x, up, down, metric, dy):
    cdev, rows, width = x.shape
    return call(
        forward_body,
        jax.ShapeDtypeStruct((rows * width // 64, cdev, 128), BF),
        [smem(), smem()] + [vmem()] * 5,
        [
            pltpu.VMEM((cdev, EXT, width), F32),
            pltpu.VMEM((cdev, rows, width), F32),
            pltpu.VMEM((cdev, rows, width), F32),
        ],
    )(taps, bias, x, up, down, metric[:, None], dy)


def norm_body(recv_ref, gain_ref, bias_ref, pair_ref, nhat_ref, rstd_ref):
    chans, lanes = recv_ref.shape
    piece = lanes // 2
    both = recv_ref[...].astype(F32).T
    h = both[:piece]
    mean = jnp.sum(h, 1, keepdims=True) / chans
    var = jnp.sum(h * h, 1, keepdims=True) / chans - mean * mean
    rstd = 1.0 / jnp.sqrt(var + 1e-06)
    nhat = (h - mean) * rstd
    nhat_ref[...] = nhat
    rstd_ref[...] = jnp.broadcast_to(rstd, rstd_ref.shape)
    n = (nhat * gain_ref[...] + bias_ref[...]).astype(BF)
    dy = both[piece:].astype(BF)
    for k in range(pair_ref.shape[0]):
        pair_ref[k, :piece] = n
        pair_ref[k, piece:] = dy


def norm(recv, gain, bias, copies):
    chans, lanes = recv.shape
    return call(
        norm_body,
        [
            jax.ShapeDtypeStruct((copies, lanes, chans), BF),
            jax.ShapeDtypeStruct((lanes // 2, chans), F32),
            jax.ShapeDtypeStruct((lanes // 2, 128), F32),
        ],
        [vmem()] * 3,
    )(recv, gain[None], bias[None])


def norm_back_body(recv_ref, nhat_ref, rstd_ref, gain_ref, gam_ref, db_ref, out_ref, flat):
    piece, chans = nhat_ref.shape
    dn = recv_ref[0].astype(F32)
    for k in range(1, recv_ref.shape[0]):
        dn = dn + recv_ref[k].astype(F32)
    nhat = nhat_ref[...]
    dnhat = dn * gain_ref[...]
    s1 = jnp.sum(dnhat, 1, keepdims=True) / chans
    s2 = jnp.sum(dnhat * nhat, 1, keepdims=True) / chans
    dh = rstd_ref[:, :1] * (dnhat - s1 - nhat * s2)
    flat[:piece] = dh
    flat[piece:] = jnp.zeros((flat.shape[0] - piece, chans), F32)
    sums = (jnp.sum(dn * nhat, 0, keepdims=True), jnp.sum(dn, 0, keepdims=True), gam_ref[...], db_ref[...])
    for k, value in enumerate(sums):
        high = value.astype(BF).astype(F32)
        flat[piece + 2 * k : piece + 2 * k + 1] = high
        flat[piece + 2 * k + 1 : piece + 2 * k + 2] = value - high
    blocks = flat[...].T.reshape(out_ref.shape[0], 24, 128)
    one, two, three = blocks[:, :8], blocks[:, 8:16], blocks[:, 16:]
    lane = lax.broadcasted_iota(jnp.int32, one.shape, 2)
    out_ref[:, :8] = jnp.where(lane < 64, one, pltpu.roll(three, 64, 2)).astype(BF)
    last = jnp.where(lane < 72, one, jnp.where(lane < 80, pltpu.roll(two, 8, 2), pltpu.roll(three, 16, 2)))
    out_ref[:, 8:] = jnp.where(lane < 64, two, last).astype(BF)


def norm_back(recv, nhat, rstd, gain, gam, db, owners):
    piece, chans = nhat.shape
    return call(
        norm_back_body,
        jax.ShapeDtypeStruct((owners, 16, 128), BF),
        [vmem()] * 6,
        [pltpu.VMEM((128, chans), F32)],
    )(recv, nhat, rstd, gain[None], gam, db)


def taps_body(recv_ref, x_ref, up_ref, down_ref, metric_ref, dy_ref, dconv_ref, ends_ref, sums_ref, extra_ref, ext, dh_rows, prods):
    cdev, rows, width = x_ref.shape
    fill_rows(x_ref, up_ref, down_ref, ext)
    low16 = lax.broadcasted_iota(jnp.int32, (16, 128), 1) < 64
    low8 = lax.broadcasted_iota(jnp.int32, (8, 128), 1) < 64
    extra = jnp.zeros((8, 128), F32)
    for r in range(rows):
        for t in range(width // 128):
            at = (r * width + t * 128) // 64
            first, second = recv_ref[at].astype(F32), recv_ref[at + 1].astype(F32)
            lanes = slice(t * 128, t * 128 + 128)
            dh_rows[:16, r, lanes] = jnp.where(low16, first, pltpu.roll(second, 64, 1))
            dh_rows[16:, r, lanes] = jnp.where(low8, pltpu.roll(first[:8], 64, 1), second[:8])
            extra = extra + first[8:] + second[8:]
    for g in range(3):
        extra_ref[8 * g : 8 * g + 8] = pltpu.roll(extra, 64 - 8 * g, 1)
    metric = jnp.broadcast_to(metric_ref[...], (rows, width))

    def channel(c, carry):
        dh = dh_rows[c]
        dconv = metric * dh
        dconv_ref[c] = dconv
        ends_ref[0, c] = dconv[:3].astype(BF)
        ends_ref[1, c] = dconv[rows - 3 :].astype(BF)
        shifts = row_shifts(ext, c, rows)
        for b in range(7):
            moved = along(dconv, 3 - b)
            for a in range(7):
                product = shifts[a] * moved
                prods[(a * 7 + b) * 8 : (a * 7 + b) * 8 + 8, :] = product[:, :128] + product[:, 128:]
        dy = dy_ref[c].astype(F32)
        prods[392:400, :] = dh[:, :128] + dh[:, 128:]
        prods[400:408, :] = dy[:, :128] + dy[:, 128:]
        total = prods[pl.ds(0, 56, 8), :]
        for i in range(1, 8):
            total = total + prods[pl.ds(i, 56, 8), :]
        sums_ref[c] = total
        return carry

    prods[408:, :] = jnp.zeros((prods.shape[0] - 408, 128), F32)
    lax.fori_loop(0, cdev, channel, 0, unroll=8)


def tap_sums(recv, x, up, down, metric, dy):
    cdev, rows, width = x.shape
    return call(
        taps_body,
        [
            jax.ShapeDtypeStruct((cdev, rows, width), F32),
            jax.ShapeDtypeStruct((2, cdev, 3, width), BF),
            jax.ShapeDtypeStruct((cdev, 56, 128), F32),
            jax.ShapeDtypeStruct((cdev, 128), F32),
        ],
        [vmem()] * 6,
        [
            pltpu.VMEM((cdev, EXT, width), F32),
            pltpu.VMEM((cdev, rows, width), F32),
            pltpu.VMEM((448, 128), F32),
        ],
    )(recv, x, up, down, metric[:, None], dy)


def spread_body(taps_ref, x_ref, up_ref, down_ref, dy_ref, out_ref, ext):
    cdev, rows, width = x_ref.shape
    fill_rows(x_ref, up_ref, down_ref, ext)

    def channel(c, carry):
        out_ref[c] = dy_ref[c].astype(F32) + stencil(taps_ref, c, row_shifts(ext, c, rows), True)
        return carry

    lax.fori_loop(0, cdev, channel, 0, unroll=8)


def spread_back(taps, dconv, up, down, dy):
    cdev, rows, width = dconv.shape
    return call(
        spread_body,
        jax.ShapeDtypeStruct((cdev, rows, width), F32),
        [smem()] + [vmem()] * 4,
        [pltpu.VMEM((cdev, EXT, width), F32)],
    )(taps, dconv, up, down, dy)


def picks(blocks, part):
    shape = (blocks * 2 * part, blocks * part)
    row = lax.broadcasted_iota(jnp.int32, shape, 0)
    place = lax.broadcasted_iota(jnp.int32, shape, 1)
    block = jnp.floor((row.astype(F32) + 0.5) * (0.5 / part)).astype(jnp.int32)
    inside = row - block * 2 * part
    first = (inside < part) & (place == block * part + inside)
    second = (inside >= part) & (place == block * part + inside - part)
    return [jnp.where(m, 1.0, 0.0).astype(BF) for m in (first, second)]


def dot(a, b, a_dim, b_dim):
    return lax.dot_general(a, b, (((a_dim,), (b_dim,)), ((), ())), preferred_element_type=F32)


def weights_body(part, own_ref, one_ref, low_ref, high_ref, last_ref, wi_ref, wo_ref, bi_ref, rows):
    blocks = 0
    for ref in (own_ref, one_ref, low_ref, high_ref, last_ref):
        for k in range(ref.shape[0]):
            at = blocks * 2 * part
            rows[at : at + 2 * part] = ref[k].astype(F32)
            blocks += 1
    chans = wi_ref.shape[1]
    flat = rows[...].astype(BF)
    first, second = picks(blocks, part)
    wi_ref[...] = dot(first, flat[:, :chans], 0, 0).astype(BF)
    wo_ref[...] = dot(second, flat[:, :chans], 0, 0).astype(BF)
    both = dot(flat[:, chans:], first, 0, 0)
    bi_ref[...] = both[:1] + both[1:2]


def weights(parts, part, chans):
    blocks = sum(p.shape[0] for p in parts)
    return call(
        functools.partial(weights_body, part),
        [
            jax.ShapeDtypeStruct((blocks * part, chans), BF),
            jax.ShapeDtypeStruct((blocks * part, chans), BF),
            jax.ShapeDtypeStruct((1, blocks * part), F32),
        ],
        [vmem()] * len(parts),
        [pltpu.VMEM((blocks * 2 * part, parts[0].shape[2]), F32)],
    )(*parts)


def mlp_body(core_ref, own_ref, other_ref, wi_ref, wo_ref, bi_ref, gamma_ref, dn_ref, n_ref, dy_ref, acts_ref):
    members, lanes, _ = own_ref.shape
    piece = lanes // 2
    for at, ref in ((0, own_ref), (members, other_ref)):
        for k in range(members):
            n_ref[(at + k) * piece : (at + k + 1) * piece] = ref[k, :piece]
            dy_ref[(at + k) * piece : (at + k + 1) * piece] = ref[k, piece:]
    pre = dot(n_ref[...], wi_ref[...], 1, 1) + bi_ref[...]
    cdf = 0.5 + 0.5 * lax.erf(pre * (0.5**0.5))
    hid = pre.shape[1]
    acts_ref[:, :hid] = (pre * cdf).astype(BF)
    slope = cdf + pre * (jnp.exp(-0.5 * pre * pre) * (0.5 / 3.141592653589793) ** 0.5)
    dmlp = (gamma_ref[...] * dy_ref[...].astype(F32)).astype(BF)
    dpre = (slope * dot(dmlp, wo_ref[...], 1, 1)).astype(BF)
    acts_ref[:, hid:] = dpre
    dn = dot(dpre, wi_ref[...], 1, 0).astype(BF)
    core = core_ref[0]
    for k in range(members):
        dn_ref[core * members + k] = dn[k * piece : (k + 1) * piece]
        dn_ref[(1 - core) * members + k] = dn[(members + k) * piece : (members + k + 1) * piece]


def mlp(core, own, other, wi, wo, bi, gamma):
    members, lanes, chans = own.shape
    toks, hid = members * lanes, wi.shape[0]
    return call(
        mlp_body,
        [
            jax.ShapeDtypeStruct((2 * members, lanes // 2, chans), BF),
            jax.ShapeDtypeStruct((toks, chans), BF),
            jax.ShapeDtypeStruct((toks, chans), BF),
            jax.ShapeDtypeStruct((toks, 2 * hid), BF),
        ],
        [smem()] + [vmem()] * 6,
    )(core, own, other, wi, wo, bi, gamma[None])


def grads_body(part, ny, y_ref, n_ref, dy_ref, acts_ref, wo_ref, gamma_ref, out_ref, gam_ref, db_ref):
    toks = n_ref.shape[0]
    hid = acts_ref.shape[1] // 2
    first, second = picks(hid // part, part)
    dpre = acts_ref[:, hid:]
    dw_in = dot(dpre, n_ref[...], 0, 0).astype(BF)
    proj = dot(acts_ref[:, :hid], dy_ref[...], 0, 0)
    gam_ref[...] = jnp.sum(wo_ref[...].astype(F32) * proj, 0, keepdims=True)
    dw_out = (proj * gamma_ref[...]).astype(BF)
    out_ref[...] = (dot(first, dw_in, 1, 0) + dot(second, dw_out, 1, 0)).astype(BF)
    nz = hid // part // ny
    lane = lax.broadcasted_iota(jnp.int32, (db_ref.shape[1], hid), 0)
    place = lax.broadcasted_iota(jnp.int32, (1, hid), 1)
    block = jnp.floor((place.astype(F32) + 0.5) * (1.0 / part)).astype(jnp.int32)
    ring = jnp.floor((block.astype(F32) + 0.5) * (1.0 / nz)).astype(jnp.int32)
    ahead = ring + y_ref[0]
    owner = (block - ring * nz) * ny + jnp.where(ahead >= ny, ahead - ny, ahead)
    spot = jnp.where(lane == owner * 2 * part + place - block * part, 1.0, 0.0).astype(BF)
    db = dot(jnp.ones((16, toks), BF), dpre, 1, 0).astype(BF)
    db_ref[...] = dot(db, spot, 1, 1)[:1]


def grads(part, ny, y, n, dy, acts, wo, gamma):
    chans = n.shape[1]
    hid = acts.shape[1] // 2
    return call(
        functools.partial(grads_body, part, ny),
        [
            jax.ShapeDtypeStruct((2 * hid, chans), BF),
            jax.ShapeDtypeStruct((1, chans), F32),
            jax.ShapeDtypeStruct((1, 2 * hid), F32),
        ],
        [smem()] + [vmem()] * 5,
    )(y, n, dy, acts, wo, gamma[None])


def slices_body(part, member_ref, w_in_hbm, w_out_hbm, b_hbm, out_ref, w_in_ref, w_out_ref, b_ref, sems):
    pairs = ((w_in_hbm, w_in_ref), (w_out_hbm, w_out_ref), (b_hbm, b_ref))
    copies = [pltpu.make_async_copy(src, dst, sems.at[i]) for i, (src, dst) in enumerate(pairs)]
    for copy in copies:
        copy.start()
    for copy in copies:
        copy.wait()
    hdev, chans = w_in_ref.shape
    row = lax.broadcasted_iota(jnp.int32, (2 * part, hdev), 0)
    place = lax.broadcasted_iota(jnp.int32, (2 * part, hdev), 1)
    start = member_ref[0] * part
    first = jnp.where((row < part) & (place == start + row), 1.0, 0.0).astype(BF)
    second = jnp.where((row >= part) & (place == start + row - part), 1.0, 0.0).astype(BF)
    rows = (dot(first, w_in_ref[...], 1, 0) + dot(second, w_out_ref[...], 1, 0)).astype(BF)
    bias = jnp.broadcast_to(b_ref[...], (SIDE, hdev))
    high = bias.astype(BF)
    low = (bias - high.astype(F32)).astype(BF)
    line = lax.broadcasted_iota(jnp.int32, (SIDE, hdev), 0)
    high = jnp.where(line == 0, high.astype(F32), jnp.where(line == 1, low.astype(F32), 0.0)).astype(BF)
    side = dot(first, high, 1, 1).astype(BF)
    for k in range(out_ref.shape[0]):
        out_ref[k, :, :chans] = rows
        out_ref[k, :, chans:] = side


def slices(part, copies, member, w_in, w_out, b_in):
    return call(
        functools.partial(slices_body, part),
        jax.ShapeDtypeStruct((copies, 2 * part, w_in.shape[1] + SIDE), BF),
        [smem()] + [pl.BlockSpec(memory_space=pl.ANY)] * 3,
        [
            pltpu.VMEM(w_in.shape, BF),
            pltpu.VMEM(w_out.shape, BF),
            pltpu.VMEM((1,) + b_in.shape, F32),
            pltpu.SemaphoreType.DMA((3,)),
        ],
    )(member, w_in, w_out, b_in[None])


def results_body(part, n_taps, gathered_ref, gamma_ref, b_out_ref, dw_in_ref, dw_out_ref, taps_ref, db_ref, rest_ref):
    chans = dw_in_ref.shape[1]
    total = None
    for k in range(gathered_ref.shape[0]):
        block = gathered_ref[k].astype(F32)
        dw_in_ref[k * part : (k + 1) * part] = block[:part, :chans]
        dw_out_ref[k * part : (k + 1) * part] = block[part:, :chans]
        side = block[:, chans:]
        side = side + pltpu.roll(side, 64, 1)
        line = side.T
        db_ref[k : k + 1] = (line[62:63] + line[63:64])[:, :part]
        total = side if total is None else total + side
    taps_ref[...] = total[:, :n_taps]
    lines = total.T
    dysum = lines[n_taps + 1 : n_taps + 2]
    rest_ref[0:1] = lines[n_taps : n_taps + 1]
    rest_ref[1:2] = lines[56:57] + lines[57:58]
    rest_ref[2:3] = lines[58:59] + lines[59:60]
    rest_ref[3:4] = gamma_ref[...] * dysum
    rest_ref[4:5] = lines[60:61] + lines[61:62] + b_out_ref[...] * dysum


def results(part, n_taps, gathered, chans, gamma, b_out):
    members, rows, _ = gathered.shape
    return call(
        functools.partial(results_body, part, n_taps),
        [
            jax.ShapeDtypeStruct((members * part, chans), F32),
            jax.ShapeDtypeStruct((members * part, chans), F32),
            jax.ShapeDtypeStruct((rows, n_taps), F32),
            jax.ShapeDtypeStruct((members, part), F32),
            jax.ShapeDtypeStruct((5, rows), F32),
        ],
        [vmem()] * 3,
    )(gathered, gamma[None], b_out[None])


def to_neighbour(blocks):
    sides = blocks.reshape((blocks.shape[0] // 2, 2) + blocks.shape[1:])
    mine = lax.axis_index("zp")
    kept = lax.dynamic_index_in_dim(sides, mine, 1, keepdims=False)
    sent = lax.dynamic_index_in_dim(sides, 1 - mine, 1, keepdims=False).astype(BF)
    return kept + lax.ppermute(sent, "zp", [(0, 1), (1, 0)]).astype(F32)


def two_parts(value):
    high = lax.reduce_precision(value, 8, 7)
    return high.astype(BF), (value - high).astype(BF)


def to_all(block, axis):
    count = lax.axis_size(axis)
    return lax.all_to_all(jnp.broadcast_to(block[None], (count,) + block.shape), axis, 0, 0, tiled=True)


def exchange(blocks):
    return lax.all_to_all(blocks, CHAN, 0, 0, tiled=True)


def halos(first, last):
    count = lax.axis_size(LAT)
    place = lax.axis_index(LAT)
    even = place % 2 == 0
    pairs = [(i, i + 1) for i in range(0, count, 2)]
    within = lax.ppermute(jnp.where(even, last, first), LAT, pairs + [(j, i) for i, j in pairs])
    pairs = [(i, i + 1) for i in range(1, count - 1, 2)]
    across = lax.ppermute(jnp.where(even, first, last), LAT, pairs + [(j, i) for i, j in pairs])
    return jnp.where(even, across, within), jnp.where(even, within, across)


def along_ring(block, ahead):
    count = lax.axis_size("y")
    return lax.ppermute(block, "y", [((i + ahead) % count, i) for i in range(count)])


def to_ring(blocks):
    count = lax.axis_size("y")
    total = blocks[0].astype(F32)
    for k in range(1, count):
        total = total + lax.ppermute(blocks[k], "y", [(i, (i + k) % count) for i in range(count)]).astype(F32)
    return total


def per_device(
    block_input,
    out_grad,
    metric,
    kernel,
    conv_bias,
    ln_gain,
    ln_bias,
    w_in,
    b_in,
    w_out,
    b_out,
    layer_scale,
):
    cdev, rows, width = block_input.shape
    chans = ln_gain.shape[0]
    tokens = rows * width
    nz, ny = lax.axis_size(ZLO), lax.axis_size("y")
    nchan = nz * ny
    hdev = w_in.shape[0]
    part = hdev // GROUP
    piece = tokens // nchan
    owner = lax.axis_index(CHAN)
    gamma_f = layer_scale.astype(F32)
    gamma_own = lax.dynamic_slice_in_dim(gamma_f, owner * cdev, cdev)

    member = lax.axis_index(("x", "c")).astype(jnp.int32)[None]
    shards = lax.all_to_all(slices(part, nz, member, w_in, w_out, b_in), ZLO, 0, 0, tiled=True)

    up, down = halos(block_input[:, :3], block_input[:, rows - 3 :])
    blocks = forward(kernel, conv_bias, block_input, up, down, metric, out_grad)
    blocks, shards = lax.optimization_barrier((blocks, shards))

    recv = exchange(blocks)
    one, last = along_ring(shards, 1), along_ring(shards, -1)
    recv, one, last = lax.optimization_barrier((recv, one, last))

    pair, nhat, rstd = norm(recv.reshape(chans, 2 * piece), ln_gain, ln_bias, GROUP // 2)
    pair = lax.all_to_all(pair, "x", 0, 0, tiled=True)
    low, high = along_ring(one[: nz // 2], 1), along_ring(last[nz // 2 :], -1)
    pair, low, high = lax.optimization_barrier((pair, low, high))
    wi, wo, bi = weights([shards, one, low, high, last], part, chans)
    other = lax.ppermute(pair, "c", [(0, 1), (1, 0)])

    core = lax.axis_index("c").astype(jnp.int32)[None]
    dn, n, dy, acts = mlp(core, pair, other, wi, wo, bi, gamma_f)
    dn = lax.all_to_all(dn, ("c", "x"), 0, 0, tiled=True)

    dws, gam_part, db_part = grads(part, ny, lax.axis_index("y").astype(jnp.int32)[None], n, dy, acts, wo, gamma_f)
    dws = to_ring(dws.reshape(ny, nz, 2 * part, chans))
    dws = to_neighbour(dws).astype(BF)
    dws = lax.all_to_all(dws, "zq", 0, 0, tiled=True)
    dws = jnp.sum(dws.astype(F32), 0)

    payload = exchange(norm_back(dn, nhat, rstd, ln_gain, gam_part, db_part, nchan))
    dconv, ends, taps, extra = tap_sums(payload, block_input, up, down, metric, out_grad)
    dup, ddown = halos(ends[0], ends[1])

    small = jnp.concatenate([jnp.sum(taps, 2), extra[:, :8]], 1)
    mine = jnp.concatenate([dws.astype(BF)] + list(two_parts(small)), 1)
    other = lax.ppermute(mine, "zh", [(0, 1), (1, 0)]).astype(F32)
    count = small.shape[1]
    dws = dws + other[:, :chans]
    small = small + other[:, chans : chans + count] + other[:, chans + count :]
    mine = jnp.concatenate([dws.astype(BF)] + list(two_parts(small)), 1)
    mine, dup, ddown = lax.optimization_barrier((mine, dup, ddown))
    grad_input = spread_back(kernel, dconv, dup, ddown, out_grad)
    grad_w_in, grad_w_out, grad_kernel, db, rest = results(
        part, kernel.shape[1], to_all(mine, ("x", "c")), chans, gamma_own, b_out
    )
    return (
        grad_input,
        grad_kernel,
        rest[0],
        rest[1],
        rest[2],
        grad_w_in,
        db.reshape(hdev),
        grad_w_out,
        rest[3],
        rest[4],
    )


def solution(mesh):
    split = Mesh(mesh.devices.reshape(2, 4, 2, 4, 2, 4), ("zh", "x", "c", "zq", "zp", "y"))
    return jax.shard_map(
        per_device,
        mesh=split,
        in_specs=(
            P(CHAN, LAT, None),
            P(CHAN, LAT, None),
            P(LAT),
            P(CHAN, None),
            P(CHAN),
            P(),
            P(),
            P(CHAN, None),
            P(CHAN),
            P(CHAN, None),
            P(CHAN),
            P(),
        ),
        out_specs=(
            P(CHAN, LAT, None),
            P(CHAN, None),
            P(CHAN),
            P(CHAN),
            P(CHAN),
            P(CHAN, None),
            P(CHAN),
            P(CHAN, None),
            P(CHAN),
            P(CHAN),
        ),
        check_vma=False,
    )
```

```python
import functools

import jax
import jax.numpy as jnp
from jax import lax
from jax.experimental import pallas as pl
from jax.experimental.pallas import tpu as pltpu
from jax.sharding import Mesh, PartitionSpec as P

LAT = ("zh", "x", "c")
ZLO = ("zq", "zp")
CHAN = ("zq", "zp", "y")
GROUP = 8
F32 = jnp.float32
BF = jnp.bfloat16
EXT = 16
VMEM_BYTES = 20 * 1024 * 1024
SIDE = 128


def vmem():
    return pl.BlockSpec(memory_space=pltpu.VMEM)


def smem():
    return pl.BlockSpec(memory_space=pltpu.SMEM)


def call(body, out_shape, in_specs, scratch=()):
    many = isinstance(out_shape, (list, tuple))
    return pl.pallas_call(
        body,
        out_shape=out_shape,
        in_specs=in_specs,
        out_specs=[vmem()] * len(out_shape) if many else vmem(),
        scratch_shapes=list(scratch),
        compiler_params=pltpu.CompilerParams(vmem_limit_bytes=VMEM_BYTES),
    )


def fill_rows(x_ref, up_ref, down_ref, ext):
    rows = x_ref.shape[1]
    ext[:, :3, :] = up_ref[...].astype(F32)
    ext[:, 3 : 3 + rows, :] = x_ref[...].astype(F32)
    ext[:, 3 + rows : 6 + rows, :] = down_ref[...].astype(F32)


def row_shifts(ext, c, rows):
    return [ext[c, a : a + rows, :] for a in range(7)]


def along(cells, move):
    width = cells.shape[1]
    if move == 0:
        return cells
    lane = lax.broadcasted_iota(jnp.int32, cells.shape, 1)
    inside = lane < width - move if move > 0 else lane >= -move
    return jnp.where(inside, pltpu.roll(cells, (-move) % width, 1), 0.0)


def stencil(taps_ref, c, shifts, flip):
    total = None
    for b in range(7):
        column = None
        for a in range(7):
            tap = a * 7 + b
            term = taps_ref[c, 48 - tap if flip else tap] * shifts[a]
            column = term if column is None else column + term
        column = along(column, b - 3)
        total = column if total is None else total + column
    return total


def forward_body(taps_ref, bias_ref, x_ref, up_ref, down_ref, metric_ref, dy_ref, out_ref, ext, h_rows, dy_rows):
    cdev, rows, width = x_ref.shape
    fill_rows(x_ref, up_ref, down_ref, ext)
    dy_flat = dy_ref[...].astype(F32).reshape(cdev * rows, width)
    for t in range(width // 128):
        dy_rows[t] = dy_flat[:, t * 128 : t * 128 + 128]
    metric = jnp.broadcast_to(metric_ref[...], (rows, width))

    def channel(c, carry):
        h = bias_ref[c] + metric * stencil(taps_ref, c, row_shifts(ext, c, rows), False)
        for t in range(width // 128):
            h_rows[t, pl.ds(pl.multiple_of(c * rows, rows), rows), :] = h[:, t * 128 : t * 128 + 128]
        return carry

    lax.fori_loop(0, cdev, channel, 0, unroll=8)
    low = lax.broadcasted_iota(jnp.int32, (cdev, 128), 1) < 64
    for r in range(rows):
        for t in range(width // 128):
            h_tile, dy_tile = h_rows[t, pl.ds(r, cdev, rows), :], dy_rows[t, pl.ds(r, cdev, rows), :]
            at = (r * width + t * 128) // 64
            out_ref[at] = jnp.where(low, h_tile, pltpu.roll(dy_tile, 64, 1)).astype(BF)
            out_ref[at + 1] = jnp.where(low, pltpu.roll(h_tile, 64, 1), dy_tile).astype(BF)


def forward(taps, bias, x, up, down, metric, dy):
    cdev, rows, width = x.shape
    return call(
        forward_body,
        jax.ShapeDtypeStruct((rows * width // 64, cdev, 128), BF),
        [smem(), smem()] + [vmem()] * 5,
        [
            pltpu.VMEM((cdev, EXT, width), F32),
            pltpu.VMEM((width // 128, cdev * rows, 128), F32),
            pltpu.VMEM((width // 128, cdev * rows, 128), F32),
        ],
    )(taps, bias, x, up, down, metric[:, None], dy)


def norm_body(recv_ref, gain_ref, bias_ref, pair_ref, nhat_ref, rstd_ref):
    chans, lanes = recv_ref.shape
    piece = lanes // 2
    both = recv_ref[...].astype(F32).T
    h = both[:piece]
    mean = jnp.sum(h, 1, keepdims=True) / chans
    var = jnp.sum(h * h, 1, keepdims=True) / chans - mean * mean
    rstd = 1.0 / jnp.sqrt(var + 1e-06)
    nhat = (h - mean) * rstd
    nhat_ref[...] = nhat
    rstd_ref[...] = jnp.broadcast_to(rstd, rstd_ref.shape)
    n = (nhat * gain_ref[...] + bias_ref[...]).astype(BF)
    dy = both[piece:].astype(BF)
    for k in range(pair_ref.shape[0]):
        pair_ref[k, :piece] = n
        pair_ref[k, piece:] = dy


def norm(recv, gain, bias, copies):
    chans, lanes = recv.shape
    return call(
        norm_body,
        [
            jax.ShapeDtypeStruct((copies, lanes, chans), BF),
            jax.ShapeDtypeStruct((lanes // 2, chans), F32),
            jax.ShapeDtypeStruct((lanes // 2, 128), F32),
        ],
        [vmem()] * 3,
    )(recv, gain[None], bias[None])


def norm_back_body(recv_ref, nhat_ref, rstd_ref, gain_ref, gam_ref, db_ref, out_ref, flat):
    piece, chans = nhat_ref.shape
    dn = recv_ref[0].astype(F32)
    for k in range(1, recv_ref.shape[0]):
        dn = dn + recv_ref[k].astype(F32)
    nhat = nhat_ref[...]
    dnhat = dn * gain_ref[...]
    s1 = jnp.sum(dnhat, 1, keepdims=True) / chans
    s2 = jnp.sum(dnhat * nhat, 1, keepdims=True) / chans
    dh = rstd_ref[:, :1] * (dnhat - s1 - nhat * s2)
    flat[:piece] = dh
    flat[piece:] = jnp.zeros((flat.shape[0] - piece, chans), F32)
    sums = (jnp.sum(dn * nhat, 0, keepdims=True), jnp.sum(dn, 0, keepdims=True), gam_ref[...], db_ref[...])
    for k, value in enumerate(sums):
        high = value.astype(BF).astype(F32)
        flat[piece + 2 * k : piece + 2 * k + 1] = high
        flat[piece + 2 * k + 1 : piece + 2 * k + 2] = value - high
    blocks = flat[...].T.reshape(out_ref.shape[0], 24, 128)
    one, two, three = blocks[:, :8], blocks[:, 8:16], blocks[:, 16:]
    lane = lax.broadcasted_iota(jnp.int32, one.shape, 2)
    out_ref[:, :8] = jnp.where(lane < 64, one, pltpu.roll(three, 64, 2)).astype(BF)
    last = jnp.where(lane < 72, one, jnp.where(lane < 80, pltpu.roll(two, 8, 2), pltpu.roll(three, 16, 2)))
    out_ref[:, 8:] = jnp.where(lane < 64, two, last).astype(BF)


def norm_back(recv, nhat, rstd, gain, gam, db, owners):
    piece, chans = nhat.shape
    return call(
        norm_back_body,
        jax.ShapeDtypeStruct((owners, 16, 128), BF),
        [vmem()] * 6,
        [pltpu.VMEM((128, chans), F32)],
    )(recv, nhat, rstd, gain[None], gam, db)


def taps_body(recv_ref, x_ref, up_ref, down_ref, metric_ref, dy_ref, dconv_ref, ends_ref, sums_ref, extra_ref, ext, dh_rows, prods):
    cdev, rows, width = x_ref.shape
    fill_rows(x_ref, up_ref, down_ref, ext)
    low16 = lax.broadcasted_iota(jnp.int32, (16, 128), 1) < 64
    low8 = lax.broadcasted_iota(jnp.int32, (8, 128), 1) < 64
    extra = jnp.zeros((8, 128), F32)
    for r in range(rows):
        for t in range(width // 128):
            at = (r * width + t * 128) // 64
            first, second = recv_ref[at].astype(F32), recv_ref[at + 1].astype(F32)
            dh_rows[t, pl.ds(r, 16, rows), :] = jnp.where(low16, first, pltpu.roll(second, 64, 1))
            dh_rows[t, pl.ds(16 * rows + r, 8, rows), :] = jnp.where(low8, pltpu.roll(first[:8], 64, 1), second[:8])
            extra = extra + first[8:] + second[8:]
    for g in range(3):
        extra_ref[8 * g : 8 * g + 8] = pltpu.roll(extra, 64 - 8 * g, 1)
    metric = jnp.broadcast_to(metric_ref[...], (rows, width))

    def channel(c, carry):
        here = pl.ds(pl.multiple_of(c * rows, rows), rows)
        dh = jnp.concatenate([dh_rows[t, here, :] for t in range(width // 128)], 1)
        dconv = metric * dh
        dconv_ref[c] = dconv
        ends_ref[0, c] = dconv[:3].astype(BF)
        ends_ref[1, c] = dconv[rows - 3 :].astype(BF)
        shifts = row_shifts(ext, c, rows)
        for b in range(7):
            moved = along(dconv, 3 - b)
            for a in range(7):
                product = shifts[a] * moved
                prods[(a * 7 + b) * 8 : (a * 7 + b) * 8 + 8, :] = product[:, :128] + product[:, 128:]
        dy = dy_ref[c].astype(F32)
        prods[392:400, :] = dh[:, :128] + dh[:, 128:]
        prods[400:408, :] = dy[:, :128] + dy[:, 128:]
        total = prods[pl.ds(0, 56, 8), :]
        for i in range(1, 8):
            total = total + prods[pl.ds(i, 56, 8), :]
        sums_ref[c] = total
        return carry

    prods[408:, :] = jnp.zeros((prods.shape[0] - 408, 128), F32)
    lax.fori_loop(0, cdev, channel, 0, unroll=8)


def tap_sums(recv, x, up, down, metric, dy):
    cdev, rows, width = x.shape
    return call(
        taps_body,
        [
            jax.ShapeDtypeStruct((cdev, rows, width), F32),
            jax.ShapeDtypeStruct((2, cdev, 3, width), BF),
            jax.ShapeDtypeStruct((cdev, 56, 128), F32),
            jax.ShapeDtypeStruct((cdev, 128), F32),
        ],
        [vmem()] * 6,
        [
            pltpu.VMEM((cdev, EXT, width), F32),
            pltpu.VMEM((width // 128, cdev * rows, 128), F32),
            pltpu.VMEM((448, 128), F32),
        ],
    )(recv, x, up, down, metric[:, None], dy)


def spread_body(taps_ref, x_ref, up_ref, down_ref, dy_ref, out_ref, ext):
    cdev, rows, width = x_ref.shape
    fill_rows(x_ref, up_ref, down_ref, ext)

    def channel(c, carry):
        out_ref[c] = dy_ref[c].astype(F32) + stencil(taps_ref, c, row_shifts(ext, c, rows), True)
        return carry

    lax.fori_loop(0, cdev, channel, 0, unroll=8)


def spread_back(taps, dconv, up, down, dy):
    cdev, rows, width = dconv.shape
    return call(
        spread_body,
        jax.ShapeDtypeStruct((cdev, rows, width), F32),
        [smem()] + [vmem()] * 4,
        [pltpu.VMEM((cdev, EXT, width), F32)],
    )(taps, dconv, up, down, dy)


def picks(blocks, part):
    shape = (blocks * 2 * part, blocks * part)
    row = lax.broadcasted_iota(jnp.int32, shape, 0)
    place = lax.broadcasted_iota(jnp.int32, shape, 1)
    block = jnp.floor((row.astype(F32) + 0.5) * (0.5 / part)).astype(jnp.int32)
    inside = row - block * 2 * part
    first = (inside < part) & (place == block * part + inside)
    second = (inside >= part) & (place == block * part + inside - part)
    return [jnp.where(m, 1.0, 0.0).astype(BF) for m in (first, second)]


def dot(a, b, a_dim, b_dim):
    return lax.dot_general(a, b, (((a_dim,), (b_dim,)), ((), ())), preferred_element_type=F32)


def weights_body(part, own_ref, one_ref, low_ref, high_ref, last_ref, wi_ref, wo_ref, bi_ref, rows):
    blocks = 0
    for ref in (own_ref, one_ref, low_ref, high_ref, last_ref):
        for k in range(ref.shape[0]):
            at = blocks * 2 * part
            rows[at : at + 2 * part] = ref[k].astype(F32)
            blocks += 1
    chans = wi_ref.shape[1]
    flat = rows[...].astype(BF)
    first, second = picks(blocks, part)
    wi_ref[...] = dot(first, flat[:, :chans], 0, 0).astype(BF)
    wo_ref[...] = dot(second, flat[:, :chans], 0, 0).astype(BF)
    both = dot(flat[:, chans:], first, 0, 0)
    bi_ref[...] = both[:1] + both[1:2]


def weights(parts, part, chans):
    blocks = sum(p.shape[0] for p in parts)
    return call(
        functools.partial(weights_body, part),
        [
            jax.ShapeDtypeStruct((blocks * part, chans), BF),
            jax.ShapeDtypeStruct((blocks * part, chans), BF),
            jax.ShapeDtypeStruct((1, blocks * part), F32),
        ],
        [vmem()] * len(parts),
        [pltpu.VMEM((blocks * 2 * part, parts[0].shape[2]), F32)],
    )(*parts)


def mlp_body(core_ref, own_ref, other_ref, wi_ref, wo_ref, bi_ref, gamma_ref, dn_ref, n_ref, dy_ref, acts_ref):
    members, lanes, _ = own_ref.shape
    piece = lanes // 2
    for at, ref in ((0, own_ref), (members, other_ref)):
        for k in range(members):
            n_ref[(at + k) * piece : (at + k + 1) * piece] = ref[k, :piece]
            dy_ref[(at + k) * piece : (at + k + 1) * piece] = ref[k, piece:]
    pre = dot(n_ref[...], wi_ref[...], 1, 1) + bi_ref[...]
    cdf = 0.5 + 0.5 * lax.erf(pre * (0.5**0.5))
    hid = pre.shape[1]
    acts_ref[:, :hid] = (pre * cdf).astype(BF)
    slope = cdf + pre * (jnp.exp(-0.5 * pre * pre) * (0.5 / 3.141592653589793) ** 0.5)
    dmlp = (gamma_ref[...] * dy_ref[...].astype(F32)).astype(BF)
    dpre = (slope * dot(dmlp, wo_ref[...], 1, 1)).astype(BF)
    acts_ref[:, hid:] = dpre
    dn = dot(dpre, wi_ref[...], 1, 0).astype(BF)
    core = core_ref[0]
    for k in range(members):
        dn_ref[core * members + k] = dn[k * piece : (k + 1) * piece]
        dn_ref[(1 - core) * members + k] = dn[(members + k) * piece : (members + k + 1) * piece]


def mlp(core, own, other, wi, wo, bi, gamma):
    members, lanes, chans = own.shape
    toks, hid = members * lanes, wi.shape[0]
    return call(
        mlp_body,
        [
            jax.ShapeDtypeStruct((2 * members, lanes // 2, chans), BF),
            jax.ShapeDtypeStruct((toks, chans), BF),
            jax.ShapeDtypeStruct((toks, chans), BF),
            jax.ShapeDtypeStruct((toks, 2 * hid), BF),
        ],
        [smem()] + [vmem()] * 6,
    )(core, own, other, wi, wo, bi, gamma[None])


def grads_body(part, ny, place_ref, n_ref, dy_ref, acts_ref, wo_ref, gamma_ref, out_ref, gam_ref, db_ref):
    toks = n_ref.shape[0]
    hid = acts_ref.shape[1] // 2
    first, second = picks(hid // part, part)
    dpre = acts_ref[:, hid:]
    dw_in = dot(dpre, n_ref[...], 0, 0).astype(BF)
    proj = dot(acts_ref[:, :hid], dy_ref[...], 0, 0)
    gam_ref[...] = jnp.sum(wo_ref[...].astype(F32) * proj, 0, keepdims=True)
    dw_out = (proj * gamma_ref[...]).astype(BF)
    out_ref[...] = (dot(first, dw_in, 1, 0) + dot(second, dw_out, 1, 0)).astype(BF)
    nz = hid // part // ny
    lane = lax.broadcasted_iota(jnp.int32, (db_ref.shape[1], hid), 0)
    place = lax.broadcasted_iota(jnp.int32, (1, hid), 1)
    block = jnp.floor((place.astype(F32) + 0.5) * (1.0 / part)).astype(jnp.int32)
    ring = jnp.floor((block.astype(F32) + 0.5) * (1.0 / nz)).astype(jnp.int32)
    ahead = ring + place_ref[0]
    along_z = block - ring * nz
    far = along_z >= nz // 2
    zq = jnp.where(far, along_z - nz // 2, along_z)
    zp = jnp.where(far, 1 - place_ref[1], place_ref[1])
    owner = (zq * 2 + zp) * ny + jnp.where(ahead >= ny, ahead - ny, ahead)
    spot = jnp.where(lane == owner * 2 * part + place - block * part, 1.0, 0.0).astype(BF)
    db = dot(jnp.ones((16, toks), BF), dpre, 1, 0).astype(BF)
    db_ref[...] = dot(db, spot, 1, 1)[:1]


def grads(part, ny, place, n, dy, acts, wo, gamma):
    chans = n.shape[1]
    hid = acts.shape[1] // 2
    return call(
        functools.partial(grads_body, part, ny),
        [
            jax.ShapeDtypeStruct((2 * hid, chans), BF),
            jax.ShapeDtypeStruct((1, chans), F32),
            jax.ShapeDtypeStruct((1, 2 * hid), F32),
        ],
        [smem()] + [vmem()] * 5,
    )(place, n, dy, acts, wo, gamma[None])


def slices_body(part, member_ref, w_in_ref, w_out_ref, b_ref, out_ref):
    hdev, chans = w_in_ref.shape
    row = lax.broadcasted_iota(jnp.int32, (2 * part, hdev), 0)
    place = lax.broadcasted_iota(jnp.int32, (2 * part, hdev), 1)
    start = member_ref[0] * part
    first = jnp.where((row < part) & (place == start + row), 1.0, 0.0).astype(BF)
    second = jnp.where((row >= part) & (place == start + row - part), 1.0, 0.0).astype(BF)
    rows = (dot(first, w_in_ref[...], 1, 0) + dot(second, w_out_ref[...], 1, 0)).astype(BF)
    bias = jnp.broadcast_to(b_ref[...], (SIDE, hdev))
    high = bias.astype(BF)
    low = (bias - high.astype(F32)).astype(BF)
    line = lax.broadcasted_iota(jnp.int32, (SIDE, hdev), 0)
    high = jnp.where(line == 0, high.astype(F32), jnp.where(line == 1, low.astype(F32), 0.0)).astype(BF)
    side = dot(first, high, 1, 1).astype(BF)
    for k in range(out_ref.shape[0]):
        out_ref[k, :, :chans] = rows
        out_ref[k, :, chans:] = side


def slices(part, copies, member, w_in, w_out, b_in):
    return call(
        functools.partial(slices_body, part),
        jax.ShapeDtypeStruct((copies, 2 * part, w_in.shape[1] + SIDE), BF),
        [smem()] + [vmem()] * 3,
    )(member, w_in, w_out, b_in[None])


def results_body(part, n_taps, gathered_ref, gamma_ref, b_out_ref, dw_in_ref, dw_out_ref, taps_ref, db_ref, rest_ref):
    chans = dw_in_ref.shape[1]
    total = None
    for k in range(gathered_ref.shape[0]):
        block = gathered_ref[k].astype(F32)
        dw_in_ref[k * part : (k + 1) * part] = block[:part, :chans]
        dw_out_ref[k * part : (k + 1) * part] = block[part:, :chans]
        side = block[:, chans:]
        side = side + pltpu.roll(side, 64, 1)
        line = side.T
        db_ref[k : k + 1] = (line[62:63] + line[63:64])[:, :part]
        total = side if total is None else total + side
    taps_ref[...] = total[:, :n_taps]
    lines = total.T
    dysum = lines[n_taps + 1 : n_taps + 2]
    rest_ref[0:1] = lines[n_taps : n_taps + 1]
    rest_ref[1:2] = lines[56:57] + lines[57:58]
    rest_ref[2:3] = lines[58:59] + lines[59:60]
    rest_ref[3:4] = gamma_ref[...] * dysum
    rest_ref[4:5] = lines[60:61] + lines[61:62] + b_out_ref[...] * dysum


def results(part, n_taps, gathered, chans, gamma, b_out):
    members, rows, _ = gathered.shape
    return call(
        functools.partial(results_body, part, n_taps),
        [
            jax.ShapeDtypeStruct((members * part, chans), F32),
            jax.ShapeDtypeStruct((members * part, chans), F32),
            jax.ShapeDtypeStruct((rows, n_taps), F32),
            jax.ShapeDtypeStruct((members, part), F32),
            jax.ShapeDtypeStruct((5, rows), F32),
        ],
        [vmem()] * 3,
    )(gathered, gamma[None], b_out[None])


def to_neighbour(blocks):
    half = blocks.shape[0] // 2
    return blocks[:half] + lax.ppermute(blocks[half:].astype(BF), "zp", [(0, 1), (1, 0)]).astype(F32)


def two_parts(value):
    high = lax.reduce_precision(value, 8, 7)
    return high.astype(BF), (value - high).astype(BF)


def to_all(block, axis):
    count = lax.axis_size(axis)
    return lax.all_to_all(jnp.broadcast_to(block[None], (count,) + block.shape), axis, 0, 0, tiled=True)


def exchange(blocks):
    return lax.all_to_all(blocks, CHAN, 0, 0, tiled=True)


def halos(first, last):
    count = lax.axis_size(LAT)
    place = lax.axis_index(LAT)
    even = place % 2 == 0
    pairs = [(i, i + 1) for i in range(0, count, 2)]
    within = lax.ppermute(jnp.where(even, last, first), LAT, pairs + [(j, i) for i, j in pairs])
    pairs = [(i, i + 1) for i in range(1, count - 1, 2)]
    across = lax.ppermute(jnp.where(even, first, last), LAT, pairs + [(j, i) for i, j in pairs])
    return jnp.where(even, across, within), jnp.where(even, within, across)


def along_ring(block, ahead):
    count = lax.axis_size("y")
    return lax.ppermute(block, "y", [((i + ahead) % count, i) for i in range(count)])


def to_ring(blocks):
    count = lax.axis_size("y")
    total = blocks[0].astype(F32)
    for k in range(1, count):
        total = total + lax.ppermute(blocks[k], "y", [(i, (i + k) % count) for i in range(count)]).astype(F32)
    return total


def per_device(
    block_input,
    out_grad,
    metric,
    kernel,
    conv_bias,
    ln_gain,
    ln_bias,
    w_in,
    b_in,
    w_out,
    b_out,
    layer_scale,
):
    cdev, rows, width = block_input.shape
    chans = ln_gain.shape[0]
    tokens = rows * width
    nz, ny = lax.axis_size(ZLO), lax.axis_size("y")
    nchan = nz * ny
    hdev = w_in.shape[0]
    part = hdev // GROUP
    piece = tokens // nchan
    owner = lax.axis_index(CHAN)
    gamma_f = layer_scale.astype(F32)
    gamma_own = lax.dynamic_slice_in_dim(gamma_f, owner * cdev, cdev)

    member = lax.axis_index(("x", "c")).astype(jnp.int32)[None]
    shards = lax.all_to_all(slices(part, nz // 2, member, w_in, w_out, b_in), "zq", 0, 0, tiled=True)
    beside = lax.ppermute(shards, "zp", [(0, 1), (1, 0)])

    up, down = halos(block_input[:, :3], block_input[:, rows - 3 :])
    blocks = forward(kernel, conv_bias, block_input, up, down, metric, out_grad)
    blocks, shards, beside = lax.optimization_barrier((blocks, shards, beside))

    recv = exchange(blocks)
    shards = jnp.concatenate([shards, beside], 0)
    one, last = along_ring(shards, 1), along_ring(shards, -1)
    recv, one, last = lax.optimization_barrier((recv, one, last))

    pair, nhat, rstd = norm(recv.reshape(chans, 2 * piece), ln_gain, ln_bias, GROUP // 2)
    pair = lax.all_to_all(pair, "x", 0, 0, tiled=True)
    low, high = along_ring(one[: nz // 2], 1), along_ring(last[nz // 2 :], -1)
    pair, low, high = lax.optimization_barrier((pair, low, high))
    wi, wo, bi = weights([shards, one, low, high, last], part, chans)
    other = lax.ppermute(pair, "c", [(0, 1), (1, 0)])

    core = lax.axis_index("c").astype(jnp.int32)[None]
    dn, n, dy, acts = mlp(core, pair, other, wi, wo, bi, gamma_f)
    dn = lax.all_to_all(dn, ("c", "x"), 0, 0, tiled=True)

    place = jnp.stack([lax.axis_index("y"), lax.axis_index("zp")]).astype(jnp.int32)
    dws, gam_part, db_part = grads(part, ny, place, n, dy, acts, wo, gamma_f)
    dws = to_ring(dws.reshape(ny, nz, 2 * part, chans))
    dws = to_neighbour(dws).astype(BF)

    payload = exchange(norm_back(dn, nhat, rstd, ln_gain, gam_part, db_part, nchan))
    payload, dws = lax.optimization_barrier((payload, dws))
    dws = lax.all_to_all(dws, "zq", 0, 0, tiled=True)
    dws = jnp.sum(dws.astype(F32), 0)
    dconv, ends, taps, extra = tap_sums(payload, block_input, up, down, metric, out_grad)
    dup, ddown = halos(ends[0], ends[1])

    small = jnp.concatenate([jnp.sum(taps, 2), extra[:, :8]], 1)
    mine = jnp.concatenate([dws.astype(BF)] + list(two_parts(small)), 1)
    other = lax.ppermute(mine, "zh", [(0, 1), (1, 0)]).astype(F32)
    count = small.shape[1]
    dws = dws + other[:, :chans]
    small = small + other[:, chans : chans + count] + other[:, chans + count :]
    mine = jnp.concatenate([dws.astype(BF)] + list(two_parts(small)), 1)
    mine, dup, ddown = lax.optimization_barrier((mine, dup, ddown))
    grad_input = spread_back(kernel, dconv, dup, ddown, out_grad)
    grad_w_in, grad_w_out, grad_kernel, db, rest = results(
        part, kernel.shape[1], to_all(mine, ("x", "c")), chans, gamma_own, b_out
    )
    return (
        grad_input,
        grad_kernel,
        rest[0],
        rest[1],
        rest[2],
        grad_w_in,
        db.reshape(hdev),
        grad_w_out,
        rest[3],
        rest[4],
    )


def solution(mesh):
    split = Mesh(mesh.devices.reshape(2, 4, 2, 4, 2, 4), ("zh", "x", "c", "zq", "zp", "y"))
    return jax.shard_map(
        per_device,
        mesh=split,
        in_specs=(
            P(CHAN, LAT, None),
            P(CHAN, LAT, None),
            P(LAT),
            P(CHAN, None),
            P(CHAN),
            P(),
            P(),
            P(CHAN, None),
            P(CHAN),
            P(CHAN, None),
            P(CHAN),
            P(),
        ),
        out_specs=(
            P(CHAN, LAT, None),
            P(CHAN, None),
            P(CHAN),
            P(CHAN),
            P(CHAN),
            P(CHAN, None),
            P(CHAN),
            P(CHAN, None),
            P(CHAN),
            P(CHAN),
        ),
        check_vma=False,
    )
```

```python
import functools

import jax
import jax.numpy as jnp
from jax import lax
from jax.experimental import pallas as pl
from jax.experimental.pallas import tpu as pltpu
from jax.sharding import Mesh, PartitionSpec as P

LAT = ("zh", "x", "c")
ZLO = ("zq", "zp")
CHAN = ("zq", "zp", "y")
GROUP = 8
F32 = jnp.float32
BF = jnp.bfloat16
EXT = 16
VMEM_BYTES = 20 * 1024 * 1024
SIDE = 128


def vmem():
    return pl.BlockSpec(memory_space=pltpu.VMEM)


def smem():
    return pl.BlockSpec(memory_space=pltpu.SMEM)


def call(body, out_shape, in_specs, scratch=()):
    many = isinstance(out_shape, (list, tuple))
    return pl.pallas_call(
        body,
        out_shape=out_shape,
        in_specs=in_specs,
        out_specs=[vmem()] * len(out_shape) if many else vmem(),
        scratch_shapes=list(scratch),
        compiler_params=pltpu.CompilerParams(vmem_limit_bytes=VMEM_BYTES),
    )


def fill_rows(x_ref, up_ref, down_ref, ext):
    rows = x_ref.shape[1]
    ext[:, :3, :] = up_ref[...].astype(F32)
    ext[:, 3 : 3 + rows, :] = x_ref[...].astype(F32)
    ext[:, 3 + rows : 6 + rows, :] = down_ref[...].astype(F32)


def row_shifts(ext, c, rows):
    return [ext[c, a : a + rows, :] for a in range(7)]


def along(cells, move):
    width = cells.shape[1]
    if move == 0:
        return cells
    lane = lax.broadcasted_iota(jnp.int32, cells.shape, 1)
    inside = lane < width - move if move > 0 else lane >= -move
    return jnp.where(inside, pltpu.roll(cells, (-move) % width, 1), 0.0)


def stencil(taps_ref, c, shifts, flip):
    total = None
    for b in range(7):
        column = None
        for a in range(7):
            tap = a * 7 + b
            term = taps_ref[c, 48 - tap if flip else tap] * shifts[a]
            column = term if column is None else column + term
        column = along(column, b - 3)
        total = column if total is None else total + column
    return total


def forward_body(taps_ref, bias_ref, x_ref, up_ref, down_ref, metric_ref, dy_ref, out_ref, ext, h_rows, dy_rows):
    cdev, rows, width = x_ref.shape
    fill_rows(x_ref, up_ref, down_ref, ext)
    dy_flat = dy_ref[...].astype(F32).reshape(cdev * rows, width)
    for t in range(width // 128):
        dy_rows[t] = dy_flat[:, t * 128 : t * 128 + 128]
    metric = jnp.broadcast_to(metric_ref[...], (rows, width))

    def channel(c, carry):
        h = bias_ref[c] + metric * stencil(taps_ref, c, row_shifts(ext, c, rows), False)
        for t in range(width // 128):
            h_rows[t, pl.ds(pl.multiple_of(c * rows, rows), rows), :] = h[:, t * 128 : t * 128 + 128]
        return carry

    lax.fori_loop(0, cdev, channel, 0, unroll=8)
    low = lax.broadcasted_iota(jnp.int32, (cdev, 128), 1) < 64
    for r in range(rows):
        for t in range(width // 128):
            h_tile, dy_tile = h_rows[t, pl.ds(r, cdev, rows), :], dy_rows[t, pl.ds(r, cdev, rows), :]
            at = (r * width + t * 128) // 64
            out_ref[at] = jnp.where(low, h_tile, pltpu.roll(dy_tile, 64, 1)).astype(BF)
            out_ref[at + 1] = jnp.where(low, pltpu.roll(h_tile, 64, 1), dy_tile).astype(BF)


def forward(taps, bias, x, up, down, metric, dy):
    cdev, rows, width = x.shape
    return call(
        forward_body,
        jax.ShapeDtypeStruct((rows * width // 64, cdev, 128), BF),
        [smem(), smem()] + [vmem()] * 5,
        [
            pltpu.VMEM((cdev, EXT, width), F32),
            pltpu.VMEM((width // 128, cdev * rows, 128), F32),
            pltpu.VMEM((width // 128, cdev * rows, 128), F32),
        ],
    )(taps, bias, x, up, down, metric[:, None], dy)


def norm_body(recv_ref, gain_ref, bias_ref, pair_ref, nhat_ref, rstd_ref):
    chans, lanes = recv_ref.shape
    piece = lanes // 2
    both = recv_ref[...].astype(F32).T
    h = both[:piece]
    mean = jnp.sum(h, 1, keepdims=True) / chans
    var = jnp.sum(h * h, 1, keepdims=True) / chans - mean * mean
    rstd = 1.0 / jnp.sqrt(var + 1e-06)
    nhat = (h - mean) * rstd
    nhat_ref[...] = nhat
    rstd_ref[...] = jnp.broadcast_to(rstd, rstd_ref.shape)
    n = (nhat * gain_ref[...] + bias_ref[...]).astype(BF)
    dy = both[piece:].astype(BF)
    for k in range(pair_ref.shape[0]):
        pair_ref[k, :piece] = n
        pair_ref[k, piece:] = dy


def norm(recv, gain, bias, copies):
    chans, lanes = recv.shape
    return call(
        norm_body,
        [
            jax.ShapeDtypeStruct((copies, lanes, chans), BF),
            jax.ShapeDtypeStruct((lanes // 2, chans), F32),
            jax.ShapeDtypeStruct((lanes // 2, 128), F32),
        ],
        [vmem()] * 3,
    )(recv, gain[None], bias[None])


def norm_back_body(recv_ref, nhat_ref, rstd_ref, gain_ref, gam_ref, db_ref, out_ref, flat):
    piece, chans = nhat_ref.shape
    dn = recv_ref[0].astype(F32)
    for k in range(1, recv_ref.shape[0]):
        dn = dn + recv_ref[k].astype(F32)
    nhat = nhat_ref[...]
    dnhat = dn * gain_ref[...]
    s1 = jnp.sum(dnhat, 1, keepdims=True) / chans
    s2 = jnp.sum(dnhat * nhat, 1, keepdims=True) / chans
    dh = rstd_ref[:, :1] * (dnhat - s1 - nhat * s2)
    flat[:piece] = dh
    flat[piece:] = jnp.zeros((flat.shape[0] - piece, chans), F32)
    sums = (jnp.sum(dn * nhat, 0, keepdims=True), jnp.sum(dn, 0, keepdims=True), gam_ref[...], db_ref[...])
    for k, value in enumerate(sums):
        high = value.astype(BF).astype(F32)
        flat[piece + 2 * k : piece + 2 * k + 1] = high
        flat[piece + 2 * k + 1 : piece + 2 * k + 2] = value - high
    blocks = flat[...].T.reshape(out_ref.shape[0], 24, 128)
    one, two, three = blocks[:, :8], blocks[:, 8:16], blocks[:, 16:]
    lane = lax.broadcasted_iota(jnp.int32, one.shape, 2)
    out_ref[:, :8] = jnp.where(lane < 64, one, pltpu.roll(three, 64, 2)).astype(BF)
    last = jnp.where(lane < 72, one, jnp.where(lane < 80, pltpu.roll(two, 8, 2), pltpu.roll(three, 16, 2)))
    out_ref[:, 8:] = jnp.where(lane < 64, two, last).astype(BF)


def norm_back(recv, nhat, rstd, gain, gam, db, owners):
    piece, chans = nhat.shape
    return call(
        norm_back_body,
        jax.ShapeDtypeStruct((owners, 16, 128), BF),
        [vmem()] * 6,
        [pltpu.VMEM((128, chans), F32)],
    )(recv, nhat, rstd, gain[None], gam, db)


def taps_body(recv_ref, x_ref, up_ref, down_ref, metric_ref, dy_ref, dconv_ref, ends_ref, sums_ref, extra_ref, ext, dh_rows, prods):
    cdev, rows, width = x_ref.shape
    fill_rows(x_ref, up_ref, down_ref, ext)
    low16 = lax.broadcasted_iota(jnp.int32, (16, 128), 1) < 64
    low8 = lax.broadcasted_iota(jnp.int32, (8, 128), 1) < 64
    extra = jnp.zeros((8, 128), F32)
    for r in range(rows):
        for t in range(width // 128):
            at = (r * width + t * 128) // 64
            first, second = recv_ref[at].astype(F32), recv_ref[at + 1].astype(F32)
            dh_rows[t, pl.ds(r, 16, rows), :] = jnp.where(low16, first, pltpu.roll(second, 64, 1))
            dh_rows[t, pl.ds(16 * rows + r, 8, rows), :] = jnp.where(low8, pltpu.roll(first[:8], 64, 1), second[:8])
            extra = extra + first[8:] + second[8:]
    for g in range(3):
        extra_ref[8 * g : 8 * g + 8] = pltpu.roll(extra, 64 - 8 * g, 1)
    metric = jnp.broadcast_to(metric_ref[...], (rows, width))

    def channel(c, carry):
        here = pl.ds(pl.multiple_of(c * rows, rows), rows)
        dh = jnp.concatenate([dh_rows[t, here, :] for t in range(width // 128)], 1)
        dconv = metric * dh
        dconv_ref[c] = dconv
        ends_ref[0, c] = dconv[:3].astype(BF)
        ends_ref[1, c] = dconv[rows - 3 :].astype(BF)
        shifts = row_shifts(ext, c, rows)
        for b in range(7):
            moved = along(dconv, 3 - b)
            for a in range(7):
                product = shifts[a] * moved
                prods[(a * 7 + b) * 8 : (a * 7 + b) * 8 + 8, :] = product[:, :128] + product[:, 128:]
        dy = dy_ref[c].astype(F32)
        prods[392:400, :] = dh[:, :128] + dh[:, 128:]
        prods[400:408, :] = dy[:, :128] + dy[:, 128:]
        total = prods[pl.ds(0, 56, 8), :]
        for i in range(1, 8):
            total = total + prods[pl.ds(i, 56, 8), :]
        sums_ref[c] = total
        return carry

    prods[408:, :] = jnp.zeros((prods.shape[0] - 408, 128), F32)
    lax.fori_loop(0, cdev, channel, 0, unroll=8)


def tap_sums(recv, x, up, down, metric, dy):
    cdev, rows, width = x.shape
    return call(
        taps_body,
        [
            jax.ShapeDtypeStruct((cdev, rows, width), F32),
            jax.ShapeDtypeStruct((2, cdev, 3, width), BF),
            jax.ShapeDtypeStruct((cdev, 56, 128), F32),
            jax.ShapeDtypeStruct((cdev, 128), F32),
        ],
        [vmem()] * 6,
        [
            pltpu.VMEM((cdev, EXT, width), F32),
            pltpu.VMEM((width // 128, cdev * rows, 128), F32),
            pltpu.VMEM((448, 128), F32),
        ],
    )(recv, x, up, down, metric[:, None], dy)


def spread_body(taps_ref, x_ref, up_ref, down_ref, dy_ref, out_ref, ext):
    cdev, rows, width = x_ref.shape
    fill_rows(x_ref, up_ref, down_ref, ext)

    def channel(c, carry):
        out_ref[c] = dy_ref[c].astype(F32) + stencil(taps_ref, c, row_shifts(ext, c, rows), True)
        return carry

    lax.fori_loop(0, cdev, channel, 0, unroll=8)


def spread_back(taps, dconv, up, down, dy):
    cdev, rows, width = dconv.shape
    return call(
        spread_body,
        jax.ShapeDtypeStruct((cdev, rows, width), F32),
        [smem()] + [vmem()] * 4,
        [pltpu.VMEM((cdev, EXT, width), F32)],
    )(taps, dconv, up, down, dy)


def picks(blocks, part):
    shape = (blocks * 2 * part, blocks * part)
    row = lax.broadcasted_iota(jnp.int32, shape, 0)
    place = lax.broadcasted_iota(jnp.int32, shape, 1)
    block = jnp.floor((row.astype(F32) + 0.5) * (0.5 / part)).astype(jnp.int32)
    inside = row - block * 2 * part
    first = (inside < part) & (place == block * part + inside)
    second = (inside >= part) & (place == block * part + inside - part)
    return [jnp.where(m, 1.0, 0.0).astype(BF) for m in (first, second)]


def dot(a, b, a_dim, b_dim):
    return lax.dot_general(a, b, (((a_dim,), (b_dim,)), ((), ())), preferred_element_type=F32)


def weights_body(part, own_ref, one_ref, low_ref, high_ref, last_ref, wi_ref, wo_ref, bi_ref, rows):
    blocks = 0
    for ref in (own_ref, one_ref, low_ref, high_ref, last_ref):
        for k in range(ref.shape[0]):
            at = blocks * 2 * part
            rows[at : at + 2 * part] = ref[k].astype(F32)
            blocks += 1
    chans = wi_ref.shape[1]
    flat = rows[...].astype(BF)
    first, second = picks(blocks, part)
    wi_ref[...] = dot(first, flat[:, :chans], 0, 0).astype(BF)
    wo_ref[...] = dot(second, flat[:, :chans], 0, 0).astype(BF)
    both = dot(flat[:, chans:], first, 0, 0)
    bi_ref[...] = both[:1] + both[1:2]


def weights(parts, part, chans):
    blocks = sum(p.shape[0] for p in parts)
    return call(
        functools.partial(weights_body, part),
        [
            jax.ShapeDtypeStruct((blocks * part, chans), BF),
            jax.ShapeDtypeStruct((blocks * part, chans), BF),
            jax.ShapeDtypeStruct((1, blocks * part), F32),
        ],
        [vmem()] * len(parts),
        [pltpu.VMEM((blocks * 2 * part, parts[0].shape[2]), F32)],
    )(*parts)


def fill_tokens(own_ref, other_ref, n_ref, dy_ref):
    members, lanes, _ = own_ref.shape
    piece = lanes // 2
    for at, ref in ((0, own_ref), (members, other_ref)):
        for k in range(members):
            n_ref[(at + k) * piece : (at + k + 1) * piece] = ref[k, :piece]
            dy_ref[(at + k) * piece : (at + k + 1) * piece] = ref[k, piece:]


def mlp_body(core_ref, own_ref, other_ref, wi_ref, wo_ref, bi_ref, gamma_ref, dn_ref, acts_ref, n_ref, dy_ref):
    members, lanes, _ = own_ref.shape
    piece = lanes // 2
    fill_tokens(own_ref, other_ref, n_ref, dy_ref)
    pre = dot(n_ref[...], wi_ref[...], 1, 1) + bi_ref[...]
    cdf = 0.5 + 0.5 * lax.erf(pre * (0.5**0.5))
    hid = pre.shape[1]
    acts_ref[:, :hid] = (pre * cdf).astype(BF)
    slope = cdf + pre * (jnp.exp(-0.5 * pre * pre) * (0.5 / 3.141592653589793) ** 0.5)
    dmlp = (gamma_ref[...] * dy_ref[...].astype(F32)).astype(BF)
    dpre = (slope * dot(dmlp, wo_ref[...], 1, 1)).astype(BF)
    acts_ref[:, hid:] = dpre
    dn = dot(dpre, wi_ref[...], 1, 0).astype(BF)
    core = core_ref[0]
    for k in range(members):
        dn_ref[core * members + k] = dn[k * piece : (k + 1) * piece]
        dn_ref[(1 - core) * members + k] = dn[(members + k) * piece : (members + k + 1) * piece]


def mlp(core, own, other, wi, wo, bi, gamma):
    members, lanes, chans = own.shape
    toks, hid = members * lanes, wi.shape[0]
    return call(
        mlp_body,
        [
            jax.ShapeDtypeStruct((2 * members, lanes // 2, chans), BF),
            jax.ShapeDtypeStruct((toks, 2 * hid), BF),
        ],
        [smem()] + [vmem()] * 6,
        [pltpu.VMEM((toks, chans), BF)] * 2,
    )(core, own, other, wi, wo, bi, gamma[None])


def grads_body(part, ny, place_ref, own_ref, other_ref, acts_ref, wo_ref, gamma_ref, out_ref, gam_ref, db_ref, n_ref, dy_ref):
    toks = n_ref.shape[0]
    fill_tokens(own_ref, other_ref, n_ref, dy_ref)
    hid = acts_ref.shape[1] // 2
    first, second = picks(hid // part, part)
    dpre = acts_ref[:, hid:]
    dw_in = dot(dpre, n_ref[...], 0, 0).astype(BF)
    proj = dot(acts_ref[:, :hid], dy_ref[...], 0, 0)
    gam_ref[...] = jnp.sum(wo_ref[...].astype(F32) * proj, 0, keepdims=True)
    dw_out = (proj * gamma_ref[...]).astype(BF)
    out_ref[...] = (dot(first, dw_in, 1, 0) + dot(second, dw_out, 1, 0)).astype(BF)
    nz = hid // part // ny
    lane = lax.broadcasted_iota(jnp.int32, (db_ref.shape[1], hid), 0)
    place = lax.broadcasted_iota(jnp.int32, (1, hid), 1)
    block = jnp.floor((place.astype(F32) + 0.5) * (1.0 / part)).astype(jnp.int32)
    ring = jnp.floor((block.astype(F32) + 0.5) * (1.0 / nz)).astype(jnp.int32)
    ahead = ring + place_ref[0]
    along_z = block - ring * nz
    far = along_z >= nz // 2
    zq = jnp.where(far, along_z - nz // 2, along_z)
    zp = jnp.where(far, 1 - place_ref[1], place_ref[1])
    owner = (zq * 2 + zp) * ny + jnp.where(ahead >= ny, ahead - ny, ahead)
    spot = jnp.where(lane == owner * 2 * part + place - block * part, 1.0, 0.0).astype(BF)
    db = dot(jnp.ones((16, toks), BF), dpre, 1, 0).astype(BF)
    db_ref[...] = dot(db, spot, 1, 1)[:1]


def grads(part, ny, place, own, other, acts, wo, gamma):
    toks, chans = acts.shape[0], own.shape[2]
    hid = acts.shape[1] // 2
    return call(
        functools.partial(grads_body, part, ny),
        [
            jax.ShapeDtypeStruct((2 * hid, chans), BF),
            jax.ShapeDtypeStruct((1, chans), F32),
            jax.ShapeDtypeStruct((1, 2 * hid), F32),
        ],
        [smem()] + [vmem()] * 5,
        [pltpu.VMEM((toks, chans), BF)] * 2,
    )(place, own, other, acts, wo, gamma[None])


def slices_body(part, member_ref, w_in_ref, w_out_ref, b_ref, out_ref):
    hdev, chans = w_in_ref.shape
    row = lax.broadcasted_iota(jnp.int32, (2 * part, hdev), 0)
    place = lax.broadcasted_iota(jnp.int32, (2 * part, hdev), 1)
    start = member_ref[0] * part
    first = jnp.where((row < part) & (place == start + row), 1.0, 0.0).astype(BF)
    second = jnp.where((row >= part) & (place == start + row - part), 1.0, 0.0).astype(BF)
    rows = (dot(first, w_in_ref[...], 1, 0) + dot(second, w_out_ref[...], 1, 0)).astype(BF)
    bias = jnp.broadcast_to(b_ref[...], (SIDE, hdev))
    high = bias.astype(BF)
    low = (bias - high.astype(F32)).astype(BF)
    line = lax.broadcasted_iota(jnp.int32, (SIDE, hdev), 0)
    high = jnp.where(line == 0, high.astype(F32), jnp.where(line == 1, low.astype(F32), 0.0)).astype(BF)
    side = dot(first, high, 1, 1).astype(BF)
    for k in range(out_ref.shape[0]):
        out_ref[k, :, :chans] = rows
        out_ref[k, :, chans:] = side


def slices(part, copies, member, w_in, w_out, b_in):
    return call(
        functools.partial(slices_body, part),
        jax.ShapeDtypeStruct((copies, 2 * part, w_in.shape[1] + SIDE), BF),
        [smem()] + [vmem()] * 3,
    )(member, w_in, w_out, b_in[None])


def results_body(part, n_taps, gathered_ref, gamma_ref, b_out_ref, dw_in_ref, dw_out_ref, taps_ref, db_ref, rest_ref):
    chans = dw_in_ref.shape[1]
    total = None
    for k in range(gathered_ref.shape[0]):
        block = gathered_ref[k].astype(F32)
        dw_in_ref[k * part : (k + 1) * part] = block[:part, :chans]
        dw_out_ref[k * part : (k + 1) * part] = block[part:, :chans]
        side = block[:, chans:]
        side = side + pltpu.roll(side, 64, 1)
        line = side.T
        db_ref[k : k + 1] = (line[62:63] + line[63:64])[:, :part]
        total = side if total is None else total + side
    taps_ref[...] = total[:, :n_taps]
    lines = total.T
    dysum = lines[n_taps + 1 : n_taps + 2]
    rest_ref[0:1] = lines[n_taps : n_taps + 1]
    rest_ref[1:2] = lines[56:57] + lines[57:58]
    rest_ref[2:3] = lines[58:59] + lines[59:60]
    rest_ref[3:4] = gamma_ref[...] * dysum
    rest_ref[4:5] = lines[60:61] + lines[61:62] + b_out_ref[...] * dysum


def results(part, n_taps, gathered, chans, gamma, b_out):
    members, rows, _ = gathered.shape
    return call(
        functools.partial(results_body, part, n_taps),
        [
            jax.ShapeDtypeStruct((members * part, chans), F32),
            jax.ShapeDtypeStruct((members * part, chans), F32),
            jax.ShapeDtypeStruct((rows, n_taps), F32),
            jax.ShapeDtypeStruct((members, part), F32),
            jax.ShapeDtypeStruct((5, rows), F32),
        ],
        [vmem()] * 3,
    )(gathered, gamma[None], b_out[None])


def to_neighbour(blocks):
    half = blocks.shape[0] // 2
    return blocks[:half] + lax.ppermute(blocks[half:].astype(BF), "zp", [(0, 1), (1, 0)]).astype(F32)


def to_both(blocks):
    both = jnp.broadcast_to(blocks[None], (2,) + blocks.shape).reshape((-1,) + blocks.shape[1:])
    return lax.all_to_all(both, ("zh", "zq"), 0, 0, tiled=True)


def two_parts(value):
    high = lax.reduce_precision(value, 8, 7)
    return high.astype(BF), (value - high).astype(BF)


def to_all(block, axis):
    count = lax.axis_size(axis)
    return lax.all_to_all(jnp.broadcast_to(block[None], (count,) + block.shape), axis, 0, 0, tiled=True)


def exchange(blocks):
    return lax.all_to_all(blocks, CHAN, 0, 0, tiled=True)


def halos(first, last):
    count = lax.axis_size(LAT)
    place = lax.axis_index(LAT)
    even = place % 2 == 0
    pairs = [(i, i + 1) for i in range(0, count, 2)]
    within = lax.ppermute(jnp.where(even, last, first), LAT, pairs + [(j, i) for i, j in pairs])
    pairs = [(i, i + 1) for i in range(1, count - 1, 2)]
    across = lax.ppermute(jnp.where(even, first, last), LAT, pairs + [(j, i) for i, j in pairs])
    return jnp.where(even, across, within), jnp.where(even, within, across)


def along_ring(block, ahead):
    count = lax.axis_size("y")
    return lax.ppermute(block, "y", [((i + ahead) % count, i) for i in range(count)])


def to_ring(blocks):
    count = lax.axis_size("y")
    total = blocks[0].astype(F32)
    for k in range(1, count):
        total = total + lax.ppermute(blocks[k], "y", [(i, (i + k) % count) for i in range(count)]).astype(F32)
    return total


def per_device(
    block_input,
    out_grad,
    metric,
    kernel,
    conv_bias,
    ln_gain,
    ln_bias,
    w_in,
    b_in,
    w_out,
    b_out,
    layer_scale,
):
    cdev, rows, width = block_input.shape
    chans = ln_gain.shape[0]
    tokens = rows * width
    nz, ny = lax.axis_size(ZLO), lax.axis_size("y")
    nchan = nz * ny
    hdev = w_in.shape[0]
    part = hdev // GROUP
    piece = tokens // nchan
    owner = lax.axis_index(CHAN)
    gamma_f = layer_scale.astype(F32)
    gamma_own = lax.dynamic_slice_in_dim(gamma_f, owner * cdev, cdev)

    member = lax.axis_index(("x", "c")).astype(jnp.int32)[None]
    shards = lax.all_to_all(slices(part, nz // 2, member, w_in, w_out, b_in), "zq", 0, 0, tiled=True)
    beside = lax.ppermute(shards, "zp", [(0, 1), (1, 0)])

    up, down = halos(block_input[:, :3], block_input[:, rows - 3 :])
    blocks = forward(kernel, conv_bias, block_input, up, down, metric, out_grad)
    blocks, shards, beside = lax.optimization_barrier((blocks, shards, beside))

    recv = exchange(blocks)
    shards = jnp.concatenate([shards, beside], 0)
    one, last = along_ring(shards, 1), along_ring(shards, -1)
    recv, one, last = lax.optimization_barrier((recv, one, last))

    pair, nhat, rstd = norm(recv.reshape(chans, 2 * piece), ln_gain, ln_bias, GROUP // 2)
    pair = lax.all_to_all(pair, "x", 0, 0, tiled=True)
    low, high = along_ring(one[: nz // 2], 1), along_ring(last[nz // 2 :], -1)
    pair, low, high = lax.optimization_barrier((pair, low, high))
    wi, wo, bi = weights([shards, one, low, high, last], part, chans)
    other = lax.ppermute(pair, "c", [(0, 1), (1, 0)])

    core = lax.axis_index("c").astype(jnp.int32)[None]
    dn, acts = mlp(core, pair, other, wi, wo, bi, gamma_f)
    dn = lax.all_to_all(dn, ("c", "x"), 0, 0, tiled=True)

    place = jnp.stack([lax.axis_index("y"), lax.axis_index("zp")]).astype(jnp.int32)
    dws, gam_part, db_part = grads(part, ny, place, pair, other, acts, wo, gamma_f)
    dws = to_ring(dws.reshape(ny, nz, 2 * part, chans))
    dws = to_neighbour(dws).astype(BF)

    payload = exchange(norm_back(dn, nhat, rstd, ln_gain, gam_part, db_part, nchan))
    dconv, ends, taps, extra = tap_sums(payload, block_input, up, down, metric, out_grad)
    dup, ddown = halos(ends[0], ends[1])

    small = jnp.concatenate([jnp.sum(taps, 2), extra[:, :8]], 1)
    count = small.shape[1]
    own = lax.broadcasted_iota(jnp.int32, (nz // 2, 1, 1), 0) == lax.axis_index("zq")
    beside = jnp.where(own, jnp.concatenate(two_parts(small), 1)[None], jnp.zeros((), BF))
    dws = to_both(jnp.concatenate([dws, beside], 2))
    dws = jnp.sum(dws.astype(F32), 0)
    small = dws[:, chans : chans + count] + dws[:, chans + count :]
    dws = dws[:, :chans]
    mine = jnp.concatenate([dws.astype(BF)] + list(two_parts(small)), 1)
    mine, dup, ddown = lax.optimization_barrier((mine, dup, ddown))
    grad_input = spread_back(kernel, dconv, dup, ddown, out_grad)
    grad_w_in, grad_w_out, grad_kernel, db, rest = results(
        part, kernel.shape[1], to_all(mine, ("x", "c")), chans, gamma_own, b_out
    )
    return (
        grad_input,
        grad_kernel,
        rest[0],
        rest[1],
        rest[2],
        grad_w_in,
        db.reshape(hdev),
        grad_w_out,
        rest[3],
        rest[4],
    )


def solution(mesh):
    split = Mesh(mesh.devices.reshape(2, 4, 2, 4, 2, 4), ("zh", "x", "c", "zq", "zp", "y"))
    return jax.shard_map(
        per_device,
        mesh=split,
        in_specs=(
            P(CHAN, LAT, None),
            P(CHAN, LAT, None),
            P(LAT),
            P(CHAN, None),
            P(CHAN),
            P(),
            P(),
            P(CHAN, None),
            P(CHAN),
            P(CHAN, None),
            P(CHAN),
            P(),
        ),
        out_specs=(
            P(CHAN, LAT, None),
            P(CHAN, None),
            P(CHAN),
            P(CHAN),
            P(CHAN),
            P(CHAN, None),
            P(CHAN),
            P(CHAN, None),
            P(CHAN),
            P(CHAN),
        ),
        check_vma=False,
    )
```

```python
import functools

import jax
import jax.numpy as jnp
from jax import lax
from jax.experimental import pallas as pl
from jax.experimental.pallas import tpu as pltpu
from jax.sharding import Mesh, PartitionSpec as P

LAT = ("zh", "x", "c")
ZLO = ("zq", "zp")
CHAN = ("zq", "zp", "y")
GROUP = 8
F32 = jnp.float32
BF = jnp.bfloat16
EXT = 16
VMEM_BYTES = 20 * 1024 * 1024
SIDE = 128


def vmem():
    return pl.BlockSpec(memory_space=pltpu.VMEM)


def smem():
    return pl.BlockSpec(memory_space=pltpu.SMEM)


def call(body, out_shape, in_specs, scratch=()):
    many = isinstance(out_shape, (list, tuple))
    return pl.pallas_call(
        body,
        out_shape=out_shape,
        in_specs=in_specs,
        out_specs=[vmem()] * len(out_shape) if many else vmem(),
        scratch_shapes=list(scratch),
        compiler_params=pltpu.CompilerParams(vmem_limit_bytes=VMEM_BYTES),
    )


def fill_rows(x_ref, up_ref, down_ref, ext):
    rows = x_ref.shape[1]
    ext[:, :3, :] = up_ref[...].astype(F32)
    ext[:, 3 : 3 + rows, :] = x_ref[...].astype(F32)
    ext[:, 3 + rows : 6 + rows, :] = down_ref[...].astype(F32)


def row_shifts(ext, c, rows):
    return [ext[c, a : a + rows, :] for a in range(7)]


def along(cells, move):
    width = cells.shape[1]
    if move == 0:
        return cells
    lane = lax.broadcasted_iota(jnp.int32, cells.shape, 1)
    inside = lane < width - move if move > 0 else lane >= -move
    return jnp.where(inside, pltpu.roll(cells, (-move) % width, 1), 0.0)


def stencil(taps_ref, c, shifts, flip):
    total = None
    for b in range(7):
        column = None
        for a in range(7):
            tap = a * 7 + b
            term = taps_ref[c, 48 - tap if flip else tap] * shifts[a]
            column = term if column is None else column + term
        column = along(column, b - 3)
        total = column if total is None else total + column
    return total


def forward_body(taps_ref, bias_ref, x_ref, up_ref, down_ref, metric_ref, dy_ref, out_ref, ext, h_rows, dy_rows):
    cdev, rows, width = x_ref.shape
    fill_rows(x_ref, up_ref, down_ref, ext)
    dy_flat = dy_ref[...].astype(F32).reshape(cdev * rows, width)
    for t in range(width // 128):
        dy_rows[t] = dy_flat[:, t * 128 : t * 128 + 128]
    metric = jnp.broadcast_to(metric_ref[...], (rows, width))

    def channel(c, carry):
        h = bias_ref[c] + metric * stencil(taps_ref, c, row_shifts(ext, c, rows), False)
        for t in range(width // 128):
            h_rows[t, pl.ds(pl.multiple_of(c * rows, rows), rows), :] = h[:, t * 128 : t * 128 + 128]
        return carry

    lax.fori_loop(0, cdev, channel, 0, unroll=8)
    low = lax.broadcasted_iota(jnp.int32, (cdev, 128), 1) < 64
    for r in range(rows):
        for t in range(width // 128):
            h_tile, dy_tile = h_rows[t, pl.ds(r, cdev, rows), :], dy_rows[t, pl.ds(r, cdev, rows), :]
            at = (r * width + t * 128) // 64
            out_ref[at] = jnp.where(low, h_tile, pltpu.roll(dy_tile, 64, 1)).astype(BF)
            out_ref[at + 1] = jnp.where(low, pltpu.roll(h_tile, 64, 1), dy_tile).astype(BF)


def forward(taps, bias, x, up, down, metric, dy):
    cdev, rows, width = x.shape
    return call(
        forward_body,
        jax.ShapeDtypeStruct((rows * width // 64, cdev, 128), BF),
        [smem(), smem()] + [vmem()] * 5,
        [
            pltpu.VMEM((cdev, EXT, width), F32),
            pltpu.VMEM((width // 128, cdev * rows, 128), F32),
            pltpu.VMEM((width // 128, cdev * rows, 128), F32),
        ],
    )(taps, bias, x, up, down, metric[:, None], dy)


def norm_body(recv_ref, gain_ref, bias_ref, pair_ref, nhat_ref, rstd_ref):
    chans, lanes = recv_ref.shape
    piece = lanes // 2
    both = recv_ref[...].astype(F32).T
    h = both[:piece]
    mean = jnp.sum(h, 1, keepdims=True) / chans
    var = jnp.sum(h * h, 1, keepdims=True) / chans - mean * mean
    rstd = 1.0 / jnp.sqrt(var + 1e-06)
    nhat = (h - mean) * rstd
    nhat_ref[...] = nhat
    rstd_ref[...] = jnp.broadcast_to(rstd, rstd_ref.shape)
    n = (nhat * gain_ref[...] + bias_ref[...]).astype(BF)
    dy = both[piece:].astype(BF)
    for k in range(pair_ref.shape[0]):
        pair_ref[k, :piece] = n
        pair_ref[k, piece:] = dy


def norm(recv, gain, bias, copies):
    chans, lanes = recv.shape
    return call(
        norm_body,
        [
            jax.ShapeDtypeStruct((copies, lanes, chans), BF),
            jax.ShapeDtypeStruct((lanes // 2, chans), F32),
            jax.ShapeDtypeStruct((lanes // 2, 128), F32),
        ],
        [vmem()] * 3,
    )(recv, gain[None], bias[None])


def norm_back_body(recv_ref, nhat_ref, rstd_ref, gain_ref, gam_ref, db_ref, out_ref, flat):
    piece, chans = nhat_ref.shape
    dn = recv_ref[0].astype(F32)
    for k in range(1, recv_ref.shape[0]):
        dn = dn + recv_ref[k].astype(F32)
    nhat = nhat_ref[...]
    dnhat = dn * gain_ref[...]
    s1 = jnp.sum(dnhat, 1, keepdims=True) / chans
    s2 = jnp.sum(dnhat * nhat, 1, keepdims=True) / chans
    dh = rstd_ref[:, :1] * (dnhat - s1 - nhat * s2)
    flat[:piece] = dh
    flat[piece:] = jnp.zeros((flat.shape[0] - piece, chans), F32)
    sums = (jnp.sum(dn * nhat, 0, keepdims=True), jnp.sum(dn, 0, keepdims=True), gam_ref[...], db_ref[...])
    for k, value in enumerate(sums):
        high = value.astype(BF).astype(F32)
        flat[piece + 2 * k : piece + 2 * k + 1] = high
        flat[piece + 2 * k + 1 : piece + 2 * k + 2] = value - high
    blocks = flat[...].T.reshape(out_ref.shape[0], 24, 128)
    one, two, three = blocks[:, :8], blocks[:, 8:16], blocks[:, 16:]
    lane = lax.broadcasted_iota(jnp.int32, one.shape, 2)
    out_ref[:, :8] = jnp.where(lane < 64, one, pltpu.roll(three, 64, 2)).astype(BF)
    last = jnp.where(lane < 72, one, jnp.where(lane < 80, pltpu.roll(two, 8, 2), pltpu.roll(three, 16, 2)))
    out_ref[:, 8:] = jnp.where(lane < 64, two, last).astype(BF)


def norm_back(recv, nhat, rstd, gain, gam, db, owners):
    piece, chans = nhat.shape
    return call(
        norm_back_body,
        jax.ShapeDtypeStruct((owners, 16, 128), BF),
        [vmem()] * 6,
        [pltpu.VMEM((128, chans), F32)],
    )(recv, nhat, rstd, gain[None], gam, db)


def dconv_body(recv_ref, metric_ref, dconv_ref, ends_ref, sums_ref, extra_ref, dh_rows):
    cdev, rows, width = dconv_ref.shape
    low16 = lax.broadcasted_iota(jnp.int32, (16, 128), 1) < 64
    low8 = lax.broadcasted_iota(jnp.int32, (8, 128), 1) < 64
    extra = jnp.zeros((8, 128), F32)
    for r in range(rows):
        for t in range(width // 128):
            at = (r * width + t * 128) // 64
            first, second = recv_ref[at].astype(F32), recv_ref[at + 1].astype(F32)
            dh_rows[t, pl.ds(r, 16, rows), :] = jnp.where(low16, first, pltpu.roll(second, 64, 1))
            dh_rows[t, pl.ds(16 * rows + r, 8, rows), :] = jnp.where(low8, pltpu.roll(first[:8], 64, 1), second[:8])
            extra = extra + first[8:] + second[8:]
    for g in range(3):
        extra_ref[8 * g : 8 * g + 8] = pltpu.roll(extra, 64 - 8 * g, 1)
    metric = jnp.broadcast_to(metric_ref[...], (rows, 128))
    for c in range(cdev):
        for t in range(width // 128):
            dh = dh_rows[t, c * rows : (c + 1) * rows, :]
            dconv = metric * dh
            lanes = slice(t * 128, t * 128 + 128)
            dconv_ref[c, :, lanes] = dconv
            ends_ref[0, c, :, lanes] = dconv[:3].astype(BF)
            ends_ref[1, c, :, lanes] = dconv[rows - 3 :].astype(BF)
            sums_ref[c] = dh if t == 0 else sums_ref[c] + dh


def stencil_cotangent(recv, metric, cdev, width):
    rows = metric.shape[0]
    return call(
        dconv_body,
        [
            jax.ShapeDtypeStruct((cdev, rows, width), F32),
            jax.ShapeDtypeStruct((2, cdev, 3, width), BF),
            jax.ShapeDtypeStruct((cdev, rows, 128), F32),
            jax.ShapeDtypeStruct((cdev, 128), F32),
        ],
        [vmem()] * 2,
        [pltpu.VMEM((width // 128, cdev * rows, 128), F32)],
    )(recv, metric[:, None])


def taps_body(dconv_ref, dh_sums_ref, x_ref, up_ref, down_ref, dy_ref, sums_ref, ext, prods):
    cdev, rows, width = x_ref.shape
    fill_rows(x_ref, up_ref, down_ref, ext)

    def channel(c, carry):
        dconv = dconv_ref[c]
        shifts = row_shifts(ext, c, rows)
        for b in range(7):
            moved = along(dconv, 3 - b)
            for a in range(7):
                product = shifts[a] * moved
                prods[(a * 7 + b) * 8 : (a * 7 + b) * 8 + 8, :] = product[:, :128] + product[:, 128:]
        dy = dy_ref[c].astype(F32)
        prods[392:400, :] = dh_sums_ref[c]
        prods[400:408, :] = dy[:, :128] + dy[:, 128:]
        total = prods[pl.ds(0, 56, 8), :]
        for i in range(1, 8):
            total = total + prods[pl.ds(i, 56, 8), :]
        sums_ref[c] = total
        return carry

    prods[408:, :] = jnp.zeros((prods.shape[0] - 408, 128), F32)
    lax.fori_loop(0, cdev, channel, 0, unroll=8)


def tap_sums(dconv, dh_sums, x, up, down, dy):
    cdev, rows, width = x.shape
    return call(
        taps_body,
        jax.ShapeDtypeStruct((cdev, 56, 128), F32),
        [vmem()] * 6,
        [pltpu.VMEM((cdev, EXT, width), F32), pltpu.VMEM((448, 128), F32)],
    )(dconv, dh_sums, x, up, down, dy)


def spread_body(taps_ref, x_ref, up_ref, down_ref, dy_ref, out_ref, ext):
    cdev, rows, width = x_ref.shape
    fill_rows(x_ref, up_ref, down_ref, ext)

    def channel(c, carry):
        out_ref[c] = dy_ref[c].astype(F32) + stencil(taps_ref, c, row_shifts(ext, c, rows), True)
        return carry

    lax.fori_loop(0, cdev, channel, 0, unroll=8)


def spread_back(taps, dconv, up, down, dy):
    cdev, rows, width = dconv.shape
    return call(
        spread_body,
        jax.ShapeDtypeStruct((cdev, rows, width), F32),
        [smem()] + [vmem()] * 4,
        [pltpu.VMEM((cdev, EXT, width), F32)],
    )(taps, dconv, up, down, dy)


def picks(blocks, part):
    shape = (blocks * 2 * part, blocks * part)
    row = lax.broadcasted_iota(jnp.int32, shape, 0)
    place = lax.broadcasted_iota(jnp.int32, shape, 1)
    block = jnp.floor((row.astype(F32) + 0.5) * (0.5 / part)).astype(jnp.int32)
    inside = row - block * 2 * part
    first = (inside < part) & (place == block * part + inside)
    second = (inside >= part) & (place == block * part + inside - part)
    return [jnp.where(m, 1.0, 0.0).astype(BF) for m in (first, second)]


def dot(a, b, a_dim, b_dim):
    return lax.dot_general(a, b, (((a_dim,), (b_dim,)), ((), ())), preferred_element_type=F32)


def weights_body(part, own_ref, one_ref, low_ref, high_ref, last_ref, wi_ref, wo_ref, bi_ref, rows):
    blocks = 0
    for ref in (own_ref, one_ref, low_ref, high_ref, last_ref):
        for k in range(ref.shape[0]):
            at = blocks * 2 * part
            rows[at : at + 2 * part] = ref[k].astype(F32)
            blocks += 1
    chans = wi_ref.shape[1]
    flat = rows[...].astype(BF)
    first, second = picks(blocks, part)
    wi_ref[...] = dot(first, flat[:, :chans], 0, 0).astype(BF)
    wo_ref[...] = dot(second, flat[:, :chans], 0, 0).astype(BF)
    both = dot(flat[:, chans:], first, 0, 0)
    bi_ref[...] = both[:1] + both[1:2]


def weights(parts, part, chans):
    blocks = sum(p.shape[0] for p in parts)
    return call(
        functools.partial(weights_body, part),
        [
            jax.ShapeDtypeStruct((blocks * part, chans), BF),
            jax.ShapeDtypeStruct((blocks * part, chans), BF),
            jax.ShapeDtypeStruct((1, blocks * part), F32),
        ],
        [vmem()] * len(parts),
        [pltpu.VMEM((blocks * 2 * part, parts[0].shape[2]), F32)],
    )(*parts)


def mlp_body(core_ref, own_ref, other_ref, wi_ref, wo_ref, bi_ref, gamma_ref, dn_ref, n_ref, dy_ref, acts_ref):
    members, lanes, _ = own_ref.shape
    piece = lanes // 2
    for at, ref in ((0, own_ref), (members, other_ref)):
        for k in range(members):
            n_ref[(at + k) * piece : (at + k + 1) * piece] = ref[k, :piece]
            dy_ref[(at + k) * piece : (at + k + 1) * piece] = ref[k, piece:]
    pre = dot(n_ref[...], wi_ref[...], 1, 1) + bi_ref[...]
    cdf = 0.5 + 0.5 * lax.erf(pre * (0.5**0.5))
    hid = pre.shape[1]
    acts_ref[:, :hid] = (pre * cdf).astype(BF)
    slope = cdf + pre * (jnp.exp(-0.5 * pre * pre) * (0.5 / 3.141592653589793) ** 0.5)
    dmlp = (gamma_ref[...] * dy_ref[...].astype(F32)).astype(BF)
    dpre = (slope * dot(dmlp, wo_ref[...], 1, 1)).astype(BF)
    acts_ref[:, hid:] = dpre
    dn = dot(dpre, wi_ref[...], 1, 0).astype(BF)
    core = core_ref[0]
    for k in range(members):
        dn_ref[core * members + k] = dn[k * piece : (k + 1) * piece]
        dn_ref[(1 - core) * members + k] = dn[(members + k) * piece : (members + k + 1) * piece]


def mlp(core, own, other, wi, wo, bi, gamma):
    members, lanes, chans = own.shape
    toks, hid = members * lanes, wi.shape[0]
    return call(
        mlp_body,
        [
            jax.ShapeDtypeStruct((2 * members, lanes // 2, chans), BF),
            jax.ShapeDtypeStruct((toks, chans), BF),
            jax.ShapeDtypeStruct((toks, chans), BF),
            jax.ShapeDtypeStruct((toks, 2 * hid), BF),
        ],
        [smem()] + [vmem()] * 6,
    )(core, own, other, wi, wo, bi, gamma[None])


def grads_body(part, ny, place_ref, n_ref, dy_ref, acts_ref, wo_ref, gamma_ref, out_ref, gam_ref, db_ref):
    toks = n_ref.shape[0]
    hid = acts_ref.shape[1] // 2
    first, second = picks(hid // part, part)
    dpre = acts_ref[:, hid:]
    dw_in = dot(dpre, n_ref[...], 0, 0).astype(BF)
    proj = dot(acts_ref[:, :hid], dy_ref[...], 0, 0)
    gam_ref[...] = jnp.sum(wo_ref[...].astype(F32) * proj, 0, keepdims=True)
    dw_out = (proj * gamma_ref[...]).astype(BF)
    out_ref[...] = (dot(first, dw_in, 1, 0) + dot(second, dw_out, 1, 0)).astype(BF)
    nz = hid // part // ny
    lane = lax.broadcasted_iota(jnp.int32, (db_ref.shape[1], hid), 0)
    place = lax.broadcasted_iota(jnp.int32, (1, hid), 1)
    block = jnp.floor((place.astype(F32) + 0.5) * (1.0 / part)).astype(jnp.int32)
    ring = jnp.floor((block.astype(F32) + 0.5) * (1.0 / nz)).astype(jnp.int32)
    ahead = ring + place_ref[0]
    along_z = block - ring * nz
    far = along_z >= nz // 2
    zq = jnp.where(far, along_z - nz // 2, along_z)
    zp = jnp.where(far, 1 - place_ref[1], place_ref[1])
    owner = (zq * 2 + zp) * ny + jnp.where(ahead >= ny, ahead - ny, ahead)
    spot = jnp.where(lane == owner * 2 * part + place - block * part, 1.0, 0.0).astype(BF)
    db = dot(jnp.ones((16, toks), BF), dpre, 1, 0).astype(BF)
    db_ref[...] = dot(db, spot, 1, 1)[:1]


def grads(part, ny, place, n, dy, acts, wo, gamma):
    chans = n.shape[1]
    hid = acts.shape[1] // 2
    return call(
        functools.partial(grads_body, part, ny),
        [
            jax.ShapeDtypeStruct((2 * hid, chans), BF),
            jax.ShapeDtypeStruct((1, chans), F32),
            jax.ShapeDtypeStruct((1, 2 * hid), F32),
        ],
        [smem()] + [vmem()] * 5,
    )(place, n, dy, acts, wo, gamma[None])


def slices_body(w_in_ref, w_out_ref, b_ref, out_ref):
    part, chans = w_in_ref.shape
    row = lax.broadcasted_iota(jnp.int32, (2 * part, part), 0)
    place = lax.broadcasted_iota(jnp.int32, (2 * part, part), 1)
    first = jnp.where(row == place, 1.0, 0.0).astype(BF)
    second = jnp.where(row == place + part, 1.0, 0.0).astype(BF)
    rows = (dot(first, w_in_ref[...], 1, 0) + dot(second, w_out_ref[...], 1, 0)).astype(BF)
    bias = jnp.broadcast_to(b_ref[...], (SIDE, part))
    high = bias.astype(BF).astype(F32)
    line = lax.broadcasted_iota(jnp.int32, (SIDE, part), 0)
    both = jnp.where(line == 0, high, jnp.where(line == 1, bias - high, 0.0)).astype(BF)
    side = dot(first, both, 1, 1).astype(BF)
    for k in range(out_ref.shape[0]):
        out_ref[k, :, :chans] = rows
        out_ref[k, :, chans:] = side


def slices(copies, w_in, w_out, b_in):
    part, chans = w_in.shape
    return call(
        slices_body,
        jax.ShapeDtypeStruct((copies, 2 * part, chans + SIDE), BF),
        [vmem()] * 3,
    )(w_in, w_out, b_in[None])


def results_body(part, n_taps, gathered_ref, gamma_ref, b_out_ref, dw_in_ref, dw_out_ref, taps_ref, db_ref, rest_ref):
    chans = dw_in_ref.shape[1]
    total = None
    for k in range(gathered_ref.shape[0]):
        block = gathered_ref[k].astype(F32)
        dw_in_ref[k * part : (k + 1) * part] = block[:part, :chans]
        dw_out_ref[k * part : (k + 1) * part] = block[part:, :chans]
        side = block[:, chans:]
        side = side + pltpu.roll(side, 64, 1)
        line = side.T
        db_ref[k : k + 1] = (line[62:63] + line[63:64])[:, :part]
        total = side if total is None else total + side
    taps_ref[...] = total[:, :n_taps]
    lines = total.T
    dysum = lines[n_taps + 1 : n_taps + 2]
    rest_ref[0:1] = lines[n_taps : n_taps + 1]
    rest_ref[1:2] = lines[56:57] + lines[57:58]
    rest_ref[2:3] = lines[58:59] + lines[59:60]
    rest_ref[3:4] = gamma_ref[...] * dysum
    rest_ref[4:5] = lines[60:61] + lines[61:62] + b_out_ref[...] * dysum


def results(part, n_taps, gathered, chans, gamma, b_out):
    members, rows, _ = gathered.shape
    return call(
        functools.partial(results_body, part, n_taps),
        [
            jax.ShapeDtypeStruct((members * part, chans), F32),
            jax.ShapeDtypeStruct((members * part, chans), F32),
            jax.ShapeDtypeStruct((rows, n_taps), F32),
            jax.ShapeDtypeStruct((members, part), F32),
            jax.ShapeDtypeStruct((5, rows), F32),
        ],
        [vmem()] * 3,
    )(gathered, gamma[None], b_out[None])


def to_neighbour(blocks):
    half = blocks.shape[0] // 2
    return blocks[:half] + lax.ppermute(blocks[half:].astype(BF), "zp", [(0, 1), (1, 0)]).astype(F32)


def two_parts(value):
    high = lax.reduce_precision(value, 8, 7)
    return high.astype(BF), (value - high).astype(BF)


def to_all(block, axis):
    count = lax.axis_size(axis)
    return lax.all_to_all(jnp.broadcast_to(block[None], (count,) + block.shape), axis, 0, 0, tiled=True)


def exchange(blocks):
    return lax.all_to_all(blocks, CHAN, 0, 0, tiled=True)


def halos(first, last):
    count = lax.axis_size(LAT)
    place = lax.axis_index(LAT)
    even = place % 2 == 0
    pairs = [(i, i + 1) for i in range(0, count, 2)]
    within = lax.ppermute(jnp.where(even, last, first), LAT, pairs + [(j, i) for i, j in pairs])
    pairs = [(i, i + 1) for i in range(1, count - 1, 2)]
    across = lax.ppermute(jnp.where(even, first, last), LAT, pairs + [(j, i) for i, j in pairs])
    return jnp.where(even, across, within), jnp.where(even, within, across)


def along_ring(block, ahead):
    count = lax.axis_size("y")
    return lax.ppermute(block, "y", [((i + ahead) % count, i) for i in range(count)])


def to_ring(blocks):
    count = lax.axis_size("y")
    total = blocks[0].astype(F32)
    for k in range(1, count):
        total = total + lax.ppermute(blocks[k], "y", [(i, (i + k) % count) for i in range(count)]).astype(F32)
    return total


def per_device(
    block_input,
    out_grad,
    metric,
    kernel,
    conv_bias,
    ln_gain,
    ln_bias,
    w_in,
    b_in,
    w_out,
    b_out,
    layer_scale,
):
    cdev, rows, width = block_input.shape
    chans = ln_gain.shape[0]
    tokens = rows * width
    nz, ny = lax.axis_size(ZLO), lax.axis_size("y")
    nchan = nz * ny
    hdev = w_in.shape[0]
    part = hdev // GROUP
    piece = tokens // nchan
    owner = lax.axis_index(CHAN)
    gamma_f = layer_scale.astype(F32)
    gamma_own = lax.dynamic_slice_in_dim(gamma_f, owner * cdev, cdev)

    start = lax.axis_index(("x", "c")) * part
    cut = [lax.dynamic_slice_in_dim(w, start, part) for w in (w_in, w_out, b_in)]
    shards = lax.all_to_all(slices(nz // 2, *cut), "zq", 0, 0, tiled=True)
    beside = lax.ppermute(shards, "zp", [(0, 1), (1, 0)])

    up, down = halos(block_input[:, :3], block_input[:, rows - 3 :])
    blocks = forward(kernel, conv_bias, block_input, up, down, metric, out_grad)
    blocks, shards, beside = lax.optimization_barrier((blocks, shards, beside))

    recv = exchange(blocks)
    shards = jnp.concatenate([shards, beside], 0)
    one, last = along_ring(shards, 1), along_ring(shards, -1)
    recv, one, last = lax.optimization_barrier((recv, one, last))

    pair, nhat, rstd = norm(recv.reshape(chans, 2 * piece), ln_gain, ln_bias, GROUP // 2)
    pair = lax.all_to_all(pair, "x", 0, 0, tiled=True)
    low, high = along_ring(one[: nz // 2], 1), along_ring(last[nz // 2 :], -1)
    pair, low, high = lax.optimization_barrier((pair, low, high))
    wi, wo, bi = weights([shards, one, low, high, last], part, chans)
    other = lax.ppermute(pair, "c", [(0, 1), (1, 0)])

    core = lax.axis_index("c").astype(jnp.int32)[None]
    dn, n, dy, acts = mlp(core, pair, other, wi, wo, bi, gamma_f)
    dn = lax.all_to_all(dn, ("c", "x"), 0, 0, tiled=True)

    place = jnp.stack([lax.axis_index("y"), lax.axis_index("zp")]).astype(jnp.int32)
    dws, gam_part, db_part = grads(part, ny, place, n, dy, acts, wo, gamma_f)
    dws = to_ring(dws.reshape(ny, nz, 2 * part, chans))
    dws = to_neighbour(dws).astype(BF)

    payload = exchange(norm_back(dn, nhat, rstd, ln_gain, gam_part, db_part, nchan))
    payload, dws = lax.optimization_barrier((payload, dws))
    dws = lax.all_to_all(dws, "zq", 0, 0, tiled=True)
    dws = jnp.sum(dws.astype(F32), 0)
    dconv, ends, dh_sums, extra = stencil_cotangent(payload, metric, cdev, width)
    taps = tap_sums(dconv, dh_sums, block_input, up, down, out_grad)
    dup, ddown = halos(ends[0], ends[1])

    small = jnp.concatenate([jnp.sum(taps, 2), extra[:, :8]], 1)
    mine = jnp.concatenate([dws.astype(BF)] + list(two_parts(small)), 1)
    other = lax.ppermute(mine, "zh", [(0, 1), (1, 0)]).astype(F32)
    count = small.shape[1]
    dws = dws + other[:, :chans]
    small = small + other[:, chans : chans + count] + other[:, chans + count :]
    mine = jnp.concatenate([dws.astype(BF)] + list(two_parts(small)), 1)
    mine, dup, ddown = lax.optimization_barrier((mine, dup, ddown))
    grad_input = spread_back(kernel, dconv, dup, ddown, out_grad)
    grad_w_in, grad_w_out, grad_kernel, db, rest = results(
        part, kernel.shape[1], to_all(mine, ("x", "c")), chans, gamma_own, b_out
    )
    return (
        grad_input,
        grad_kernel,
        rest[0],
        rest[1],
        rest[2],
        grad_w_in,
        db.reshape(hdev),
        grad_w_out,
        rest[3],
        rest[4],
    )


def solution(mesh):
    split = Mesh(mesh.devices.reshape(2, 4, 2, 4, 2, 4), ("zh", "x", "c", "zq", "zp", "y"))
    return jax.shard_map(
        per_device,
        mesh=split,
        in_specs=(
            P(CHAN, LAT, None),
            P(CHAN, LAT, None),
            P(LAT),
            P(CHAN, None),
            P(CHAN),
            P(),
            P(),
            P(CHAN, None),
            P(CHAN),
            P(CHAN, None),
            P(CHAN),
            P(),
        ),
        out_specs=(
            P(CHAN, LAT, None),
            P(CHAN, None),
            P(CHAN),
            P(CHAN),
            P(CHAN),
            P(CHAN, None),
            P(CHAN),
            P(CHAN, None),
            P(CHAN),
            P(CHAN),
        ),
        check_vma=False,
    )
```

```python
import functools

import jax
import jax.numpy as jnp
from jax import lax
from jax.experimental import pallas as pl
from jax.experimental.pallas import tpu as pltpu
from jax.sharding import Mesh, PartitionSpec as P

LAT = ("zh", "x", "c")
ZLO = ("zq", "zp")
CHAN = ("zq", "zp", "y")
GROUP = 8
F32 = jnp.float32
BF = jnp.bfloat16
EXT = 16
VMEM_BYTES = 12 * 1024 * 1024
SIDE = 128


def vmem():
    return pl.BlockSpec(memory_space=pltpu.VMEM)


def smem():
    return pl.BlockSpec(memory_space=pltpu.SMEM)


def call(body, out_shape, in_specs, scratch=()):
    many = isinstance(out_shape, (list, tuple))
    return pl.pallas_call(
        body,
        out_shape=out_shape,
        in_specs=in_specs,
        out_specs=[vmem()] * len(out_shape) if many else vmem(),
        scratch_shapes=list(scratch),
        compiler_params=pltpu.CompilerParams(vmem_limit_bytes=VMEM_BYTES),
    )


def fill_rows(x_ref, up_ref, down_ref, ext):
    rows = x_ref.shape[1]
    ext[:, :3, :] = up_ref[...].astype(F32)
    ext[:, 3 : 3 + rows, :] = x_ref[...].astype(F32)
    ext[:, 3 + rows : 6 + rows, :] = down_ref[...].astype(F32)


def row_shifts(ext, c, rows):
    return [ext[c, a : a + rows, :] for a in range(7)]


def along(cells, move):
    width = cells.shape[1]
    if move == 0:
        return cells
    lane = lax.broadcasted_iota(jnp.int32, cells.shape, 1)
    inside = lane < width - move if move > 0 else lane >= -move
    return jnp.where(inside, pltpu.roll(cells, (-move) % width, 1), 0.0)


def stencil(taps_ref, c, shifts, flip):
    total = None
    for b in range(7):
        column = None
        for a in range(7):
            tap = a * 7 + b
            term = taps_ref[c, 48 - tap if flip else tap] * shifts[a]
            column = term if column is None else column + term
        column = along(column, b - 3)
        total = column if total is None else total + column
    return total


def forward_body(taps_ref, x_ref, up_ref, down_ref, metric_ref, dy_ref, out_ref, ext, h_rows, dy_rows):
    cdev, rows, width = x_ref.shape
    fill_rows(x_ref, up_ref, down_ref, ext)
    dy_flat = dy_ref[...].astype(F32).reshape(cdev * rows, width)
    for t in range(width // 128):
        dy_rows[t] = dy_flat[:, t * 128 : t * 128 + 128]
    metric = jnp.broadcast_to(metric_ref[...], (rows, width))

    def channel(c, carry):
        h = taps_ref[c, 49] + metric * stencil(taps_ref, c, row_shifts(ext, c, rows), False)
        for t in range(width // 128):
            h_rows[t, pl.ds(pl.multiple_of(c * rows, rows), rows), :] = h[:, t * 128 : t * 128 + 128]
        return carry

    lax.fori_loop(0, cdev, channel, 0, unroll=8)
    low = lax.broadcasted_iota(jnp.int32, (cdev, 128), 1) < 64
    for r in range(rows):
        for t in range(width // 128):
            h_tile, dy_tile = h_rows[t, pl.ds(r, cdev, rows), :], dy_rows[t, pl.ds(r, cdev, rows), :]
            at = (r * width + t * 128) // 64
            out_ref[at] = jnp.where(low, h_tile, pltpu.roll(dy_tile, 64, 1)).astype(BF)
            out_ref[at + 1] = jnp.where(low, pltpu.roll(h_tile, 64, 1), dy_tile).astype(BF)


def forward(taps, x, up, down, metric, dy):
    cdev, rows, width = x.shape
    return call(
        forward_body,
        jax.ShapeDtypeStruct((rows * width // 64, cdev, 128), BF),
        [smem()] + [vmem()] * 5,
        [
            pltpu.VMEM((cdev, EXT, width), F32),
            pltpu.VMEM((width // 128, cdev * rows, 128), F32),
            pltpu.VMEM((width // 128, cdev * rows, 128), F32),
        ],
    )(taps, x, up, down, metric[:, None], dy)


def norm_body(recv_ref, gain_ref, bias_ref, pair_ref, nhat_ref, rstd_ref):
    chans, lanes = recv_ref.shape
    piece = lanes // 2
    both = recv_ref[...].astype(F32).T
    h = both[:piece]
    mean = jnp.sum(h, 1, keepdims=True) / chans
    var = jnp.sum(h * h, 1, keepdims=True) / chans - mean * mean
    rstd = 1.0 / jnp.sqrt(var + 1e-06)
    nhat = (h - mean) * rstd
    nhat_ref[...] = nhat
    rstd_ref[...] = jnp.broadcast_to(rstd, rstd_ref.shape)
    n = (nhat * gain_ref[...] + bias_ref[...]).astype(BF)
    dy = both[piece:].astype(BF)
    for k in range(pair_ref.shape[0]):
        pair_ref[k, :piece] = n
        pair_ref[k, piece:] = dy


def norm(recv, gain, bias, copies):
    chans, lanes = recv.shape
    return call(
        norm_body,
        [
            jax.ShapeDtypeStruct((copies, lanes, chans), BF),
            jax.ShapeDtypeStruct((lanes // 2, chans), F32),
            jax.ShapeDtypeStruct((lanes // 2, 128), F32),
        ],
        [vmem()] * 3,
    )(recv, gain[None], bias[None])


def norm_back_body(recv_ref, nhat_ref, rstd_ref, gain_ref, gam_ref, db_ref, out_ref, flat):
    piece, chans = nhat_ref.shape
    dn = recv_ref[0].astype(F32)
    for k in range(1, recv_ref.shape[0]):
        dn = dn + recv_ref[k].astype(F32)
    nhat = nhat_ref[...]
    dnhat = dn * gain_ref[...]
    s1 = jnp.sum(dnhat, 1, keepdims=True) / chans
    s2 = jnp.sum(dnhat * nhat, 1, keepdims=True) / chans
    dh = rstd_ref[:, :1] * (dnhat - s1 - nhat * s2)
    flat[:piece] = dh
    flat[piece:] = jnp.zeros((flat.shape[0] - piece, chans), F32)
    sums = (jnp.sum(dn * nhat, 0, keepdims=True), jnp.sum(dn, 0, keepdims=True), gam_ref[...], db_ref[...])
    for k, value in enumerate(sums):
        high = value.astype(BF).astype(F32)
        flat[piece + 2 * k : piece + 2 * k + 1] = high
        flat[piece + 2 * k + 1 : piece + 2 * k + 2] = value - high
    blocks = flat[...].T.reshape(out_ref.shape[0], 24, 128)
    one, two, three = blocks[:, :8], blocks[:, 8:16], blocks[:, 16:]
    lane = lax.broadcasted_iota(jnp.int32, one.shape, 2)
    out_ref[:, :8] = jnp.where(lane < 64, one, pltpu.roll(three, 64, 2)).astype(BF)
    last = jnp.where(lane < 72, one, jnp.where(lane < 80, pltpu.roll(two, 8, 2), pltpu.roll(three, 16, 2)))
    out_ref[:, 8:] = jnp.where(lane < 64, two, last).astype(BF)


def norm_back(recv, nhat, rstd, gain, gam, db, owners):
    piece, chans = nhat.shape
    return call(
        norm_back_body,
        jax.ShapeDtypeStruct((owners, 16, 128), BF),
        [vmem()] * 6,
        [pltpu.VMEM((128, chans), F32)],
    )(recv, nhat, rstd, gain[None], gam, db)


def dconv_body(recv_ref, metric_ref, dconv_ref, ends_ref, sums_ref, extra_ref, dh_rows):
    cdev, rows, width = dconv_ref.shape
    low16 = lax.broadcasted_iota(jnp.int32, (16, 128), 1) < 64
    low8 = lax.broadcasted_iota(jnp.int32, (8, 128), 1) < 64
    extra = jnp.zeros((8, 128), F32)
    for r in range(rows):
        for t in range(width // 128):
            at = (r * width + t * 128) // 64
            first, second = recv_ref[at].astype(F32), recv_ref[at + 1].astype(F32)
            dh_rows[t, pl.ds(r, 16, rows), :] = jnp.where(low16, first, pltpu.roll(second, 64, 1))
            dh_rows[t, pl.ds(16 * rows + r, 8, rows), :] = jnp.where(low8, pltpu.roll(first[:8], 64, 1), second[:8])
            extra = extra + first[8:] + second[8:]
    for g in range(3):
        extra_ref[8 * g : 8 * g + 8] = pltpu.roll(extra, 64 - 8 * g, 1)
    metric = jnp.broadcast_to(metric_ref[...], (rows, 128))
    for c in range(cdev):
        for t in range(width // 128):
            dh = dh_rows[t, c * rows : (c + 1) * rows, :]
            dconv = metric * dh
            lanes = slice(t * 128, t * 128 + 128)
            dconv_ref[c, :, lanes] = dconv
            ends_ref[0, c, :, lanes] = dconv[:3].astype(BF)
            ends_ref[1, c, :, lanes] = dconv[rows - 3 :].astype(BF)
            sums_ref[c] = dh if t == 0 else sums_ref[c] + dh


def stencil_cotangent(recv, metric, cdev, width):
    rows = metric.shape[0]
    return call(
        dconv_body,
        [
            jax.ShapeDtypeStruct((cdev, rows, width), F32),
            jax.ShapeDtypeStruct((2, cdev, 3, width), BF),
            jax.ShapeDtypeStruct((cdev, rows, 128), F32),
            jax.ShapeDtypeStruct((cdev, 128), F32),
        ],
        [vmem()] * 2,
        [pltpu.VMEM((width // 128, cdev * rows, 128), F32)],
    )(recv, metric[:, None])


def taps_body(dconv_ref, dh_sums_ref, x_ref, up_ref, down_ref, dy_ref, sums_ref, ext, prods):
    cdev, rows, width = x_ref.shape
    fill_rows(x_ref, up_ref, down_ref, ext)

    def channel(c, carry):
        dconv = dconv_ref[c]
        shifts = row_shifts(ext, c, rows)
        for b in range(7):
            moved = along(dconv, 3 - b)
            for a in range(7):
                product = shifts[a] * moved
                prods[(a * 7 + b) * 8 : (a * 7 + b) * 8 + 8, :] = product[:, :128] + product[:, 128:]
        dy = dy_ref[c].astype(F32)
        prods[392:400, :] = dh_sums_ref[c]
        prods[400:408, :] = dy[:, :128] + dy[:, 128:]
        total = prods[pl.ds(0, 56, 8), :]
        for i in range(1, 8):
            total = total + prods[pl.ds(i, 56, 8), :]
        sums_ref[c] = total
        return carry

    prods[408:, :] = jnp.zeros((prods.shape[0] - 408, 128), F32)
    lax.fori_loop(0, cdev, channel, 0, unroll=8)


def tap_sums(dconv, dh_sums, x, up, down, dy):
    cdev, rows, width = x.shape
    return call(
        taps_body,
        jax.ShapeDtypeStruct((cdev, 56, 128), F32),
        [vmem()] * 6,
        [pltpu.VMEM((cdev, EXT, width), F32), pltpu.VMEM((448, 128), F32)],
    )(dconv, dh_sums, x, up, down, dy)


def spread_body(taps_ref, x_ref, up_ref, down_ref, dy_ref, out_ref, ext):
    cdev, rows, width = x_ref.shape
    fill_rows(x_ref, up_ref, down_ref, ext)

    def channel(c, carry):
        out_ref[c] = dy_ref[c].astype(F32) + stencil(taps_ref, c, row_shifts(ext, c, rows), True)
        return carry

    lax.fori_loop(0, cdev, channel, 0, unroll=8)


def spread_back(taps, dconv, up, down, dy):
    cdev, rows, width = dconv.shape
    return call(
        spread_body,
        jax.ShapeDtypeStruct((cdev, rows, width), F32),
        [smem()] + [vmem()] * 4,
        [pltpu.VMEM((cdev, EXT, width), F32)],
    )(taps, dconv, up, down, dy)


def picks(blocks, part):
    shape = (blocks * 2 * part, blocks * part)
    row = lax.broadcasted_iota(jnp.int32, shape, 0)
    place = lax.broadcasted_iota(jnp.int32, shape, 1)
    block = jnp.floor((row.astype(F32) + 0.5) * (0.5 / part)).astype(jnp.int32)
    inside = row - block * 2 * part
    first = (inside < part) & (place == block * part + inside)
    second = (inside >= part) & (place == block * part + inside - part)
    return [jnp.where(m, 1.0, 0.0).astype(BF) for m in (first, second)]


def dot(a, b, a_dim, b_dim):
    return lax.dot_general(a, b, (((a_dim,), (b_dim,)), ((), ())), preferred_element_type=F32)


def weights_body(part, own_ref, one_ref, low_ref, high_ref, last_ref, wi_ref, wo_ref, bi_ref, rows):
    blocks = 0
    for ref in (own_ref, one_ref, low_ref, high_ref, last_ref):
        for k in range(ref.shape[0]):
            at = blocks * 2 * part
            rows[at : at + 2 * part] = ref[k].astype(F32)
            blocks += 1
    chans = wi_ref.shape[1]
    flat = rows[...].astype(BF)
    first, second = picks(blocks, part)
    wi_ref[...] = dot(first, flat[:, :chans], 0, 0).astype(BF)
    wo_ref[...] = dot(second, flat[:, :chans], 0, 0).astype(BF)
    both = dot(flat[:, chans:], first, 0, 0)
    bi_ref[...] = both[:1] + both[1:2]


def weights(parts, part, chans):
    blocks = sum(p.shape[0] for p in parts)
    return call(
        functools.partial(weights_body, part),
        [
            jax.ShapeDtypeStruct((blocks * part, chans), BF),
            jax.ShapeDtypeStruct((blocks * part, chans), BF),
            jax.ShapeDtypeStruct((1, blocks * part), F32),
        ],
        [vmem()] * len(parts),
        [pltpu.VMEM((blocks * 2 * part, parts[0].shape[2]), F32)],
    )(*parts)


def mlp_body(core_ref, own_ref, other_ref, wi_ref, wo_ref, bi_ref, gamma_ref, dn_ref, n_ref, dy_ref, acts_ref):
    members, lanes, _ = own_ref.shape
    piece = lanes // 2
    for at, ref in ((0, own_ref), (members, other_ref)):
        for k in range(members):
            n_ref[(at + k) * piece : (at + k + 1) * piece] = ref[k, :piece]
            dy_ref[(at + k) * piece : (at + k + 1) * piece] = ref[k, piece:]
    pre = dot(n_ref[...], wi_ref[...], 1, 1) + bi_ref[...]
    cdf = 0.5 + 0.5 * lax.erf(pre * (0.5**0.5))
    hid = pre.shape[1]
    acts_ref[:, :hid] = (pre * cdf).astype(BF)
    slope = cdf + pre * (jnp.exp(-0.5 * pre * pre) * (0.5 / 3.141592653589793) ** 0.5)
    dmlp = (gamma_ref[...] * dy_ref[...].astype(F32)).astype(BF)
    dpre = (slope * dot(dmlp, wo_ref[...], 1, 1)).astype(BF)
    acts_ref[:, hid:] = dpre
    dn = dot(dpre, wi_ref[...], 1, 0).astype(BF)
    core = core_ref[0]
    for k in range(members):
        dn_ref[core * members + k] = dn[k * piece : (k + 1) * piece]
        dn_ref[(1 - core) * members + k] = dn[(members + k) * piece : (members + k + 1) * piece]


def mlp(core, own, other, wi, wo, bi, gamma):
    members, lanes, chans = own.shape
    toks, hid = members * lanes, wi.shape[0]
    return call(
        mlp_body,
        [
            jax.ShapeDtypeStruct((2 * members, lanes // 2, chans), BF),
            jax.ShapeDtypeStruct((toks, chans), BF),
            jax.ShapeDtypeStruct((toks, chans), BF),
            jax.ShapeDtypeStruct((toks, 2 * hid), BF),
        ],
        [smem()] + [vmem()] * 6,
    )(core, own, other, wi, wo, bi, gamma[None])


def grads_body(part, ny, place_ref, n_ref, dy_ref, acts_ref, wo_ref, gamma_ref, out_ref, gam_ref, db_ref):
    toks = n_ref.shape[0]
    hid = acts_ref.shape[1] // 2
    first, second = picks(hid // part, part)
    dpre = acts_ref[:, hid:]
    dw_in = dot(dpre, n_ref[...], 0, 0).astype(BF)
    proj = dot(acts_ref[:, :hid], dy_ref[...], 0, 0)
    gam_ref[...] = jnp.sum(wo_ref[...].astype(F32) * proj, 0, keepdims=True)
    dw_out = (proj * gamma_ref[...]).astype(BF)
    out_ref[...] = (dot(first, dw_in, 1, 0) + dot(second, dw_out, 1, 0)).astype(BF)
    nz = hid // part // ny
    lane = lax.broadcasted_iota(jnp.int32, (db_ref.shape[1], hid), 0)
    place = lax.broadcasted_iota(jnp.int32, (1, hid), 1)
    block = jnp.floor((place.astype(F32) + 0.5) * (1.0 / part)).astype(jnp.int32)
    ring = jnp.floor((block.astype(F32) + 0.5) * (1.0 / nz)).astype(jnp.int32)
    ahead = ring + place_ref[0]
    along_z = block - ring * nz
    far = along_z >= nz // 2
    zq = jnp.where(far, along_z - nz // 2, along_z)
    zp = jnp.where(far, 1 - place_ref[1], place_ref[1])
    owner = (zq * 2 + zp) * ny + jnp.where(ahead >= ny, ahead - ny, ahead)
    spot = jnp.where(lane == owner * 2 * part + place - block * part, 1.0, 0.0).astype(BF)
    db = dot(jnp.ones((16, toks), BF), dpre, 1, 0).astype(BF)
    db_ref[...] = dot(db, spot, 1, 1)[:1]


def grads(part, ny, place, n, dy, acts, wo, gamma):
    chans = n.shape[1]
    hid = acts.shape[1] // 2
    return call(
        functools.partial(grads_body, part, ny),
        [
            jax.ShapeDtypeStruct((2 * hid, chans), BF),
            jax.ShapeDtypeStruct((1, chans), F32),
            jax.ShapeDtypeStruct((1, 2 * hid), F32),
        ],
        [smem()] + [vmem()] * 5,
    )(place, n, dy, acts, wo, gamma[None])


def slices_body(w_in_ref, w_out_ref, b_ref, out_ref):
    part, chans = w_in_ref.shape
    row = lax.broadcasted_iota(jnp.int32, (2 * part, part), 0)
    place = lax.broadcasted_iota(jnp.int32, (2 * part, part), 1)
    first = jnp.where(row == place, 1.0, 0.0).astype(BF)
    second = jnp.where(row == place + part, 1.0, 0.0).astype(BF)
    rows = (dot(first, w_in_ref[...], 1, 0) + dot(second, w_out_ref[...], 1, 0)).astype(BF)
    bias = jnp.broadcast_to(b_ref[...], (SIDE, part))
    high = bias.astype(BF).astype(F32)
    line = lax.broadcasted_iota(jnp.int32, (SIDE, part), 0)
    both = jnp.where(line == 0, high, jnp.where(line == 1, bias - high, 0.0)).astype(BF)
    side = dot(first, both, 1, 1).astype(BF)
    for k in range(out_ref.shape[0]):
        out_ref[k, :, :chans] = rows
        out_ref[k, :, chans:] = side


def slices(copies, w_in, w_out, b_in):
    part, chans = w_in.shape
    return call(
        slices_body,
        jax.ShapeDtypeStruct((copies, 2 * part, chans + SIDE), BF),
        [vmem()] * 3,
    )(w_in, w_out, b_in[None])


def results_body(part, n_taps, gathered_ref, gamma_ref, b_out_ref, dw_in_ref, dw_out_ref, taps_ref, db_ref, *rest):
    chans = dw_in_ref.shape[1]
    lane = lax.broadcasted_iota(jnp.int32, (1, 128), 1)
    total, db = None, None
    for k in range(gathered_ref.shape[0]):
        block = gathered_ref[k].astype(F32)
        dw_in_ref[k * part : (k + 1) * part] = block[:part, :chans]
        dw_out_ref[k * part : (k + 1) * part] = block[part:, :chans]
        side = block[:, chans:]
        side = side + pltpu.roll(side, 64, 1)
        line = side.T
        line = line[62:63] + line[63:64]
        line = jnp.concatenate([line, jnp.zeros((1, 128 - line.shape[1]), F32)], 1)
        line = jnp.where(lane < part, line, 0.0)
        line = line if k == 0 else pltpu.roll(line, k * part, 1)
        db = line if db is None else db + line
        total = side if total is None else total + side
    db_ref[...] = db[0, : db_ref.shape[0]]
    taps_ref[...] = total[:, :n_taps]
    lines = total.T
    dysum = lines[n_taps + 1]
    rest[0][...] = lines[n_taps]
    rest[1][...] = lines[56] + lines[57]
    rest[2][...] = lines[58] + lines[59]
    rest[3][...] = gamma_ref[...] * dysum
    rest[4][...] = lines[60] + lines[61] + b_out_ref[...] * dysum


def results(part, n_taps, gathered, chans, gamma, b_out):
    members, rows, _ = gathered.shape
    return call(
        functools.partial(results_body, part, n_taps),
        [
            jax.ShapeDtypeStruct((members * part, chans), F32),
            jax.ShapeDtypeStruct((members * part, chans), F32),
            jax.ShapeDtypeStruct((rows, n_taps), F32),
            jax.ShapeDtypeStruct((members * part,), F32),
        ]
        + [jax.ShapeDtypeStruct((rows,), F32)] * 5,
        [vmem()] * 3,
    )(gathered, gamma, b_out)


def to_neighbour(blocks):
    half = blocks.shape[0] // 2
    return blocks[:half] + lax.ppermute(blocks[half:].astype(BF), "zp", [(0, 1), (1, 0)]).astype(F32)


def two_parts(value):
    high = lax.reduce_precision(value, 8, 7)
    return high.astype(BF), (value - high).astype(BF)


def to_all(block, axis):
    count = lax.axis_size(axis)
    return lax.all_to_all(jnp.broadcast_to(block[None], (count,) + block.shape), axis, 0, 0, tiled=True)


def exchange(blocks):
    return lax.all_to_all(blocks, CHAN, 0, 0, tiled=True)


def halos(first, last):
    count = lax.axis_size(LAT)
    place = lax.axis_index(LAT)
    even = place % 2 == 0
    pairs = [(i, i + 1) for i in range(0, count, 2)]
    within = lax.ppermute(jnp.where(even, last, first), LAT, pairs + [(j, i) for i, j in pairs])
    pairs = [(i, i + 1) for i in range(1, count - 1, 2)]
    across = lax.ppermute(jnp.where(even, first, last), LAT, pairs + [(j, i) for i, j in pairs])
    return jnp.where(even, across, within), jnp.where(even, within, across)


def along_ring(block, ahead):
    count = lax.axis_size("y")
    return lax.ppermute(block, "y", [((i + ahead) % count, i) for i in range(count)])


def to_ring(blocks):
    count = lax.axis_size("y")
    total = blocks[0].astype(F32)
    for k in range(1, count):
        total = total + lax.ppermute(blocks[k], "y", [(i, (i + k) % count) for i in range(count)]).astype(F32)
    return total


def per_device(
    block_input,
    out_grad,
    metric,
    kernel,
    conv_bias,
    ln_gain,
    ln_bias,
    w_in,
    b_in,
    w_out,
    b_out,
    layer_scale,
):
    cdev, rows, width = block_input.shape
    chans = ln_gain.shape[0]
    tokens = rows * width
    nz, ny = lax.axis_size(ZLO), lax.axis_size("y")
    nchan = nz * ny
    hdev = w_in.shape[0]
    part = hdev // GROUP
    piece = tokens // nchan
    owner = lax.axis_index(CHAN)
    gamma_f = layer_scale.astype(F32)
    gamma_own = lax.dynamic_slice_in_dim(gamma_f, owner * cdev, cdev)

    start = lax.axis_index(("x", "c")) * part
    cut = [lax.dynamic_slice_in_dim(w, start, part) for w in (w_in, w_out, b_in)]
    shards = lax.all_to_all(slices(nz // 2, *cut), "zq", 0, 0, tiled=True)
    beside = lax.ppermute(shards, "zp", [(0, 1), (1, 0)])

    up, down = halos(block_input[:, :3], block_input[:, rows - 3 :])
    taps_bias = jnp.concatenate([kernel, conv_bias[:, None]], 1)
    blocks = forward(taps_bias, block_input, up, down, metric, out_grad)
    blocks, shards, beside = lax.optimization_barrier((blocks, shards, beside))

    recv = exchange(blocks)
    shards = jnp.concatenate([shards, beside], 0)
    one, last = along_ring(shards, 1), along_ring(shards, -1)
    recv, one, last = lax.optimization_barrier((recv, one, last))

    pair, nhat, rstd = norm(recv.reshape(chans, 2 * piece), ln_gain, ln_bias, GROUP // 2)
    pair = lax.all_to_all(pair, "x", 0, 0, tiled=True)
    low, high = along_ring(one[: nz // 2], 1), along_ring(last[nz // 2 :], -1)
    pair, low, high = lax.optimization_barrier((pair, low, high))
    wi, wo, bi = weights([shards, one, low, high, last], part, chans)
    other = lax.ppermute(pair, "c", [(0, 1), (1, 0)])

    core = lax.axis_index("c").astype(jnp.int32)[None]
    dn, n, dy, acts = mlp(core, pair, other, wi, wo, bi, gamma_f)
    dn = lax.all_to_all(dn, ("c", "x"), 0, 0, tiled=True)

    place = jnp.stack([lax.axis_index("y"), lax.axis_index("zp")]).astype(jnp.int32)
    dws, gam_part, db_part = grads(part, ny, place, n, dy, acts, wo, gamma_f)
    dws = to_ring(dws.reshape(ny, nz, 2 * part, chans))
    dws = to_neighbour(dws).astype(BF)

    payload = exchange(norm_back(dn, nhat, rstd, ln_gain, gam_part, db_part, nchan))
    payload, dws = lax.optimization_barrier((payload, dws))
    dws = lax.all_to_all(dws, "zq", 0, 0, tiled=True)
    dws = jnp.sum(dws.astype(F32), 0)
    dconv, ends, dh_sums, extra = stencil_cotangent(payload, metric, cdev, width)
    taps = tap_sums(dconv, dh_sums, block_input, up, down, out_grad)
    dup, ddown = halos(ends[0], ends[1])

    small = jnp.concatenate([jnp.sum(taps, 2), extra[:, :8]], 1)
    mine = jnp.concatenate([dws.astype(BF)] + list(two_parts(small)), 1)
    other = lax.ppermute(mine, "zh", [(0, 1), (1, 0)]).astype(F32)
    count = small.shape[1]
    dws = dws + other[:, :chans]
    small = small + other[:, chans : chans + count] + other[:, chans + count :]
    mine = jnp.concatenate([dws.astype(BF)] + list(two_parts(small)), 1)
    mine, dup, ddown = lax.optimization_barrier((mine, dup, ddown))
    grad_input = spread_back(taps_bias, dconv, dup, ddown, out_grad)
    grad_w_in, grad_w_out, grad_kernel, db, *rest = results(
        part, kernel.shape[1], to_all(mine, ("x", "c")), chans, gamma_own, b_out
    )
    return (
        grad_input,
        grad_kernel,
        rest[0],
        rest[1],
        rest[2],
        grad_w_in,
        db,
        grad_w_out,
        rest[3],
        rest[4],
    )


def solution(mesh):
    split = Mesh(mesh.devices.reshape(2, 4, 2, 4, 2, 4), ("zh", "x", "c", "zq", "zp", "y"))
    return jax.shard_map(
        per_device,
        mesh=split,
        in_specs=(
            P(CHAN, LAT, None),
            P(CHAN, LAT, None),
            P(LAT),
            P(CHAN, None),
            P(CHAN),
            P(),
            P(),
            P(CHAN, None),
            P(CHAN),
            P(CHAN, None),
            P(CHAN),
            P(),
        ),
        out_specs=(
            P(CHAN, LAT, None),
            P(CHAN, None),
            P(CHAN),
            P(CHAN),
            P(CHAN),
            P(CHAN, None),
            P(CHAN),
            P(CHAN, None),
            P(CHAN),
            P(CHAN),
        ),
        check_vma=False,
    )
```

```python
import functools

import jax
import jax.numpy as jnp
from jax import lax
from jax.experimental import pallas as pl
from jax.experimental.pallas import tpu as pltpu
from jax.sharding import Mesh, PartitionSpec as P

LAT = ("zh", "x", "c")
ZLO = ("zq", "zp")
CHAN = ("zq", "zp", "y")
GROUP = 8
F32 = jnp.float32
BF = jnp.bfloat16
EXT = 16
VMEM_BYTES = 12 * 1024 * 1024
SIDE = 128


def vmem():
    return pl.BlockSpec(memory_space=pltpu.VMEM)


def smem():
    return pl.BlockSpec(memory_space=pltpu.SMEM)


def call(body, out_shape, in_specs, scratch=()):
    many = isinstance(out_shape, (list, tuple))
    return pl.pallas_call(
        body,
        out_shape=out_shape,
        in_specs=in_specs,
        out_specs=[vmem()] * len(out_shape) if many else vmem(),
        scratch_shapes=list(scratch),
        compiler_params=pltpu.CompilerParams(vmem_limit_bytes=VMEM_BYTES),
    )


def fill_rows(x_ref, up_ref, down_ref, ext):
    rows = x_ref.shape[1]
    ext[:, :3, :] = up_ref[...].astype(F32)
    ext[:, 3 : 3 + rows, :] = x_ref[...].astype(F32)
    ext[:, 3 + rows : 6 + rows, :] = down_ref[...].astype(F32)


def row_shifts(ext, c, rows):
    return [ext[c, a : a + rows, :] for a in range(7)]


def along(cells, move):
    width = cells.shape[1]
    if move == 0:
        return cells
    lane = lax.broadcasted_iota(jnp.int32, cells.shape, 1)
    inside = lane < width - move if move > 0 else lane >= -move
    return jnp.where(inside, pltpu.roll(cells, (-move) % width, 1), 0.0)


def stencil(taps_ref, c, shifts, flip):
    total = None
    for b in range(7):
        column = None
        for a in range(7):
            tap = a * 7 + b
            term = taps_ref[c, 48 - tap if flip else tap] * shifts[a]
            column = term if column is None else column + term
        column = along(column, b - 3)
        total = column if total is None else total + column
    return total


def forward_body(taps_ref, x_ref, up_ref, down_ref, metric_ref, dy_ref, out_ref, ext, h_rows, dy_rows):
    cdev, rows, width = x_ref.shape
    fill_rows(x_ref, up_ref, down_ref, ext)
    dy_flat = dy_ref[...].astype(F32).reshape(cdev * rows, width)
    for t in range(width // 128):
        dy_rows[t] = dy_flat[:, t * 128 : t * 128 + 128]
    metric = jnp.broadcast_to(metric_ref[...], (rows, width))

    def channel(c, carry):
        h = taps_ref[c, 49] + metric * stencil(taps_ref, c, row_shifts(ext, c, rows), False)
        for t in range(width // 128):
            h_rows[t, pl.ds(pl.multiple_of(c * rows, rows), rows), :] = h[:, t * 128 : t * 128 + 128]
        return carry

    lax.fori_loop(0, cdev, channel, 0, unroll=8)
    low = lax.broadcasted_iota(jnp.int32, (cdev, 128), 1) < 64
    for r in range(rows):
        for t in range(width // 128):
            h_tile, dy_tile = h_rows[t, pl.ds(r, cdev, rows), :], dy_rows[t, pl.ds(r, cdev, rows), :]
            at = (r * width + t * 128) // 64
            out_ref[at] = jnp.where(low, h_tile, pltpu.roll(dy_tile, 64, 1)).astype(BF)
            out_ref[at + 1] = jnp.where(low, pltpu.roll(h_tile, 64, 1), dy_tile).astype(BF)


def forward(taps, x, up, down, metric, dy):
    cdev, rows, width = x.shape
    return call(
        forward_body,
        jax.ShapeDtypeStruct((rows * width // 64, cdev, 128), BF),
        [smem()] + [vmem()] * 5,
        [
            pltpu.VMEM((cdev, EXT, width), F32),
            pltpu.VMEM((width // 128, cdev * rows, 128), F32),
            pltpu.VMEM((width // 128, cdev * rows, 128), F32),
        ],
    )(taps, x, up, down, metric[:, None], dy)


def norm_body(recv_ref, gain_ref, bias_ref, pair_ref, nhat_ref, rstd_ref):
    chans, lanes = recv_ref.shape
    piece = lanes // 2
    both = recv_ref[...].astype(F32).T
    h = both[:piece]
    mean = jnp.sum(h, 1, keepdims=True) / chans
    var = jnp.sum(h * h, 1, keepdims=True) / chans - mean * mean
    rstd = 1.0 / jnp.sqrt(var + 1e-06)
    nhat = (h - mean) * rstd
    nhat_ref[...] = nhat
    rstd_ref[...] = jnp.broadcast_to(rstd, rstd_ref.shape)
    n = (nhat * gain_ref[...] + bias_ref[...]).astype(BF)
    dy = both[piece:].astype(BF)
    for k in range(pair_ref.shape[0]):
        pair_ref[k, :piece] = n
        pair_ref[k, piece:] = dy


def norm(recv, gain, bias, copies):
    chans, lanes = recv.shape
    return call(
        norm_body,
        [
            jax.ShapeDtypeStruct((copies, lanes, chans), BF),
            jax.ShapeDtypeStruct((lanes // 2, chans), F32),
            jax.ShapeDtypeStruct((lanes // 2, 128), F32),
        ],
        [vmem()] * 3,
    )(recv, gain[None], bias[None])


def norm_back_body(recv_ref, nhat_ref, rstd_ref, gain_ref, gam_ref, db_ref, out_ref, flat):
    piece, chans = nhat_ref.shape
    dn = recv_ref[0].astype(F32)
    for k in range(1, recv_ref.shape[0]):
        dn = dn + recv_ref[k].astype(F32)
    nhat = nhat_ref[...]
    dnhat = dn * gain_ref[...]
    s1 = jnp.sum(dnhat, 1, keepdims=True) / chans
    s2 = jnp.sum(dnhat * nhat, 1, keepdims=True) / chans
    dh = rstd_ref[:, :1] * (dnhat - s1 - nhat * s2)
    flat[:piece] = dh
    flat[piece:] = jnp.zeros((flat.shape[0] - piece, chans), F32)
    sums = (jnp.sum(dn * nhat, 0, keepdims=True), jnp.sum(dn, 0, keepdims=True), gam_ref[...], db_ref[...])
    for k, value in enumerate(sums):
        high = value.astype(BF).astype(F32)
        flat[piece + 2 * k : piece + 2 * k + 1] = high
        flat[piece + 2 * k + 1 : piece + 2 * k + 2] = value - high
    blocks = flat[...].T.reshape(out_ref.shape[0], 24, 128)
    one, two, three = blocks[:, :8], blocks[:, 8:16], blocks[:, 16:]
    lane = lax.broadcasted_iota(jnp.int32, one.shape, 2)
    out_ref[:, :8] = jnp.where(lane < 64, one, pltpu.roll(three, 64, 2)).astype(BF)
    last = jnp.where(lane < 72, one, jnp.where(lane < 80, pltpu.roll(two, 8, 2), pltpu.roll(three, 16, 2)))
    out_ref[:, 8:] = jnp.where(lane < 64, two, last).astype(BF)


def norm_back(recv, nhat, rstd, gain, gam, db, owners):
    piece, chans = nhat.shape
    return call(
        norm_back_body,
        jax.ShapeDtypeStruct((owners, 16, 128), BF),
        [vmem()] * 6,
        [pltpu.VMEM((128, chans), F32)],
    )(recv, nhat, rstd, gain[None], gam, db)


def dconv_body(recv_ref, metric_ref, dconv_ref, ends_ref, sums_ref, extra_ref, dh_rows):
    cdev, rows, width = dconv_ref.shape
    low16 = lax.broadcasted_iota(jnp.int32, (16, 128), 1) < 64
    low8 = lax.broadcasted_iota(jnp.int32, (8, 128), 1) < 64
    extra = jnp.zeros((8, 128), F32)
    for r in range(rows):
        for t in range(width // 128):
            at = (r * width + t * 128) // 64
            first, second = recv_ref[at].astype(F32), recv_ref[at + 1].astype(F32)
            dh_rows[t, pl.ds(r, 16, rows), :] = jnp.where(low16, first, pltpu.roll(second, 64, 1))
            dh_rows[t, pl.ds(16 * rows + r, 8, rows), :] = jnp.where(low8, pltpu.roll(first[:8], 64, 1), second[:8])
            extra = extra + first[8:] + second[8:]
    for g in range(3):
        extra_ref[8 * g : 8 * g + 8] = pltpu.roll(extra, 64 - 8 * g, 1)
    metric = jnp.broadcast_to(metric_ref[...], (rows, 128))
    for c in range(cdev):
        for t in range(width // 128):
            dh = dh_rows[t, c * rows : (c + 1) * rows, :]
            dconv = metric * dh
            lanes = slice(t * 128, t * 128 + 128)
            dconv_ref[c, :, lanes] = dconv
            ends_ref[0, c, :, lanes] = dconv[:3].astype(BF)
            ends_ref[1, c, :, lanes] = dconv[rows - 3 :].astype(BF)
            sums_ref[c] = dh if t == 0 else sums_ref[c] + dh


def stencil_cotangent(recv, metric, cdev, width):
    rows = metric.shape[0]
    return call(
        dconv_body,
        [
            jax.ShapeDtypeStruct((cdev, rows, width), F32),
            jax.ShapeDtypeStruct((2, cdev, 3, width), BF),
            jax.ShapeDtypeStruct((cdev, rows, 128), F32),
            jax.ShapeDtypeStruct((cdev, 128), F32),
        ],
        [vmem()] * 2,
        [pltpu.VMEM((width // 128, cdev * rows, 128), F32)],
    )(recv, metric[:, None])


def taps_body(dconv_ref, dh_sums_ref, x_ref, up_ref, down_ref, dy_ref, sums_ref, ext, prods):
    cdev, rows, width = x_ref.shape
    fill_rows(x_ref, up_ref, down_ref, ext)

    def channel(c, carry):
        dconv = dconv_ref[c]
        shifts = row_shifts(ext, c, rows)
        for b in range(7):
            moved = along(dconv, 3 - b)
            for a in range(7):
                product = shifts[a] * moved
                prods[(a * 7 + b) * 8 : (a * 7 + b) * 8 + 8, :] = product[:, :128] + product[:, 128:]
        dy = dy_ref[c].astype(F32)
        prods[392:400, :] = dh_sums_ref[c]
        prods[400:408, :] = dy[:, :128] + dy[:, 128:]
        total = prods[pl.ds(0, 56, 8), :]
        for i in range(1, 8):
            total = total + prods[pl.ds(i, 56, 8), :]
        sums_ref[c] = total
        return carry

    prods[408:, :] = jnp.zeros((prods.shape[0] - 408, 128), F32)
    lax.fori_loop(0, cdev, channel, 0, unroll=8)


def tap_sums(dconv, dh_sums, x, up, down, dy):
    cdev, rows, width = x.shape
    return call(
        taps_body,
        jax.ShapeDtypeStruct((cdev, 56, 128), F32),
        [vmem()] * 6,
        [pltpu.VMEM((cdev, EXT, width), F32), pltpu.VMEM((448, 128), F32)],
    )(dconv, dh_sums, x, up, down, dy)


def spread_body(taps_ref, x_ref, up_ref, down_ref, dy_ref, out_ref, ext):
    cdev, rows, width = x_ref.shape
    fill_rows(x_ref, up_ref, down_ref, ext)

    def channel(c, carry):
        out_ref[c] = dy_ref[c].astype(F32) + stencil(taps_ref, c, row_shifts(ext, c, rows), True)
        return carry

    lax.fori_loop(0, cdev, channel, 0, unroll=8)


def spread_back(taps, dconv, up, down, dy):
    cdev, rows, width = dconv.shape
    return call(
        spread_body,
        jax.ShapeDtypeStruct((cdev, rows, width), F32),
        [smem()] + [vmem()] * 4,
        [pltpu.VMEM((cdev, EXT, width), F32)],
    )(taps, dconv, up, down, dy)


def picks(blocks, part):
    shape = (blocks * 2 * part, blocks * part)
    row = lax.broadcasted_iota(jnp.int32, shape, 0)
    place = lax.broadcasted_iota(jnp.int32, shape, 1)
    block = jnp.floor((row.astype(F32) + 0.5) * (0.5 / part)).astype(jnp.int32)
    inside = row - block * 2 * part
    first = (inside < part) & (place == block * part + inside)
    second = (inside >= part) & (place == block * part + inside - part)
    return [jnp.where(m, 1.0, 0.0).astype(BF) for m in (first, second)]


def dot(a, b, a_dim, b_dim):
    return lax.dot_general(a, b, (((a_dim,), (b_dim,)), ((), ())), preferred_element_type=F32)


def weights_body(part, own_ref, one_ref, low_ref, high_ref, last_ref, wi_ref, wo_ref, bi_ref, rows):
    blocks = 0
    for ref in (own_ref, one_ref, low_ref, high_ref, last_ref):
        for k in range(ref.shape[0]):
            at = blocks * 2 * part
            rows[at : at + 2 * part] = ref[k].astype(F32)
            blocks += 1
    chans = wi_ref.shape[1]
    flat = rows[...].astype(BF)
    first, second = picks(blocks, part)
    wi_ref[...] = dot(first, flat[:, :chans], 0, 0).astype(BF)
    wo_ref[...] = dot(second, flat[:, :chans], 0, 0).astype(BF)
    both = dot(flat[:, chans:], first, 0, 0)
    bi_ref[...] = both[:1] + both[1:2]


def weights(parts, part, chans):
    blocks = sum(p.shape[0] for p in parts)
    return call(
        functools.partial(weights_body, part),
        [
            jax.ShapeDtypeStruct((blocks * part, chans), BF),
            jax.ShapeDtypeStruct((blocks * part, chans), BF),
            jax.ShapeDtypeStruct((1, blocks * part), F32),
        ],
        [vmem()] * len(parts),
        [pltpu.VMEM((blocks * 2 * part, parts[0].shape[2]), F32)],
    )(*parts)


def mlp_body(core_ref, own_ref, other_ref, wi_ref, wo_ref, bi_ref, gamma_ref, dn_ref, n_ref, dy_ref, acts_ref):
    members, lanes, _ = own_ref.shape
    piece = lanes // 2
    for at, ref in ((0, own_ref), (members, other_ref)):
        for k in range(members):
            n_ref[(at + k) * piece : (at + k + 1) * piece] = ref[k, :piece]
            dy_ref[(at + k) * piece : (at + k + 1) * piece] = ref[k, piece:]
    pre = dot(n_ref[...], wi_ref[...], 1, 1) + bi_ref[...]
    cdf = 0.5 + 0.5 * lax.erf(pre * (0.5**0.5))
    hid = pre.shape[1]
    acts_ref[:, :hid] = (pre * cdf).astype(BF)
    slope = cdf + pre * (jnp.exp(-0.5 * pre * pre) * (0.5 / 3.141592653589793) ** 0.5)
    dmlp = (gamma_ref[...] * dy_ref[...].astype(F32)).astype(BF)
    dpre = (slope * dot(dmlp, wo_ref[...], 1, 1)).astype(BF)
    acts_ref[:, hid:] = dpre
    dn = dot(dpre, wi_ref[...], 1, 0).astype(BF)
    core = core_ref[0]
    for k in range(members):
        dn_ref[core * members + k] = dn[k * piece : (k + 1) * piece]
        dn_ref[(1 - core) * members + k] = dn[(members + k) * piece : (members + k + 1) * piece]


def mlp(core, own, other, wi, wo, bi, gamma):
    members, lanes, chans = own.shape
    toks, hid = members * lanes, wi.shape[0]
    return call(
        mlp_body,
        [
            jax.ShapeDtypeStruct((2 * members, lanes // 2, chans), BF),
            jax.ShapeDtypeStruct((toks, chans), BF),
            jax.ShapeDtypeStruct((toks, chans), BF),
            jax.ShapeDtypeStruct((toks, 2 * hid), BF),
        ],
        [smem()] + [vmem()] * 6,
    )(core, own, other, wi, wo, bi, gamma[None])


def grads_body(part, ny, place_ref, n_ref, dy_ref, acts_ref, wo_ref, gamma_ref, out_ref, gam_ref, db_ref):
    toks = n_ref.shape[0]
    hid = acts_ref.shape[1] // 2
    first, second = picks(hid // part, part)
    dpre = acts_ref[:, hid:]
    dw_in = dot(dpre, n_ref[...], 0, 0).astype(BF)
    proj = dot(acts_ref[:, :hid], dy_ref[...], 0, 0)
    gam_ref[...] = jnp.sum(wo_ref[...].astype(F32) * proj, 0, keepdims=True)
    dw_out = (proj * gamma_ref[...]).astype(BF)
    out_ref[...] = (dot(first, dw_in, 1, 0) + dot(second, dw_out, 1, 0)).astype(BF)
    nz = hid // part // ny
    lane = lax.broadcasted_iota(jnp.int32, (db_ref.shape[1], hid), 0)
    place = lax.broadcasted_iota(jnp.int32, (1, hid), 1)
    block = jnp.floor((place.astype(F32) + 0.5) * (1.0 / part)).astype(jnp.int32)
    ring = jnp.floor((block.astype(F32) + 0.5) * (1.0 / nz)).astype(jnp.int32)
    ahead = ring + place_ref[0]
    along_z = block - ring * nz
    far = along_z >= nz // 2
    zq = jnp.where(far, along_z - nz // 2, along_z)
    zp = jnp.where(far, 1 - place_ref[1], place_ref[1])
    owner = (zq * 2 + zp) * ny + jnp.where(ahead >= ny, ahead - ny, ahead)
    spot = jnp.where(lane == owner * 2 * part + place - block * part, 1.0, 0.0).astype(BF)
    db = dot(jnp.ones((16, toks), BF), dpre, 1, 0).astype(BF)
    db_ref[...] = dot(db, spot, 1, 1)[:1]


def grads(part, ny, place, n, dy, acts, wo, gamma):
    chans = n.shape[1]
    hid = acts.shape[1] // 2
    return call(
        functools.partial(grads_body, part, ny),
        [
            jax.ShapeDtypeStruct((2 * hid, chans), BF),
            jax.ShapeDtypeStruct((1, chans), F32),
            jax.ShapeDtypeStruct((1, 2 * hid), F32),
        ],
        [smem()] + [vmem()] * 5,
    )(place, n, dy, acts, wo, gamma[None])


def slices_body(w_in_ref, w_out_ref, b_ref, out_ref):
    part, chans = w_in_ref.shape
    row = lax.broadcasted_iota(jnp.int32, (2 * part, part), 0)
    place = lax.broadcasted_iota(jnp.int32, (2 * part, part), 1)
    first = jnp.where(row == place, 1.0, 0.0).astype(BF)
    second = jnp.where(row == place + part, 1.0, 0.0).astype(BF)
    rows = (dot(first, w_in_ref[...], 1, 0) + dot(second, w_out_ref[...], 1, 0)).astype(BF)
    bias = jnp.broadcast_to(b_ref[...], (SIDE, part))
    high = bias.astype(BF).astype(F32)
    line = lax.broadcasted_iota(jnp.int32, (SIDE, part), 0)
    both = jnp.where(line == 0, high, jnp.where(line == 1, bias - high, 0.0)).astype(BF)
    side = dot(first, both, 1, 1).astype(BF)
    for k in range(out_ref.shape[0]):
        out_ref[k, :, :chans] = rows
        out_ref[k, :, chans:] = side


def slices(copies, w_in, w_out, b_in):
    part, chans = w_in.shape
    return call(
        slices_body,
        jax.ShapeDtypeStruct((copies, 2 * part, chans + SIDE), BF),
        [vmem()] * 3,
    )(w_in, w_out, b_in[None])


def results_body(part, n_taps, gathered_ref, gamma_ref, b_out_ref, dw_in_ref, dw_out_ref, taps_ref, db_ref, *rest):
    chans = dw_in_ref.shape[1]
    lane = lax.broadcasted_iota(jnp.int32, (1, 128), 1)
    total, db = None, None
    for k in range(gathered_ref.shape[0]):
        block = gathered_ref[k].astype(F32)
        dw_in_ref[k * part : (k + 1) * part] = block[:part, :chans]
        dw_out_ref[k * part : (k + 1) * part] = block[part:, :chans]
        side = block[:, chans:]
        side = side + pltpu.roll(side, 64, 1)
        line = side.T
        line = line[62:63] + line[63:64]
        line = jnp.concatenate([line, jnp.zeros((1, 128 - line.shape[1]), F32)], 1)
        line = jnp.where(lane < part, line, 0.0)
        line = line if k == 0 else pltpu.roll(line, k * part, 1)
        db = line if db is None else db + line
        total = side if total is None else total + side
    db_ref[...] = db[0, : db_ref.shape[0]]
    taps_ref[...] = total[:, :n_taps]
    lines = total.T
    dysum = lines[n_taps + 1]
    rest[0][...] = lines[n_taps]
    rest[1][...] = lines[56] + lines[57]
    rest[2][...] = lines[58] + lines[59]
    rest[3][...] = gamma_ref[...] * dysum
    rest[4][...] = lines[60] + lines[61] + b_out_ref[...] * dysum


def results(part, n_taps, gathered, chans, gamma, b_out):
    members, rows, _ = gathered.shape
    return call(
        functools.partial(results_body, part, n_taps),
        [
            jax.ShapeDtypeStruct((members * part, chans), F32),
            jax.ShapeDtypeStruct((members * part, chans), F32),
            jax.ShapeDtypeStruct((rows, n_taps), F32),
            jax.ShapeDtypeStruct((members * part,), F32),
        ]
        + [jax.ShapeDtypeStruct((rows,), F32)] * 5,
        [vmem()] * 3,
    )(gathered, gamma, b_out)


def to_neighbour(blocks):
    half = blocks.shape[0] // 2
    return blocks[:half] + lax.ppermute(blocks[half:].astype(BF), "zp", [(0, 1), (1, 0)]).astype(F32)


def two_parts(value):
    high = lax.reduce_precision(value, 8, 7)
    return high.astype(BF), (value - high).astype(BF)


def to_all(block, axis):
    count = lax.axis_size(axis)
    return lax.all_to_all(jnp.broadcast_to(block[None], (count,) + block.shape), axis, 0, 0, tiled=True)


def exchange(blocks):
    return lax.all_to_all(blocks, CHAN, 0, 0, tiled=True)


def halo_swaps(first, last):
    count = lax.axis_size(LAT)
    even = lax.axis_index(LAT) % 2 == 0
    pairs = [(i, i + 1) for i in range(0, count, 2)]
    within = lax.ppermute(jnp.where(even, last, first), LAT, pairs + [(j, i) for i, j in pairs])
    pairs = [(i, i + 1) for i in range(1, count - 1, 2)]
    across = lax.ppermute(jnp.where(even, first, last), LAT, pairs + [(j, i) for i, j in pairs])
    return within, across


def halos(first, last):
    count = lax.axis_size(LAT)
    place = lax.axis_index(LAT)
    even = place % 2 == 0
    pairs = [(i, i + 1) for i in range(0, count, 2)]
    within = lax.ppermute(jnp.where(even, last, first), LAT, pairs + [(j, i) for i, j in pairs])
    pairs = [(i, i + 1) for i in range(1, count - 1, 2)]
    across = lax.ppermute(jnp.where(even, first, last), LAT, pairs + [(j, i) for i, j in pairs])
    return jnp.where(even, across, within), jnp.where(even, within, across)


def along_ring(block, ahead):
    count = lax.axis_size("y")
    return lax.ppermute(block, "y", [((i + ahead) % count, i) for i in range(count)])


def to_ring(blocks):
    count = lax.axis_size("y")
    total = blocks[0].astype(F32)
    for k in range(1, count):
        total = total + lax.ppermute(blocks[k], "y", [(i, (i + k) % count) for i in range(count)]).astype(F32)
    return total


def per_device(
    block_input,
    out_grad,
    metric,
    kernel,
    conv_bias,
    ln_gain,
    ln_bias,
    w_in,
    b_in,
    w_out,
    b_out,
    layer_scale,
):
    cdev, rows, width = block_input.shape
    chans = ln_gain.shape[0]
    tokens = rows * width
    nz, ny = lax.axis_size(ZLO), lax.axis_size("y")
    nchan = nz * ny
    hdev = w_in.shape[0]
    part = hdev // GROUP
    piece = tokens // nchan
    owner = lax.axis_index(CHAN)
    gamma_f = layer_scale.astype(F32)
    gamma_own = lax.dynamic_slice_in_dim(gamma_f, owner * cdev, cdev)

    start = lax.axis_index(("x", "c")) * part
    cut = [lax.dynamic_slice_in_dim(w, start, part) for w in (w_in, w_out, b_in)]
    shards = lax.all_to_all(slices(nz // 2, *cut), "zq", 0, 0, tiled=True)
    beside = lax.ppermute(shards, "zp", [(0, 1), (1, 0)])

    up, down = halos(block_input[:, :3], block_input[:, rows - 3 :])
    taps_bias = jnp.concatenate([kernel, conv_bias[:, None]], 1)
    blocks = forward(taps_bias, block_input, up, down, metric, out_grad)
    blocks, shards, beside = lax.optimization_barrier((blocks, shards, beside))

    recv = exchange(blocks)
    shards = jnp.concatenate([shards, beside], 0)
    one, last = along_ring(shards, 1), along_ring(shards, -1)
    recv, one, last = lax.optimization_barrier((recv, one, last))

    pair, nhat, rstd = norm(recv.reshape(chans, 2 * piece), ln_gain, ln_bias, GROUP // 2)
    pair = lax.all_to_all(pair, "x", 0, 0, tiled=True)
    low, high = along_ring(one[: nz // 2], 1), along_ring(last[nz // 2 :], -1)
    pair, low, high = lax.optimization_barrier((pair, low, high))
    wi, wo, bi = weights([shards, one, low, high, last], part, chans)
    other = lax.ppermute(pair, "c", [(0, 1), (1, 0)])

    core = lax.axis_index("c").astype(jnp.int32)[None]
    dn, n, dy, acts = mlp(core, pair, other, wi, wo, bi, gamma_f)
    dn = lax.all_to_all(dn, ("c", "x"), 0, 0, tiled=True)

    place = jnp.stack([lax.axis_index("y"), lax.axis_index("zp")]).astype(jnp.int32)
    dws, gam_part, db_part = grads(part, ny, place, n, dy, acts, wo, gamma_f)
    dws = to_ring(dws.reshape(ny, nz, 2 * part, chans))
    dws = to_neighbour(dws).astype(BF)

    payload = exchange(norm_back(dn, nhat, rstd, ln_gain, gam_part, db_part, nchan))
    payload, dws = lax.optimization_barrier((payload, dws))
    dws = lax.all_to_all(dws, "zq", 0, 0, tiled=True)
    dws = jnp.sum(dws.astype(F32), 0)
    dconv, ends, dh_sums, extra = stencil_cotangent(payload, metric, cdev, width)
    taps = tap_sums(dconv, dh_sums, block_input, up, down, out_grad)

    small = jnp.concatenate([jnp.sum(taps, 2), extra[:, :8]], 1)
    mine = jnp.concatenate([dws.astype(BF)] + list(two_parts(small)), 1)
    mine, ends = lax.optimization_barrier((mine, ends))
    other = lax.ppermute(mine, "zh", [(0, 1), (1, 0)])
    within, across = halo_swaps(ends[0], ends[1])
    other, within, across = lax.optimization_barrier((other, within, across))
    even = lax.axis_index(LAT) % 2 == 0
    dup, ddown = jnp.where(even, across, within), jnp.where(even, within, across)
    other = other.astype(F32)
    count = small.shape[1]
    dws = dws + other[:, :chans]
    small = small + other[:, chans : chans + count] + other[:, chans + count :]
    mine = jnp.concatenate([dws.astype(BF)] + list(two_parts(small)), 1)
    grad_input = spread_back(taps_bias, dconv, dup, ddown, out_grad)
    grad_w_in, grad_w_out, grad_kernel, db, *rest = results(
        part, kernel.shape[1], to_all(mine, ("x", "c")), chans, gamma_own, b_out
    )
    return (
        grad_input,
        grad_kernel,
        rest[0],
        rest[1],
        rest[2],
        grad_w_in,
        db,
        grad_w_out,
        rest[3],
        rest[4],
    )


def solution(mesh):
    split = Mesh(mesh.devices.reshape(2, 4, 2, 4, 2, 4), ("zh", "x", "c", "zq", "zp", "y"))
    return jax.shard_map(
        per_device,
        mesh=split,
        in_specs=(
            P(CHAN, LAT, None),
            P(CHAN, LAT, None),
            P(LAT),
            P(CHAN, None),
            P(CHAN),
            P(),
            P(),
            P(CHAN, None),
            P(CHAN),
            P(CHAN, None),
            P(CHAN),
            P(),
        ),
        out_specs=(
            P(CHAN, LAT, None),
            P(CHAN, None),
            P(CHAN),
            P(CHAN),
            P(CHAN),
            P(CHAN, None),
            P(CHAN),
            P(CHAN, None),
            P(CHAN),
            P(CHAN),
        ),
        check_vma=False,
    )
```

```python
import functools

import jax
import jax.numpy as jnp
from jax import lax
from jax.experimental import pallas as pl
from jax.experimental.pallas import tpu as pltpu
from jax.sharding import Mesh, PartitionSpec as P

LAT = ("zh", "x", "c")
ZLO = ("zq", "zp")
CHAN = ("zq", "zp", "y")
GROUP = 8
F32 = jnp.float32
BF = jnp.bfloat16
EXT = 16
VMEM_BYTES = 12 * 1024 * 1024
SIDE = 128


def vmem():
    return pl.BlockSpec(memory_space=pltpu.VMEM)


def smem():
    return pl.BlockSpec(memory_space=pltpu.SMEM)


def call(body, out_shape, in_specs, scratch=()):
    many = isinstance(out_shape, (list, tuple))
    return pl.pallas_call(
        body,
        out_shape=out_shape,
        in_specs=in_specs,
        out_specs=[vmem()] * len(out_shape) if many else vmem(),
        scratch_shapes=list(scratch),
        compiler_params=pltpu.CompilerParams(vmem_limit_bytes=VMEM_BYTES),
    )


def fill_rows(x_ref, up_ref, down_ref, ext):
    rows = x_ref.shape[1]
    ext[:, :3, :] = up_ref[...].astype(F32)
    ext[:, 3 : 3 + rows, :] = x_ref[...].astype(F32)
    ext[:, 3 + rows : 6 + rows, :] = down_ref[...].astype(F32)


def row_shifts(ext, c, rows):
    return [ext[c, a : a + rows, :] for a in range(7)]


def along(cells, move):
    width = cells.shape[1]
    if move == 0:
        return cells
    lane = lax.broadcasted_iota(jnp.int32, cells.shape, 1)
    inside = lane < width - move if move > 0 else lane >= -move
    return jnp.where(inside, pltpu.roll(cells, (-move) % width, 1), 0.0)


def stencil(taps_ref, c, shifts, flip):
    total = None
    for b in range(7):
        column = None
        for a in range(7):
            tap = a * 7 + b
            term = taps_ref[c, 48 - tap if flip else tap] * shifts[a]
            column = term if column is None else column + term
        column = along(column, b - 3)
        total = column if total is None else total + column
    return total


def forward_body(taps_ref, x_ref, up_ref, down_ref, metric_ref, dy_ref, out_ref, ext, h_rows, dy_rows):
    cdev, rows, width = x_ref.shape
    fill_rows(x_ref, up_ref, down_ref, ext)
    dy_flat = dy_ref[...].astype(F32).reshape(cdev * rows, width)
    for t in range(width // 128):
        dy_rows[t] = dy_flat[:, t * 128 : t * 128 + 128]
    metric = jnp.broadcast_to(metric_ref[...], (rows, width))

    def channel(c, carry):
        h = taps_ref[c, 49] + metric * stencil(taps_ref, c, row_shifts(ext, c, rows), False)
        for t in range(width // 128):
            h_rows[t, pl.ds(pl.multiple_of(c * rows, rows), rows), :] = h[:, t * 128 : t * 128 + 128]
        return carry

    lax.fori_loop(0, cdev, channel, 0, unroll=8)
    low = lax.broadcasted_iota(jnp.int32, (cdev, 128), 1) < 64
    for r in range(rows):
        for t in range(width // 128):
            h_tile, dy_tile = h_rows[t, pl.ds(r, cdev, rows), :], dy_rows[t, pl.ds(r, cdev, rows), :]
            at = (r * width + t * 128) // 64
            out_ref[at] = jnp.where(low, h_tile, pltpu.roll(dy_tile, 64, 1)).astype(BF)
            out_ref[at + 1] = jnp.where(low, pltpu.roll(h_tile, 64, 1), dy_tile).astype(BF)


def forward(taps, x, up, down, metric, dy):
    cdev, rows, width = x.shape
    return call(
        forward_body,
        jax.ShapeDtypeStruct((rows * width // 64, cdev, 128), BF),
        [smem()] + [vmem()] * 5,
        [
            pltpu.VMEM((cdev, EXT, width), F32),
            pltpu.VMEM((width // 128, cdev * rows, 128), F32),
            pltpu.VMEM((width // 128, cdev * rows, 128), F32),
        ],
    )(taps, x, up, down, metric[:, None], dy)


def norm_body(recv_ref, gain_ref, bias_ref, pair_ref, nhat_ref, rstd_ref):
    chans, lanes = recv_ref.shape
    piece = lanes // 2
    both = recv_ref[...].astype(F32).T
    h = both[:piece]
    mean = jnp.sum(h, 1, keepdims=True) / chans
    var = jnp.sum(h * h, 1, keepdims=True) / chans - mean * mean
    rstd = 1.0 / jnp.sqrt(var + 1e-06)
    nhat = (h - mean) * rstd
    nhat_ref[...] = nhat
    rstd_ref[...] = jnp.broadcast_to(rstd, rstd_ref.shape)
    n = (nhat * gain_ref[...] + bias_ref[...]).astype(BF)
    dy = both[piece:].astype(BF)
    for k in range(pair_ref.shape[0]):
        pair_ref[k, :piece] = n
        pair_ref[k, piece:] = dy


def norm(recv, gain, bias, copies):
    chans, lanes = recv.shape
    return call(
        norm_body,
        [
            jax.ShapeDtypeStruct((copies, lanes, chans), BF),
            jax.ShapeDtypeStruct((lanes // 2, chans), F32),
            jax.ShapeDtypeStruct((lanes // 2, 128), F32),
        ],
        [vmem()] * 3,
    )(recv, gain[None], bias[None])


def norm_back_body(recv_ref, nhat_ref, rstd_ref, gain_ref, gam_ref, db_ref, out_ref, flat):
    piece, chans = nhat_ref.shape
    dn = recv_ref[0].astype(F32)
    for k in range(1, recv_ref.shape[0]):
        dn = dn + recv_ref[k].astype(F32)
    nhat = nhat_ref[...]
    dnhat = dn * gain_ref[...]
    s1 = jnp.sum(dnhat, 1, keepdims=True) / chans
    s2 = jnp.sum(dnhat * nhat, 1, keepdims=True) / chans
    dh = rstd_ref[:, :1] * (dnhat - s1 - nhat * s2)
    flat[:piece] = dh
    flat[piece:] = jnp.zeros((flat.shape[0] - piece, chans), F32)
    sums = (jnp.sum(dn * nhat, 0, keepdims=True), jnp.sum(dn, 0, keepdims=True), gam_ref[...], db_ref[...])
    for k, value in enumerate(sums):
        high = value.astype(BF).astype(F32)
        flat[piece + 2 * k : piece + 2 * k + 1] = high
        flat[piece + 2 * k + 1 : piece + 2 * k + 2] = value - high
    blocks = flat[...].T.reshape(out_ref.shape[0], 24, 128)
    one, two, three = blocks[:, :8], blocks[:, 8:16], blocks[:, 16:]
    lane = lax.broadcasted_iota(jnp.int32, one.shape, 2)
    out_ref[:, :8] = jnp.where(lane < 64, one, pltpu.roll(three, 64, 2)).astype(BF)
    last = jnp.where(lane < 72, one, jnp.where(lane < 80, pltpu.roll(two, 8, 2), pltpu.roll(three, 16, 2)))
    out_ref[:, 8:] = jnp.where(lane < 64, two, last).astype(BF)


def norm_back(recv, nhat, rstd, gain, gam, db, owners):
    piece, chans = nhat.shape
    return call(
        norm_back_body,
        jax.ShapeDtypeStruct((owners, 16, 128), BF),
        [vmem()] * 6,
        [pltpu.VMEM((128, chans), F32)],
    )(recv, nhat, rstd, gain[None], gam, db)


def dconv_body(recv_ref, metric_ref, dconv_ref, ends_ref, sums_ref, extra_ref, dh_rows):
    cdev, rows, width = dconv_ref.shape
    low16 = lax.broadcasted_iota(jnp.int32, (16, 128), 1) < 64
    low8 = lax.broadcasted_iota(jnp.int32, (8, 128), 1) < 64
    extra = jnp.zeros((8, 128), F32)
    for r in range(rows):
        for t in range(width // 128):
            at = (r * width + t * 128) // 64
            first, second = recv_ref[at].astype(F32), recv_ref[at + 1].astype(F32)
            dh_rows[t, pl.ds(r, 16, rows), :] = jnp.where(low16, first, pltpu.roll(second, 64, 1))
            dh_rows[t, pl.ds(16 * rows + r, 8, rows), :] = jnp.where(low8, pltpu.roll(first[:8], 64, 1), second[:8])
            extra = extra + first[8:] + second[8:]
    for g in range(3):
        extra_ref[8 * g : 8 * g + 8] = pltpu.roll(extra, 64 - 8 * g, 1)
    metric = jnp.broadcast_to(metric_ref[...], (rows, 128))
    for c in range(cdev):
        for t in range(width // 128):
            dh = dh_rows[t, c * rows : (c + 1) * rows, :]
            dconv = metric * dh
            lanes = slice(t * 128, t * 128 + 128)
            dconv_ref[c, :, lanes] = dconv
            ends_ref[0, c, :, lanes] = dconv[:3].astype(BF)
            ends_ref[1, c, :, lanes] = dconv[rows - 3 :].astype(BF)
            sums_ref[c] = dh if t == 0 else sums_ref[c] + dh


def stencil_cotangent(recv, metric, cdev, width):
    rows = metric.shape[0]
    return call(
        dconv_body,
        [
            jax.ShapeDtypeStruct((cdev, rows, width), F32),
            jax.ShapeDtypeStruct((2, cdev, 3, width), BF),
            jax.ShapeDtypeStruct((cdev, rows, 128), F32),
            jax.ShapeDtypeStruct((cdev, 128), F32),
        ],
        [vmem()] * 2,
        [pltpu.VMEM((width // 128, cdev * rows, 128), F32)],
    )(recv, metric[:, None])


def taps_body(dconv_ref, dh_sums_ref, x_ref, up_ref, down_ref, dy_ref, sums_ref, ext, prods):
    cdev, rows, width = x_ref.shape
    fill_rows(x_ref, up_ref, down_ref, ext)

    def channel(c, carry):
        dconv = dconv_ref[c]
        shifts = row_shifts(ext, c, rows)
        for b in range(7):
            moved = along(dconv, 3 - b)
            for a in range(7):
                product = shifts[a] * moved
                prods[(a * 7 + b) * 8 : (a * 7 + b) * 8 + 8, :] = product[:, :128] + product[:, 128:]
        dy = dy_ref[c].astype(F32)
        prods[392:400, :] = dh_sums_ref[c]
        prods[400:408, :] = dy[:, :128] + dy[:, 128:]
        total = prods[pl.ds(0, 56, 8), :]
        for i in range(1, 8):
            total = total + prods[pl.ds(i, 56, 8), :]
        sums_ref[c] = total
        return carry

    prods[408:, :] = jnp.zeros((prods.shape[0] - 408, 128), F32)
    lax.fori_loop(0, cdev, channel, 0, unroll=8)


def tap_sums(dconv, dh_sums, x, up, down, dy):
    cdev, rows, width = x.shape
    return call(
        taps_body,
        jax.ShapeDtypeStruct((cdev, 56, 128), F32),
        [vmem()] * 6,
        [pltpu.VMEM((cdev, EXT, width), F32), pltpu.VMEM((448, 128), F32)],
    )(dconv, dh_sums, x, up, down, dy)


def spread_body(taps_ref, x_ref, up_ref, down_ref, dy_ref, out_ref, ext):
    cdev, rows, width = x_ref.shape
    fill_rows(x_ref, up_ref, down_ref, ext)

    def channel(c, carry):
        out_ref[c] = dy_ref[c].astype(F32) + stencil(taps_ref, c, row_shifts(ext, c, rows), True)
        return carry

    lax.fori_loop(0, cdev, channel, 0, unroll=8)


def spread_back(taps, dconv, up, down, dy):
    cdev, rows, width = dconv.shape
    return call(
        spread_body,
        jax.ShapeDtypeStruct((cdev, rows, width), F32),
        [smem()] + [vmem()] * 4,
        [pltpu.VMEM((cdev, EXT, width), F32)],
    )(taps, dconv, up, down, dy)


def picks(blocks, part):
    shape = (blocks * 2 * part, blocks * part)
    row = lax.broadcasted_iota(jnp.int32, shape, 0)
    place = lax.broadcasted_iota(jnp.int32, shape, 1)
    block = jnp.floor((row.astype(F32) + 0.5) * (0.5 / part)).astype(jnp.int32)
    inside = row - block * 2 * part
    first = (inside < part) & (place == block * part + inside)
    second = (inside >= part) & (place == block * part + inside - part)
    return [jnp.where(m, 1.0, 0.0).astype(BF) for m in (first, second)]


def dot(a, b, a_dim, b_dim):
    return lax.dot_general(a, b, (((a_dim,), (b_dim,)), ((), ())), preferred_element_type=F32)


def weights_body(part, own_ref, one_ref, low_ref, high_ref, last_ref, wi_ref, wo_ref, bi_ref, rows):
    blocks = 0
    for ref in (own_ref, one_ref, low_ref, high_ref, last_ref):
        for k in range(ref.shape[0]):
            at = blocks * 2 * part
            rows[at : at + 2 * part] = ref[k].astype(F32)
            blocks += 1
    chans = wi_ref.shape[1]
    flat = rows[...].astype(BF)
    first, second = picks(blocks, part)
    wi_ref[...] = dot(first, flat[:, :chans], 0, 0).astype(BF)
    wo_ref[...] = dot(second, flat[:, :chans], 0, 0).astype(BF)
    both = dot(flat[:, chans:], first, 0, 0)
    bi_ref[...] = both[:1] + both[1:2]


def weights(parts, part, chans):
    blocks = sum(p.shape[0] for p in parts)
    return call(
        functools.partial(weights_body, part),
        [
            jax.ShapeDtypeStruct((blocks * part, chans), BF),
            jax.ShapeDtypeStruct((blocks * part, chans), BF),
            jax.ShapeDtypeStruct((1, blocks * part), F32),
        ],
        [vmem()] * len(parts),
        [pltpu.VMEM((blocks * 2 * part, parts[0].shape[2]), F32)],
    )(*parts)


def mlp_body(core_ref, own_ref, other_ref, wi_ref, wo_ref, bi_ref, gamma_ref, dn_ref, n_ref, dy_ref, acts_ref):
    members, lanes, _ = own_ref.shape
    piece = lanes // 2
    for at, ref in ((0, own_ref), (members, other_ref)):
        for k in range(members):
            n_ref[(at + k) * piece : (at + k + 1) * piece] = ref[k, :piece]
            dy_ref[(at + k) * piece : (at + k + 1) * piece] = ref[k, piece:]
    pre = dot(n_ref[...], wi_ref[...], 1, 1) + bi_ref[...]
    cdf = 0.5 + 0.5 * lax.erf(pre * (0.5**0.5))
    hid = pre.shape[1]
    acts_ref[:, :hid] = (pre * cdf).astype(BF)
    slope = cdf + pre * (jnp.exp(-0.5 * pre * pre) * (0.5 / 3.141592653589793) ** 0.5)
    dmlp = (gamma_ref[...] * dy_ref[...].astype(F32)).astype(BF)
    dpre = (slope * dot(dmlp, wo_ref[...], 1, 1)).astype(BF)
    acts_ref[:, hid:] = dpre
    dn = dot(dpre, wi_ref[...], 1, 0).astype(BF)
    core = core_ref[0]
    for k in range(members):
        dn_ref[core * members + k] = dn[k * piece : (k + 1) * piece]
        dn_ref[(1 - core) * members + k] = dn[(members + k) * piece : (members + k + 1) * piece]


def mlp(core, own, other, wi, wo, bi, gamma):
    members, lanes, chans = own.shape
    toks, hid = members * lanes, wi.shape[0]
    return call(
        mlp_body,
        [
            jax.ShapeDtypeStruct((2 * members, lanes // 2, chans), BF),
            jax.ShapeDtypeStruct((toks, chans), BF),
            jax.ShapeDtypeStruct((toks, chans), BF),
            jax.ShapeDtypeStruct((toks, 2 * hid), BF),
        ],
        [smem()] + [vmem()] * 6,
    )(core, own, other, wi, wo, bi, gamma[None])


def grads_body(part, ny, place_ref, n_ref, dy_ref, acts_ref, wo_ref, gamma_ref, out_ref, gam_ref, db_ref):
    toks = n_ref.shape[0]
    hid = acts_ref.shape[1] // 2
    first, second = picks(hid // part, part)
    dpre = acts_ref[:, hid:]
    dw_in = dot(dpre, n_ref[...], 0, 0).astype(BF)
    proj = dot(acts_ref[:, :hid], dy_ref[...], 0, 0)
    gam_ref[...] = jnp.sum(wo_ref[...].astype(F32) * proj, 0, keepdims=True)
    dw_out = (proj * gamma_ref[...]).astype(BF)
    out_ref[...] = (dot(first, dw_in, 1, 0) + dot(second, dw_out, 1, 0)).astype(BF)
    nz = hid // part // ny
    lane = lax.broadcasted_iota(jnp.int32, (db_ref.shape[1], hid), 0)
    place = lax.broadcasted_iota(jnp.int32, (1, hid), 1)
    block = jnp.floor((place.astype(F32) + 0.5) * (1.0 / part)).astype(jnp.int32)
    ring = jnp.floor((block.astype(F32) + 0.5) * (1.0 / nz)).astype(jnp.int32)
    ahead = ring + place_ref[0]
    along_z = block - ring * nz
    far = along_z >= nz // 2
    zq = jnp.where(far, along_z - nz // 2, along_z)
    zp = jnp.where(far, 1 - place_ref[1], place_ref[1])
    owner = (zq * 2 + zp) * ny + jnp.where(ahead >= ny, ahead - ny, ahead)
    spot = jnp.where(lane == owner * 2 * part + place - block * part, 1.0, 0.0).astype(BF)
    db = dot(jnp.ones((16, toks), BF), dpre, 1, 0).astype(BF)
    db_ref[...] = dot(db, spot, 1, 1)[:1]


def grads(part, ny, place, n, dy, acts, wo, gamma):
    chans = n.shape[1]
    hid = acts.shape[1] // 2
    return call(
        functools.partial(grads_body, part, ny),
        [
            jax.ShapeDtypeStruct((2 * hid, chans), BF),
            jax.ShapeDtypeStruct((1, chans), F32),
            jax.ShapeDtypeStruct((1, 2 * hid), F32),
        ],
        [smem()] + [vmem()] * 5,
    )(place, n, dy, acts, wo, gamma[None])


def slices_body(w_in_ref, w_out_ref, b_ref, out_ref):
    part, chans = w_in_ref.shape
    row = lax.broadcasted_iota(jnp.int32, (2 * part, part), 0)
    place = lax.broadcasted_iota(jnp.int32, (2 * part, part), 1)
    first = jnp.where(row == place, 1.0, 0.0).astype(BF)
    second = jnp.where(row == place + part, 1.0, 0.0).astype(BF)
    rows = (dot(first, w_in_ref[...], 1, 0) + dot(second, w_out_ref[...], 1, 0)).astype(BF)
    bias = jnp.broadcast_to(b_ref[...], (SIDE, part))
    high = bias.astype(BF).astype(F32)
    line = lax.broadcasted_iota(jnp.int32, (SIDE, part), 0)
    both = jnp.where(line == 0, high, jnp.where(line == 1, bias - high, 0.0)).astype(BF)
    side = dot(first, both, 1, 1).astype(BF)
    for k in range(out_ref.shape[0]):
        out_ref[k, :, :chans] = rows
        out_ref[k, :, chans:] = side


def slices(copies, w_in, w_out, b_in):
    part, chans = w_in.shape
    return call(
        slices_body,
        jax.ShapeDtypeStruct((copies, 2 * part, chans + SIDE), BF),
        [vmem()] * 3,
    )(w_in, w_out, b_in[None])


def results_body(part, n_taps, gathered_ref, gamma_ref, b_out_ref, dw_in_ref, dw_out_ref, taps_ref, db_ref, *rest):
    chans = dw_in_ref.shape[1]
    lane = lax.broadcasted_iota(jnp.int32, (1, 128), 1)
    total, db = None, None
    for k in range(gathered_ref.shape[0]):
        block = gathered_ref[k].astype(F32)
        dw_in_ref[k * part : (k + 1) * part] = block[:part, :chans]
        dw_out_ref[k * part : (k + 1) * part] = block[part:, :chans]
        side = block[:, chans:]
        side = side + pltpu.roll(side, 64, 1)
        line = side.T
        line = line[62:63] + line[63:64]
        line = jnp.concatenate([line, jnp.zeros((1, 128 - line.shape[1]), F32)], 1)
        line = jnp.where(lane < part, line, 0.0)
        line = line if k == 0 else pltpu.roll(line, k * part, 1)
        db = line if db is None else db + line
        total = side if total is None else total + side
    db_ref[...] = db[0, : db_ref.shape[0]]
    taps_ref[...] = total[:, :n_taps]
    lines = total.T
    dysum = lines[n_taps + 1]
    rest[0][...] = lines[n_taps]
    rest[1][...] = lines[56] + lines[57]
    rest[2][...] = lines[58] + lines[59]
    rest[3][...] = gamma_ref[...] * dysum
    rest[4][...] = lines[60] + lines[61] + b_out_ref[...] * dysum


def results(part, n_taps, gathered, chans, gamma, b_out):
    members, rows, _ = gathered.shape
    return call(
        functools.partial(results_body, part, n_taps),
        [
            jax.ShapeDtypeStruct((members * part, chans), F32),
            jax.ShapeDtypeStruct((members * part, chans), F32),
            jax.ShapeDtypeStruct((rows, n_taps), F32),
            jax.ShapeDtypeStruct((members * part,), F32),
        ]
        + [jax.ShapeDtypeStruct((rows,), F32)] * 5,
        [vmem()] * 3,
    )(gathered, gamma, b_out)


def to_neighbour(blocks):
    half = blocks.shape[0] // 2
    return blocks[:half] + lax.ppermute(blocks[half:].astype(BF), "zp", [(0, 1), (1, 0)]).astype(F32)


def two_parts(value):
    high = lax.reduce_precision(value, 8, 7)
    return high.astype(BF), (value - high).astype(BF)


def to_all(block, axis):
    count = lax.axis_size(axis)
    return lax.all_to_all(jnp.broadcast_to(block[None], (count,) + block.shape), axis, 0, 0, tiled=True)


def exchange(blocks):
    return lax.all_to_all(blocks, CHAN, 0, 0, tiled=True)


def swap_even(first, last):
    even = lax.axis_index(LAT) % 2 == 0
    pairs = [(i, i + 1) for i in range(0, lax.axis_size(LAT), 2)]
    return lax.ppermute(jnp.where(even, last, first), LAT, pairs + [(j, i) for i, j in pairs])


def swap_odd(first, last):
    even = lax.axis_index(LAT) % 2 == 0
    pairs = [(i, i + 1) for i in range(1, lax.axis_size(LAT) - 1, 2)]
    return lax.ppermute(jnp.where(even, first, last), LAT, pairs + [(j, i) for i, j in pairs])


def up_down(within, across):
    even = lax.axis_index(LAT) % 2 == 0
    return jnp.where(even, across, within), jnp.where(even, within, across)


def along_ring(block, ahead):
    count = lax.axis_size("y")
    return lax.ppermute(block, "y", [((i + ahead) % count, i) for i in range(count)])


def to_ring(blocks):
    count = lax.axis_size("y")
    total = blocks[0].astype(F32)
    for k in range(1, count):
        total = total + lax.ppermute(blocks[k], "y", [(i, (i + k) % count) for i in range(count)]).astype(F32)
    return total


def per_device(
    block_input,
    out_grad,
    metric,
    kernel,
    conv_bias,
    ln_gain,
    ln_bias,
    w_in,
    b_in,
    w_out,
    b_out,
    layer_scale,
):
    cdev, rows, width = block_input.shape
    chans = ln_gain.shape[0]
    tokens = rows * width
    nz, ny = lax.axis_size(ZLO), lax.axis_size("y")
    nchan = nz * ny
    hdev = w_in.shape[0]
    part = hdev // GROUP
    piece = tokens // nchan
    owner = lax.axis_index(CHAN)
    gamma_f = layer_scale.astype(F32)
    gamma_own = lax.dynamic_slice_in_dim(gamma_f, owner * cdev, cdev)

    start = lax.axis_index(("x", "c")) * part
    cut = [lax.dynamic_slice_in_dim(w, start, part) for w in (w_in, w_out, b_in)]
    shards = lax.all_to_all(slices(nz // 2, *cut), "zq", 0, 0, tiled=True)
    beside = lax.ppermute(shards, "zp", [(0, 1), (1, 0)])

    across = swap_odd(block_input[:, :3], block_input[:, rows - 3 :])
    up, down = up_down(swap_even(block_input[:, :3], block_input[:, rows - 3 :]), across)
    taps_bias = jnp.concatenate([kernel, conv_bias[:, None]], 1)
    blocks = forward(taps_bias, block_input, up, down, metric, out_grad)
    blocks, shards, beside = lax.optimization_barrier((blocks, shards, beside))

    recv = exchange(blocks)
    shards = jnp.concatenate([shards, beside], 0)
    one, last = along_ring(shards, 1), along_ring(shards, -1)
    recv, one, last = lax.optimization_barrier((recv, one, last))

    pair, nhat, rstd = norm(recv.reshape(chans, 2 * piece), ln_gain, ln_bias, GROUP // 2)
    pair = lax.all_to_all(pair, "x", 0, 0, tiled=True)
    low, high = along_ring(one[: nz // 2], 1), along_ring(last[nz // 2 :], -1)
    pair, low, high = lax.optimization_barrier((pair, low, high))
    wi, wo, bi = weights([shards, one, low, high, last], part, chans)
    other = lax.ppermute(pair, "c", [(0, 1), (1, 0)])

    core = lax.axis_index("c").astype(jnp.int32)[None]
    dn, n, dy, acts = mlp(core, pair, other, wi, wo, bi, gamma_f)
    dn = lax.all_to_all(dn, ("c", "x"), 0, 0, tiled=True)

    place = jnp.stack([lax.axis_index("y"), lax.axis_index("zp")]).astype(jnp.int32)
    dws, gam_part, db_part = grads(part, ny, place, n, dy, acts, wo, gamma_f)
    dws = to_ring(dws.reshape(ny, nz, 2 * part, chans))
    dws = to_neighbour(dws).astype(BF)

    payload = exchange(norm_back(dn, nhat, rstd, ln_gain, gam_part, db_part, nchan))
    payload, dws = lax.optimization_barrier((payload, dws))
    dws = lax.all_to_all(dws, "zq", 0, 0, tiled=True)
    dws = jnp.sum(dws.astype(F32), 0)
    dconv, ends, dh_sums, extra = stencil_cotangent(payload, metric, cdev, width)
    taps = tap_sums(dconv, dh_sums, block_input, up, down, out_grad)
    across = swap_odd(ends[0], ends[1])

    small = jnp.concatenate([jnp.sum(taps, 2), extra[:, :8]], 1)
    mine = jnp.concatenate([dws.astype(BF)] + list(two_parts(small)), 1)
    mine, ends = lax.optimization_barrier((mine, ends))
    other = lax.ppermute(mine, "zh", [(0, 1), (1, 0)])
    within = swap_even(ends[0], ends[1])
    other, within, across = lax.optimization_barrier((other, within, across))
    other = other.astype(F32)
    count = small.shape[1]
    dws = dws + other[:, :chans]
    small = small + other[:, chans : chans + count] + other[:, chans + count :]
    mine = jnp.concatenate([dws.astype(BF)] + list(two_parts(small)), 1)
    dup, ddown = up_down(within, across)
    grad_input = spread_back(taps_bias, dconv, dup, ddown, out_grad)
    grad_w_in, grad_w_out, grad_kernel, db, *rest = results(
        part, kernel.shape[1], to_all(mine, ("x", "c")), chans, gamma_own, b_out
    )
    return (
        grad_input,
        grad_kernel,
        rest[0],
        rest[1],
        rest[2],
        grad_w_in,
        db,
        grad_w_out,
        rest[3],
        rest[4],
    )


def solution(mesh):
    split = Mesh(mesh.devices.reshape(2, 4, 2, 4, 2, 4), ("zh", "x", "c", "zq", "zp", "y"))
    return jax.shard_map(
        per_device,
        mesh=split,
        in_specs=(
            P(CHAN, LAT, None),
            P(CHAN, LAT, None),
            P(LAT),
            P(CHAN, None),
            P(CHAN),
            P(),
            P(),
            P(CHAN, None),
            P(CHAN),
            P(CHAN, None),
            P(CHAN),
            P(),
        ),
        out_specs=(
            P(CHAN, LAT, None),
            P(CHAN, None),
            P(CHAN),
            P(CHAN),
            P(CHAN),
            P(CHAN, None),
            P(CHAN),
            P(CHAN, None),
            P(CHAN),
            P(CHAN),
        ),
        check_vma=False,
    )
```

```python
import functools

import jax
import jax.numpy as jnp
from jax import lax
from jax.experimental import pallas as pl
from jax.experimental.pallas import tpu as pltpu
from jax.sharding import Mesh, PartitionSpec as P

LAT = ("zh", "x", "c")
ZLO = ("zq", "zp")
CHAN = ("zq", "zp", "y")
GROUP = 8
F32 = jnp.float32
BF = jnp.bfloat16
EXT = 16
VMEM_BYTES = 12 * 1024 * 1024
SIDE = 128


def vmem():
    return pl.BlockSpec(memory_space=pltpu.VMEM)


def smem():
    return pl.BlockSpec(memory_space=pltpu.SMEM)


def call(body, out_shape, in_specs, scratch=()):
    many = isinstance(out_shape, (list, tuple))
    return pl.pallas_call(
        body,
        out_shape=out_shape,
        in_specs=in_specs,
        out_specs=[vmem()] * len(out_shape) if many else vmem(),
        scratch_shapes=list(scratch),
        compiler_params=pltpu.CompilerParams(vmem_limit_bytes=VMEM_BYTES),
    )


def fill_rows(x_ref, up_ref, down_ref, ext):
    rows = x_ref.shape[1]
    ext[:, :3, :] = up_ref[...].astype(F32)
    ext[:, 3 : 3 + rows, :] = x_ref[...].astype(F32)
    ext[:, 3 + rows : 6 + rows, :] = down_ref[...].astype(F32)


def row_shifts(ext, c, rows):
    return [ext[c, a : a + rows, :] for a in range(7)]


def along(cells, move):
    width = cells.shape[1]
    if move == 0:
        return cells
    lane = lax.broadcasted_iota(jnp.int32, cells.shape, 1)
    inside = lane < width - move if move > 0 else lane >= -move
    return jnp.where(inside, pltpu.roll(cells, (-move) % width, 1), 0.0)


def stencil(taps_ref, c, shifts, flip):
    total = None
    for b in range(7):
        column = None
        for a in range(7):
            tap = a * 7 + b
            term = taps_ref[c, 48 - tap if flip else tap] * shifts[a]
            column = term if column is None else column + term
        column = along(column, b - 3)
        total = column if total is None else total + column
    return total


def forward_body(taps_ref, x_ref, up_ref, down_ref, metric_ref, dy_ref, out_ref, ext, h_rows, dy_rows):
    cdev, rows, width = x_ref.shape
    fill_rows(x_ref, up_ref, down_ref, ext)
    dy_flat = dy_ref[...].astype(F32).reshape(cdev * rows, width)
    for t in range(width // 128):
        dy_rows[t] = dy_flat[:, t * 128 : t * 128 + 128]
    metric = jnp.broadcast_to(metric_ref[...], (rows, width))

    def channel(c, carry):
        h = taps_ref[c, 49] + metric * stencil(taps_ref, c, row_shifts(ext, c, rows), False)
        for t in range(width // 128):
            h_rows[t, pl.ds(pl.multiple_of(c * rows, rows), rows), :] = h[:, t * 128 : t * 128 + 128]
        return carry

    lax.fori_loop(0, cdev, channel, 0, unroll=8)
    low = lax.broadcasted_iota(jnp.int32, (cdev, 128), 1) < 64
    for r in range(rows):
        for t in range(width // 128):
            h_tile, dy_tile = h_rows[t, pl.ds(r, cdev, rows), :], dy_rows[t, pl.ds(r, cdev, rows), :]
            at = (r * width + t * 128) // 64
            out_ref[at] = jnp.where(low, h_tile, pltpu.roll(dy_tile, 64, 1)).astype(BF)
            out_ref[at + 1] = jnp.where(low, pltpu.roll(h_tile, 64, 1), dy_tile).astype(BF)


def forward(taps, x, up, down, metric, dy):
    cdev, rows, width = x.shape
    return call(
        forward_body,
        jax.ShapeDtypeStruct((rows * width // 64, cdev, 128), BF),
        [smem()] + [vmem()] * 5,
        [
            pltpu.VMEM((cdev, EXT, width), F32),
            pltpu.VMEM((width // 128, cdev * rows, 128), F32),
            pltpu.VMEM((width // 128, cdev * rows, 128), F32),
        ],
    )(taps, x, up, down, metric[:, None], dy)


def norm_body(recv_ref, gain_ref, bias_ref, pair_ref, nhat_ref, rstd_ref):
    chans, lanes = recv_ref.shape
    piece = lanes // 2
    both = recv_ref[...].astype(F32).T
    h = both[:piece]
    mean = jnp.sum(h, 1, keepdims=True) / chans
    var = jnp.sum(h * h, 1, keepdims=True) / chans - mean * mean
    rstd = 1.0 / jnp.sqrt(var + 1e-06)
    nhat = (h - mean) * rstd
    nhat_ref[...] = nhat
    rstd_ref[...] = jnp.broadcast_to(rstd, rstd_ref.shape)
    n = (nhat * gain_ref[...] + bias_ref[...]).astype(BF)
    dy = both[piece:].astype(BF)
    for k in range(pair_ref.shape[0]):
        pair_ref[k, :piece] = n
        pair_ref[k, piece:] = dy


def norm(recv, gain, bias, copies):
    chans, lanes = recv.shape
    return call(
        norm_body,
        [
            jax.ShapeDtypeStruct((copies, lanes, chans), BF),
            jax.ShapeDtypeStruct((lanes // 2, chans), F32),
            jax.ShapeDtypeStruct((lanes // 2, 128), F32),
        ],
        [vmem()] * 3,
    )(recv, gain[None], bias[None])


def norm_back_body(recv_ref, nhat_ref, rstd_ref, gain_ref, gam_ref, db_ref, out_ref, flat):
    piece, chans = nhat_ref.shape
    dn = recv_ref[0].astype(F32)
    for k in range(1, recv_ref.shape[0]):
        dn = dn + recv_ref[k].astype(F32)
    nhat = nhat_ref[...]
    dnhat = dn * gain_ref[...]
    s1 = jnp.sum(dnhat, 1, keepdims=True) / chans
    s2 = jnp.sum(dnhat * nhat, 1, keepdims=True) / chans
    dh = rstd_ref[:, :1] * (dnhat - s1 - nhat * s2)
    flat[:piece] = dh
    flat[piece:] = jnp.zeros((flat.shape[0] - piece, chans), F32)
    sums = (jnp.sum(dn * nhat, 0, keepdims=True), jnp.sum(dn, 0, keepdims=True), gam_ref[...], db_ref[...])
    for k, value in enumerate(sums):
        high = value.astype(BF).astype(F32)
        flat[piece + 2 * k : piece + 2 * k + 1] = high
        flat[piece + 2 * k + 1 : piece + 2 * k + 2] = value - high
    blocks = flat[...].T.reshape(out_ref.shape[0], 24, 128)
    one, two, three = blocks[:, :8], blocks[:, 8:16], blocks[:, 16:]
    lane = lax.broadcasted_iota(jnp.int32, one.shape, 2)
    out_ref[:, :8] = jnp.where(lane < 64, one, pltpu.roll(three, 64, 2)).astype(BF)
    last = jnp.where(lane < 72, one, jnp.where(lane < 80, pltpu.roll(two, 8, 2), pltpu.roll(three, 16, 2)))
    out_ref[:, 8:] = jnp.where(lane < 64, two, last).astype(BF)


def norm_back(recv, nhat, rstd, gain, gam, db, owners):
    piece, chans = nhat.shape
    return call(
        norm_back_body,
        jax.ShapeDtypeStruct((owners, 16, 128), BF),
        [vmem()] * 6,
        [pltpu.VMEM((128, chans), F32)],
    )(recv, nhat, rstd, gain[None], gam, db)


def dconv_body(recv_ref, metric_ref, dconv_ref, ends_ref, sums_ref, extra_ref, dh_rows):
    cdev, rows, width = dconv_ref.shape
    low16 = lax.broadcasted_iota(jnp.int32, (16, 128), 1) < 64
    low8 = lax.broadcasted_iota(jnp.int32, (8, 128), 1) < 64
    extra = jnp.zeros((8, 128), F32)
    for r in range(rows):
        for t in range(width // 128):
            at = (r * width + t * 128) // 64
            first, second = recv_ref[at].astype(F32), recv_ref[at + 1].astype(F32)
            dh_rows[t, pl.ds(r, 16, rows), :] = jnp.where(low16, first, pltpu.roll(second, 64, 1))
            dh_rows[t, pl.ds(16 * rows + r, 8, rows), :] = jnp.where(low8, pltpu.roll(first[:8], 64, 1), second[:8])
            extra = extra + first[8:] + second[8:]
    for g in range(3):
        extra_ref[8 * g : 8 * g + 8] = pltpu.roll(extra, 64 - 8 * g, 1)
    metric = jnp.broadcast_to(metric_ref[...], (rows, 128))
    for c in range(cdev):
        for t in range(width // 128):
            dh = dh_rows[t, c * rows : (c + 1) * rows, :]
            dconv = metric * dh
            lanes = slice(t * 128, t * 128 + 128)
            dconv_ref[c, :, lanes] = dconv
            ends_ref[0, c, :, lanes] = dconv[:3].astype(BF)
            ends_ref[1, c, :, lanes] = dconv[rows - 3 :].astype(BF)
            sums_ref[c] = dh if t == 0 else sums_ref[c] + dh


def stencil_cotangent(recv, metric, cdev, width):
    rows = metric.shape[0]
    return call(
        dconv_body,
        [
            jax.ShapeDtypeStruct((cdev, rows, width), F32),
            jax.ShapeDtypeStruct((2, cdev, 3, width), BF),
            jax.ShapeDtypeStruct((cdev, rows, 128), F32),
            jax.ShapeDtypeStruct((cdev, 128), F32),
        ],
        [vmem()] * 2,
        [pltpu.VMEM((width // 128, cdev * rows, 128), F32)],
    )(recv, metric[:, None])


def taps_body(dconv_ref, dh_sums_ref, x_ref, up_ref, down_ref, dy_ref, sums_ref, ext, prods):
    cdev, rows, width = x_ref.shape
    fill_rows(x_ref, up_ref, down_ref, ext)

    def channel(c, carry):
        dconv = dconv_ref[c]
        shifts = row_shifts(ext, c, rows)
        for b in range(7):
            moved = along(dconv, 3 - b)
            for a in range(7):
                product = shifts[a] * moved
                prods[(a * 7 + b) * 8 : (a * 7 + b) * 8 + 8, :] = product[:, :128] + product[:, 128:]
        dy = dy_ref[c].astype(F32)
        prods[392:400, :] = dh_sums_ref[c]
        prods[400:408, :] = dy[:, :128] + dy[:, 128:]
        total = prods[pl.ds(0, 56, 8), :]
        for i in range(1, 8):
            total = total + prods[pl.ds(i, 56, 8), :]
        sums_ref[c] = total
        return carry

    prods[408:, :] = jnp.zeros((prods.shape[0] - 408, 128), F32)
    lax.fori_loop(0, cdev, channel, 0, unroll=8)


def tap_sums(dconv, dh_sums, x, up, down, dy):
    cdev, rows, width = x.shape
    return call(
        taps_body,
        jax.ShapeDtypeStruct((cdev, 56, 128), F32),
        [vmem()] * 6,
        [pltpu.VMEM((cdev, EXT, width), F32), pltpu.VMEM((448, 128), F32)],
    )(dconv, dh_sums, x, up, down, dy)


def spread_body(taps_ref, x_ref, up_ref, down_ref, dy_ref, out_ref, ext):
    cdev, rows, width = x_ref.shape
    fill_rows(x_ref, up_ref, down_ref, ext)

    def channel(c, carry):
        out_ref[c] = dy_ref[c].astype(F32) + stencil(taps_ref, c, row_shifts(ext, c, rows), True)
        return carry

    lax.fori_loop(0, cdev, channel, 0, unroll=8)


def spread_back(taps, dconv, up, down, dy):
    cdev, rows, width = dconv.shape
    return call(
        spread_body,
        jax.ShapeDtypeStruct((cdev, rows, width), F32),
        [smem()] + [vmem()] * 4,
        [pltpu.VMEM((cdev, EXT, width), F32)],
    )(taps, dconv, up, down, dy)


def picks(blocks, part):
    shape = (blocks * 2 * part, blocks * part)
    row = lax.broadcasted_iota(jnp.int32, shape, 0)
    place = lax.broadcasted_iota(jnp.int32, shape, 1)
    block = jnp.floor((row.astype(F32) + 0.5) * (0.5 / part)).astype(jnp.int32)
    inside = row - block * 2 * part
    first = (inside < part) & (place == block * part + inside)
    second = (inside >= part) & (place == block * part + inside - part)
    return [jnp.where(m, 1.0, 0.0).astype(BF) for m in (first, second)]


def dot(a, b, a_dim, b_dim):
    return lax.dot_general(a, b, (((a_dim,), (b_dim,)), ((), ())), preferred_element_type=F32)


def weights_body(part, own_ref, one_ref, low_ref, high_ref, last_ref, wi_ref, wo_ref, bi_ref, rows):
    blocks = 0
    for ref in (own_ref, one_ref, low_ref, high_ref, last_ref):
        for k in range(ref.shape[0]):
            at = blocks * 2 * part
            rows[at : at + 2 * part] = ref[k].astype(F32)
            blocks += 1
    chans = wi_ref.shape[1]
    flat = rows[...].astype(BF)
    first, second = picks(blocks, part)
    wi_ref[...] = dot(first, flat[:, :chans], 0, 0).astype(BF)
    wo_ref[...] = dot(second, flat[:, :chans], 0, 0).astype(BF)
    both = dot(flat[:, chans:], first, 0, 0)
    bi_ref[...] = both[:1] + both[1:2]


def weights(parts, part, chans):
    blocks = sum(p.shape[0] for p in parts)
    return call(
        functools.partial(weights_body, part),
        [
            jax.ShapeDtypeStruct((blocks * part, chans), BF),
            jax.ShapeDtypeStruct((blocks * part, chans), BF),
            jax.ShapeDtypeStruct((1, blocks * part), F32),
        ],
        [vmem()] * len(parts),
        [pltpu.VMEM((blocks * 2 * part, parts[0].shape[2]), F32)],
    )(*parts)


def mlp_body(core_ref, own_ref, other_ref, wi_ref, wo_ref, bi_ref, gamma_ref, dn_ref, n_ref, dy_ref, acts_ref, gam_ref):
    members, lanes, _ = own_ref.shape
    piece = lanes // 2
    for at, ref in ((0, own_ref), (members, other_ref)):
        for k in range(members):
            n_ref[(at + k) * piece : (at + k + 1) * piece] = ref[k, :piece]
            dy_ref[(at + k) * piece : (at + k + 1) * piece] = ref[k, piece:]
    pre = dot(n_ref[...], wi_ref[...], 1, 1) + bi_ref[...]
    cdf = 0.5 + 0.5 * lax.erf(pre * (0.5**0.5))
    hid = pre.shape[1]
    acts_ref[:, :hid] = (pre * cdf).astype(BF)
    slope = cdf + pre * (jnp.exp(-0.5 * pre * pre) * (0.5 / 3.141592653589793) ** 0.5)
    dmlp = (gamma_ref[...] * dy_ref[...].astype(F32)).astype(BF)
    dpre = (slope * dot(dmlp, wo_ref[...], 1, 1)).astype(BF)
    acts_ref[:, hid:] = dpre
    dn = dot(dpre, wi_ref[...], 1, 0).astype(BF)
    core = core_ref[0]
    for k in range(members):
        dn_ref[core * members + k] = dn[k * piece : (k + 1) * piece]
        dn_ref[(1 - core) * members + k] = dn[(members + k) * piece : (members + k + 1) * piece]
    back = dot(acts_ref[:, :hid], wo_ref[...], 1, 0)
    gam_ref[...] = jnp.sum(dy_ref[...].astype(F32) * back, 0, keepdims=True)


def mlp(core, own, other, wi, wo, bi, gamma):
    members, lanes, chans = own.shape
    toks, hid = members * lanes, wi.shape[0]
    return call(
        mlp_body,
        [
            jax.ShapeDtypeStruct((2 * members, lanes // 2, chans), BF),
            jax.ShapeDtypeStruct((toks, chans), BF),
            jax.ShapeDtypeStruct((toks, chans), BF),
            jax.ShapeDtypeStruct((toks, 2 * hid), BF),
            jax.ShapeDtypeStruct((1, chans), F32),
        ],
        [smem()] + [vmem()] * 6,
    )(core, own, other, wi, wo, bi, gamma[None])


def grads_body(part, ny, place_ref, n_ref, dy_ref, acts_ref, gamma_ref, out_ref, db_ref):
    toks = n_ref.shape[0]
    hid = acts_ref.shape[1] // 2
    first, second = picks(hid // part, part)
    dpre = acts_ref[:, hid:]
    dw_in = dot(dpre, n_ref[...], 0, 0).astype(BF)
    proj = dot(acts_ref[:, :hid], dy_ref[...], 0, 0)
    dw_out = (proj * gamma_ref[...]).astype(BF)
    out_ref[...] = (dot(first, dw_in, 1, 0) + dot(second, dw_out, 1, 0)).astype(BF)
    nz = hid // part // ny
    lane = lax.broadcasted_iota(jnp.int32, (db_ref.shape[1], hid), 0)
    place = lax.broadcasted_iota(jnp.int32, (1, hid), 1)
    block = jnp.floor((place.astype(F32) + 0.5) * (1.0 / part)).astype(jnp.int32)
    ring = jnp.floor((block.astype(F32) + 0.5) * (1.0 / nz)).astype(jnp.int32)
    ahead = ring + place_ref[0]
    along_z = block - ring * nz
    far = along_z >= nz // 2
    zq = jnp.where(far, along_z - nz // 2, along_z)
    zp = jnp.where(far, 1 - place_ref[1], place_ref[1])
    owner = (zq * 2 + zp) * ny + jnp.where(ahead >= ny, ahead - ny, ahead)
    spot = jnp.where(lane == owner * 2 * part + place - block * part, 1.0, 0.0).astype(BF)
    db = dot(jnp.ones((16, toks), BF), dpre, 1, 0).astype(BF)
    db_ref[...] = dot(db, spot, 1, 1)[:1]


def grads(part, ny, place, n, dy, acts, gamma):
    chans = n.shape[1]
    hid = acts.shape[1] // 2
    return call(
        functools.partial(grads_body, part, ny),
        [
            jax.ShapeDtypeStruct((2 * hid, chans), BF),
            jax.ShapeDtypeStruct((1, 2 * hid), F32),
        ],
        [smem()] + [vmem()] * 4,
    )(place, n, dy, acts, gamma[None])


def slices_body(w_in_ref, w_out_ref, b_ref, out_ref):
    part, chans = w_in_ref.shape
    row = lax.broadcasted_iota(jnp.int32, (2 * part, part), 0)
    place = lax.broadcasted_iota(jnp.int32, (2 * part, part), 1)
    first = jnp.where(row == place, 1.0, 0.0).astype(BF)
    second = jnp.where(row == place + part, 1.0, 0.0).astype(BF)
    rows = (dot(first, w_in_ref[...], 1, 0) + dot(second, w_out_ref[...], 1, 0)).astype(BF)
    bias = jnp.broadcast_to(b_ref[...], (SIDE, part))
    high = bias.astype(BF).astype(F32)
    line = lax.broadcasted_iota(jnp.int32, (SIDE, part), 0)
    both = jnp.where(line == 0, high, jnp.where(line == 1, bias - high, 0.0)).astype(BF)
    side = dot(first, both, 1, 1).astype(BF)
    for k in range(out_ref.shape[0]):
        out_ref[k, :, :chans] = rows
        out_ref[k, :, chans:] = side


def slices(copies, w_in, w_out, b_in):
    part, chans = w_in.shape
    return call(
        slices_body,
        jax.ShapeDtypeStruct((copies, 2 * part, chans + SIDE), BF),
        [vmem()] * 3,
    )(w_in, w_out, b_in[None])


def results_body(part, n_taps, gathered_ref, gamma_ref, b_out_ref, dw_in_ref, dw_out_ref, taps_ref, db_ref, *rest):
    chans = dw_in_ref.shape[1]
    lane = lax.broadcasted_iota(jnp.int32, (1, 128), 1)
    total, db = None, None
    for k in range(gathered_ref.shape[0]):
        block = gathered_ref[k].astype(F32)
        dw_in_ref[k * part : (k + 1) * part] = block[:part, :chans]
        dw_out_ref[k * part : (k + 1) * part] = block[part:, :chans]
        side = block[:, chans:]
        side = side + pltpu.roll(side, 64, 1)
        line = side.T
        line = line[62:63] + line[63:64]
        line = jnp.concatenate([line, jnp.zeros((1, 128 - line.shape[1]), F32)], 1)
        line = jnp.where(lane < part, line, 0.0)
        line = line if k == 0 else pltpu.roll(line, k * part, 1)
        db = line if db is None else db + line
        total = side if total is None else total + side
    db_ref[...] = db[0, : db_ref.shape[0]]
    taps_ref[...] = total[:, :n_taps]
    lines = total.T
    dysum = lines[n_taps + 1]
    rest[0][...] = lines[n_taps]
    rest[1][...] = lines[56] + lines[57]
    rest[2][...] = lines[58] + lines[59]
    rest[3][...] = gamma_ref[...] * dysum
    rest[4][...] = lines[60] + lines[61] + b_out_ref[...] * dysum


def results(part, n_taps, gathered, chans, gamma, b_out):
    members, rows, _ = gathered.shape
    return call(
        functools.partial(results_body, part, n_taps),
        [
            jax.ShapeDtypeStruct((members * part, chans), F32),
            jax.ShapeDtypeStruct((members * part, chans), F32),
            jax.ShapeDtypeStruct((rows, n_taps), F32),
            jax.ShapeDtypeStruct((members * part,), F32),
        ]
        + [jax.ShapeDtypeStruct((rows,), F32)] * 5,
        [vmem()] * 3,
    )(gathered, gamma, b_out)


def to_neighbour(blocks):
    half = blocks.shape[0] // 2
    return blocks[:half] + lax.ppermute(blocks[half:].astype(BF), "zp", [(0, 1), (1, 0)]).astype(F32)


def two_parts(value):
    high = lax.reduce_precision(value, 8, 7)
    return high.astype(BF), (value - high).astype(BF)


def to_all(block, axis):
    count = lax.axis_size(axis)
    return lax.all_to_all(jnp.broadcast_to(block[None], (count,) + block.shape), axis, 0, 0, tiled=True)


def exchange(blocks):
    return lax.all_to_all(blocks, CHAN, 0, 0, tiled=True)


def swap_even(first, last):
    even = lax.axis_index(LAT) % 2 == 0
    pairs = [(i, i + 1) for i in range(0, lax.axis_size(LAT), 2)]
    return lax.ppermute(jnp.where(even, last, first), LAT, pairs + [(j, i) for i, j in pairs])


def swap_odd(first, last):
    even = lax.axis_index(LAT) % 2 == 0
    pairs = [(i, i + 1) for i in range(1, lax.axis_size(LAT) - 1, 2)]
    return lax.ppermute(jnp.where(even, first, last), LAT, pairs + [(j, i) for i, j in pairs])


def up_down(within, across):
    even = lax.axis_index(LAT) % 2 == 0
    return jnp.where(even, across, within), jnp.where(even, within, across)


def along_ring(block, ahead):
    count = lax.axis_size("y")
    return lax.ppermute(block, "y", [((i + ahead) % count, i) for i in range(count)])


def to_ring(blocks):
    count = lax.axis_size("y")
    total = blocks[0].astype(F32)
    for k in range(1, count):
        total = total + lax.ppermute(blocks[k], "y", [(i, (i + k) % count) for i in range(count)]).astype(F32)
    return total


def per_device(
    block_input,
    out_grad,
    metric,
    kernel,
    conv_bias,
    ln_gain,
    ln_bias,
    w_in,
    b_in,
    w_out,
    b_out,
    layer_scale,
):
    cdev, rows, width = block_input.shape
    chans = ln_gain.shape[0]
    tokens = rows * width
    nz, ny = lax.axis_size(ZLO), lax.axis_size("y")
    nchan = nz * ny
    hdev = w_in.shape[0]
    part = hdev // GROUP
    piece = tokens // nchan
    owner = lax.axis_index(CHAN)
    gamma_f = layer_scale.astype(F32)
    gamma_own = lax.dynamic_slice_in_dim(gamma_f, owner * cdev, cdev)

    start = lax.axis_index(("x", "c")) * part
    cut = [lax.dynamic_slice_in_dim(w, start, part) for w in (w_in, w_out, b_in)]
    shards = lax.all_to_all(slices(nz // 2, *cut), "zq", 0, 0, tiled=True)
    beside = lax.ppermute(shards, "zp", [(0, 1), (1, 0)])

    across = swap_odd(block_input[:, :3], block_input[:, rows - 3 :])
    up, down = up_down(swap_even(block_input[:, :3], block_input[:, rows - 3 :]), across)
    taps_bias = jnp.concatenate([kernel, conv_bias[:, None]], 1)
    blocks = forward(taps_bias, block_input, up, down, metric, out_grad)
    blocks, shards, beside = lax.optimization_barrier((blocks, shards, beside))

    recv = exchange(blocks)
    shards = jnp.concatenate([shards, beside], 0)
    one, last = along_ring(shards, 1), along_ring(shards, -1)
    recv, one, last = lax.optimization_barrier((recv, one, last))

    pair, nhat, rstd = norm(recv.reshape(chans, 2 * piece), ln_gain, ln_bias, GROUP // 2)
    pair = lax.all_to_all(pair, "x", 0, 0, tiled=True)
    low, high = along_ring(one[: nz // 2], 1), along_ring(last[nz // 2 :], -1)
    pair, low, high = lax.optimization_barrier((pair, low, high))
    wi, wo, bi = weights([shards, one, low, high, last], part, chans)
    other = lax.ppermute(pair, "c", [(0, 1), (1, 0)])

    core = lax.axis_index("c").astype(jnp.int32)[None]
    dn, n, dy, acts, gam_part = mlp(core, pair, other, wi, wo, bi, gamma_f)
    dn = lax.all_to_all(dn, ("c", "x"), 0, 0, tiled=True)

    place = jnp.stack([lax.axis_index("y"), lax.axis_index("zp")]).astype(jnp.int32)
    dws, db_part = grads(part, ny, place, n, dy, acts, gamma_f)
    dws = to_ring(dws.reshape(ny, nz, 2 * part, chans))
    dws = to_neighbour(dws).astype(BF)

    payload = exchange(norm_back(dn, nhat, rstd, ln_gain, gam_part, db_part, nchan))
    payload, dws = lax.optimization_barrier((payload, dws))
    dws = lax.all_to_all(dws, "zq", 0, 0, tiled=True)
    dws = jnp.sum(dws.astype(F32), 0)
    dconv, ends, dh_sums, extra = stencil_cotangent(payload, metric, cdev, width)
    taps = tap_sums(dconv, dh_sums, block_input, up, down, out_grad)
    across = swap_odd(ends[0], ends[1])

    small = jnp.concatenate([jnp.sum(taps, 2), extra[:, :8]], 1)
    mine = jnp.concatenate([dws.astype(BF)] + list(two_parts(small)), 1)
    mine, ends = lax.optimization_barrier((mine, ends))
    other = lax.ppermute(mine, "zh", [(0, 1), (1, 0)])
    within = swap_even(ends[0], ends[1])
    other, within, across = lax.optimization_barrier((other, within, across))
    other = other.astype(F32)
    count = small.shape[1]
    dws = dws + other[:, :chans]
    small = small + other[:, chans : chans + count] + other[:, chans + count :]
    mine = jnp.concatenate([dws.astype(BF)] + list(two_parts(small)), 1)
    dup, ddown = up_down(within, across)
    grad_input = spread_back(taps_bias, dconv, dup, ddown, out_grad)
    grad_w_in, grad_w_out, grad_kernel, db, *rest = results(
        part, kernel.shape[1], to_all(mine, ("x", "c")), chans, gamma_own, b_out
    )
    return (
        grad_input,
        grad_kernel,
        rest[0],
        rest[1],
        rest[2],
        grad_w_in,
        db,
        grad_w_out,
        rest[3],
        rest[4],
    )


def solution(mesh):
    split = Mesh(mesh.devices.reshape(2, 4, 2, 4, 2, 4), ("zh", "x", "c", "zq", "zp", "y"))
    return jax.shard_map(
        per_device,
        mesh=split,
        in_specs=(
            P(CHAN, LAT, None),
            P(CHAN, LAT, None),
            P(LAT),
            P(CHAN, None),
            P(CHAN),
            P(),
            P(),
            P(CHAN, None),
            P(CHAN),
            P(CHAN, None),
            P(CHAN),
            P(),
        ),
        out_specs=(
            P(CHAN, LAT, None),
            P(CHAN, None),
            P(CHAN),
            P(CHAN),
            P(CHAN),
            P(CHAN, None),
            P(CHAN),
            P(CHAN, None),
            P(CHAN),
            P(CHAN),
        ),
        check_vma=False,
    )
```
